128 devices in a mesh: along: 64 (over z, x_lo, y, core), cross: 2 (over x_hi).
Axes of the slice: x: 4 (x_hi: 2, x_lo: 2; x = x_hi * 2 + x_lo), y: 4, z: 4, core: 2. Of those that a mesh axis runs over, the one named last changes fastest.
Arguments:
- velocity: float32 [4, 2048, 3072], P(None, 'along', 'cross'), may hold values from -6 to 6
- surface: float32 [2048, 3072], P('along', 'cross'), may hold values from -0.25 to 0.25
- wet_mask: int32 [2048, 3072], P('along', 'cross'), may hold values from 0 to 1
- bathy_class: int32 [2048, 3072], P('along', 'cross'), may hold values from 0 to 15
- depth_table: float32 [16], replicated, may hold values from 0.5 to 4
- hull_ranges: int32 [8, 4], replicated, may hold values from 0 to 3072, as said below
- hull_pressure: float32 [8], replicated, may hold values from 0.2 to 1
Outputs:
- new_velocity: float32 [4, 2048, 3072], P(None, 'along', 'cross')
- new_surface: float32 [2048, 3072], P('along', 'cross')
- pressure: float32 [2, 2048, 3072], P(None, 'along', 'cross')
The draws below stay inside these ranges and needn't reach their ends.
Inputs may be any that keep to these rules, and one draw needn't show every extreme that they name: `hull_ranges`: every ship covers 100 // 2 to 100 cells along the channel and 10 to 20 cells across it, inside the grid. Ship 0 lies at the channel's far end, ship 1 at its far bank, ship 2 at its near bank.
All inputs are finite; a program needn't handle non-finite values.
Results may differ from the reference program's by a relative error of at most 0.0003.
Values sent between devices are 32-bit elements; how exact they have to be, the bound alone decides.
No kernel may reach another device: no remote copies, remote signals or barrier semaphores. Data moves between devices by JAX's collectives and lax.ppermute only.
A program may use at most 64 MiB of HBM per device.

```python
import math
import jax
import jax.numpy as jnp
from jax import lax

LAYERS = 2
ITERS = 3
STEPS = 2
CLASSES = 16
SHIPS = 8
NX = 2048
NY = 3072
HULL_X = 100
HULL_Y = 20


def draw_velocity(key, part):
    key = jax.random.fold_in(key, 17)
    position = jnp.arange(NX, dtype=jnp.float32) / NX
    amplitude = 0.5 * (1.0 + 2.0 * position)
    values = jnp.clip(jax.random.normal(key, (4, NX, NY), jnp.float32), -4.0, 4.0)
    return values * amplitude[None, :, None]


def draw_surface(key, part):
    key = jax.random.fold_in(key, 23)
    subkeys = jax.random.split(key, 1)
    return jax.random.uniform(subkeys[0], (NX, NY), jnp.float32, -0.2, 0.2)


def draw_wet_mask(key, part):
    key = jax.random.fold_in(key, 31)
    along_index = jnp.arange(NX, dtype=jnp.int32)
    cross_index = jnp.arange(NY, dtype=jnp.int32)
    flats = 16 + 40 * along_index // NX
    threshold = jnp.where(cross_index[None, :] * 2 >= NY, flats[:, None], 56)
    ticket = jax.random.randint(key, (NX, NY), 0, 64)
    return (ticket < threshold).astype(jnp.int32)


def draw_hull_ranges(key, part):
    key = jax.random.fold_in(key, 29)
    subkeys = jax.random.split(key, 4)
    length_a = jax.random.randint(subkeys[0], (SHIPS,), HULL_X // 2, HULL_X + 1)
    start_a = jax.random.randint(subkeys[1], (SHIPS,), 0, NX - HULL_X + 1)
    length_c = jax.random.randint(subkeys[2], (SHIPS,), HULL_Y // 2, HULL_Y + 1)
    start_c = jax.random.randint(subkeys[3], (SHIPS,), 0, NY - HULL_Y + 1)
    ship_number = jnp.arange(SHIPS, dtype=jnp.int32)
    start_a = jnp.where(ship_number == 0, NX - length_a, start_a)
    start_c = jnp.where(ship_number == 1, NY - length_c, start_c)
    start_c = jnp.where(ship_number == 2, 0, start_c)
    return jnp.stack([start_a, start_a + length_a, start_c, start_c + length_c], axis=1).astype(jnp.int32)


def touch_ends(drawn, stream_key, least, high):
    place = [jax.random.randint(jax.random.fold_in(stream_key, axis), (), 0, length) for axis, length in enumerate(drawn.shape)]
    longest = drawn.shape.index(max(drawn.shape))
    neighbour = place[:longest] + [(place[longest] + 1) % drawn.shape[longest]] + place[longest + 1:]
    return drawn.at[tuple(place)].set(least).at[tuple(neighbour)].set(high)


def setup_inputs(seed: int = 0) -> dict:
    arg_keys = jax.random.split(jax.random.key(seed), 8)
    velocity = draw_velocity(jax.random.fold_in(arg_keys[7], 71), 0)
    surface = draw_surface(jax.random.fold_in(arg_keys[7], 71), 0)
    wet_mask = draw_wet_mask(jax.random.fold_in(arg_keys[7], 71), 0)
    bathy_class = touch_ends(jax.random.randint(arg_keys[3], (NX, NY), 0, CLASSES), jax.random.fold_in(arg_keys[3], 1), 0, CLASSES - 1).astype(jnp.int32)
    depth_table = jnp.clip(jnp.exp(jax.random.uniform(arg_keys[4], (CLASSES,), jnp.float32, math.log(0.5), math.log(4.0))), 0.5, 4.0)
    hull_ranges = draw_hull_ranges(jax.random.fold_in(arg_keys[7], 71), 0)
    hull_pressure = jnp.clip(jnp.exp(jax.random.uniform(arg_keys[6], (SHIPS,), jnp.float32, math.log(0.2), math.log(1.0))), 0.2, 1.0)
    return {"velocity": velocity, "surface": surface, "wet_mask": wet_mask, "bathy_class": bathy_class, "depth_table": depth_table, "hull_ranges": hull_ranges, "hull_pressure": hull_pressure}


gravity = 9.81
time_step = 0.1
viscosity = 0.5
layer_drag = 0.5
bottom_drag = 0.5
storage = 0.1
vertical = 0.5
corner_weight = 0.25
link_table = ((1, 0, 1.0), (-1, 0, 1.0), (0, 1, 1.0), (0, -1, 1.0), (1, 1, corner_weight), (-1, -1, corner_weight), (1, -1, corner_weight), (-1, 1, corner_weight))


def shifted(values, step_along, step_cross, margin):
    row_count = values.shape[-2] - 2 * margin
    col_count = values.shape[-1] - 2 * margin
    return values[..., margin + step_along:margin + step_along + row_count, margin + step_cross:margin + step_cross + col_count]


def depth_of(bathy_class, depth_table):
    result = jnp.zeros(bathy_class.shape, jnp.float32)
    for number in range(CLASSES):
        result = jnp.where(bathy_class == number, depth_table[number], result)
    return result


def hull_heads(hull_ranges, hull_pressure, along_first, along_count, cross_first, cross_count):
    along_index = along_first + jnp.arange(along_count, dtype=jnp.int32)
    cross_index = cross_first + jnp.arange(cross_count, dtype=jnp.int32)
    inside_along = jnp.logical_and(along_index[None, :] >= hull_ranges[:, 0:1], along_index[None, :] < hull_ranges[:, 1:2]).astype(jnp.float32)
    inside_cross = jnp.logical_and(cross_index[None, :] >= hull_ranges[:, 2:3], cross_index[None, :] < hull_ranges[:, 3:4]).astype(jnp.float32)
    return jnp.einsum("si,sj->ij", inside_along * hull_pressure[:, None], inside_cross, precision=lax.Precision.HIGHEST)


def predict(fields_ext, heads_ext, layer_thick, wet_cells):
    potential = gravity * (fields_ext[4] + heads_ext)
    grad_along = 0.5 * (shifted(potential, 1, 0, 2) - shifted(potential, -1, 0, 2))
    grad_cross = 0.5 * (shifted(potential, 0, 1, 2) - shifted(potential, 0, -1, 2))
    along_vel = fields_ext[0:2]
    cross_vel = fields_ext[2:4]
    centre_u = shifted(along_vel, 0, 0, 2)
    centre_v = shifted(cross_vel, 0, 0, 2)
    layer_mask = jnp.array([0.0, 1.0], jnp.float32)[:, None, None]

    def tendency(values, gradient):
        center = shifted(values, 0, 0, 2)
        back_a = 0.5 * (3.0 * center - 4.0 * shifted(values, -1, 0, 2) + shifted(values, -2, 0, 2))
        fore_a = 0.5 * (-3.0 * center + 4.0 * shifted(values, 1, 0, 2) - shifted(values, 2, 0, 2))
        back_c = 0.5 * (3.0 * center - 4.0 * shifted(values, 0, -1, 2) + shifted(values, 0, -2, 2))
        fore_c = 0.5 * (-3.0 * center + 4.0 * shifted(values, 0, 1, 2) - shifted(values, 0, 2, 2))
        advect = jnp.maximum(centre_u, 0.0) * back_a + jnp.minimum(centre_u, 0.0) * fore_a + jnp.maximum(centre_v, 0.0) * back_c + jnp.minimum(centre_v, 0.0) * fore_c
        spread = shifted(values, 1, 0, 2) + shifted(values, -1, 0, 2) + shifted(values, 0, 1, 2) + shifted(values, 0, -1, 2) - 4.0 * center
        coupling = (center[::-1] - center) / layer_thick
        change = -gradient - advect + viscosity * spread + layer_drag * coupling - bottom_drag * layer_mask * center / layer_thick
        return wet_cells * (center + time_step * change)

    return jnp.concatenate([tendency(along_vel, grad_along), tendency(cross_vel, grad_cross)], axis=0)


def divergence(ustar_ext, conduct_ext):
    flux_a = conduct_ext * ustar_ext[0:2]
    flux_c = conduct_ext * ustar_ext[2:4]
    return -((shifted(flux_a, 1, 0, 1) - shifted(flux_a, -1, 0, 1)) + (shifted(flux_c, 0, 1, 1) - shifted(flux_c, 0, -1, 1))) / (2.0 * time_step)


def apply_operator(search_ext, conduct_ext, layer_thick):
    middle = shifted(search_ext, 0, 0, 1)
    conduct_mid = shifted(conduct_ext, 0, 0, 1)
    result = storage * layer_thick * middle + vertical / layer_thick * (middle - middle[::-1])
    for step_along, step_cross, weight in link_table:
        link_coef = weight * 0.5 * (conduct_mid + shifted(conduct_ext, step_along, step_cross, 1))
        result = result + link_coef * (middle - shifted(search_ext, step_along, step_cross, 1))
    return result


def diagonal_of(conduct_ext, layer_thick):
    conduct_mid = shifted(conduct_ext, 0, 0, 1)
    result = storage * layer_thick + vertical / layer_thick
    for step_along, step_cross, weight in link_table:
        result = result + weight * 0.5 * (conduct_mid + shifted(conduct_ext, step_along, step_cross, 1))
    return result


def solve(source, conduct_ext, diagonal, layer_thick):
    solution = jnp.zeros_like(source)
    residual = source
    precond = residual / diagonal
    search = precond
    norm_now = jnp.sum(residual * precond)
    for iteration in range(ITERS):
        applied = apply_operator(jnp.pad(search, ((0, 0), (1, 1), (1, 1))), conduct_ext, layer_thick)
        step_size = norm_now / jnp.sum(search * applied)
        solution = solution + step_size * search
        residual = residual - step_size * applied
        if iteration + 1 < ITERS:
            precond = residual / diagonal
            norm_next = jnp.sum(residual * precond)
            search = precond + (norm_next / norm_now) * search
            norm_now = norm_next
    return solution


def correct(surface_now, ustar_ext, pressure_ext, conduct_ext, wet_cells):
    slope_a = 0.5 * (shifted(pressure_ext, 1, 0, 1) - shifted(pressure_ext, -1, 0, 1))
    slope_c = 0.5 * (shifted(pressure_ext, 0, 1, 1) - shifted(pressure_ext, 0, -1, 1))
    moved_a = ustar_ext[0:2] - time_step * slope_a
    moved_c = ustar_ext[2:4] - time_step * slope_c
    flux_a = jnp.sum(conduct_ext * moved_a, axis=0)
    flux_c = jnp.sum(conduct_ext * moved_c, axis=0)
    new_surface = surface_now - time_step * 0.5 * ((shifted(flux_a, 1, 0, 1) - shifted(flux_a, -1, 0, 1)) + (shifted(flux_c, 0, 1, 1) - shifted(flux_c, 0, -1, 1)))
    new_vel = wet_cells * jnp.concatenate([shifted(moved_a, 0, 0, 1), shifted(moved_c, 0, 0, 1)], axis=0)
    return jnp.concatenate([new_vel, new_surface[None]], axis=0)


def reference(velocity, surface, wet_mask, bathy_class, depth_table, hull_ranges, hull_pressure):
    wet_cells = wet_mask.astype(jnp.float32)
    layer_thick = 0.5 * depth_of(bathy_class, depth_table)
    conduct_ext = jnp.pad(wet_cells * layer_thick, 1)
    diagonal = diagonal_of(conduct_ext, layer_thick)
    heads_ext = hull_heads(hull_ranges, hull_pressure, -2, NX + 4, -2, NY + 4)
    start_fields = jnp.concatenate([velocity * wet_cells, surface[None]], axis=0)

    def advance(step_number, carried):
        fields, pressure = carried
        ustar = predict(jnp.pad(fields, ((0, 0), (2, 2), (2, 2))), heads_ext, layer_thick, wet_cells)
        ustar_ext = jnp.pad(ustar, ((0, 0), (1, 1), (1, 1)))
        source = divergence(ustar_ext, conduct_ext)
        pressure = solve(source, conduct_ext, diagonal, layer_thick)
        fields = correct(fields[4], ustar_ext, jnp.pad(pressure, ((0, 0), (2, 2), (2, 2))), conduct_ext, wet_cells)
        return fields, pressure

    fields, pressure = lax.fori_loop(0, STEPS, advance, (start_fields, jnp.zeros((LAYERS, NX, NY), jnp.float32)))
    return fields[0:4], fields[4], pressure
```

```python
import jax
import jax.numpy as jnp
from jax import lax
from jax.sharding import PartitionSpec as P

LAYERS = 2
ITERS = 3
STEPS = 2
CLASSES = 16


gravity = 9.81
time_step = 0.1
viscosity = 0.5
layer_drag = 0.5
bottom_drag = 0.5
storage = 0.1
vertical = 0.5
corner_weight = 0.25
link_table = (
    (1, 0, 1.0),
    (-1, 0, 1.0),
    (0, 1, 1.0),
    (0, -1, 1.0),
    (1, 1, corner_weight),
    (-1, -1, corner_weight),
    (1, -1, corner_weight),
    (-1, 1, corner_weight),
)


def padded(x, sides, width):
    for axis, dim in sides:
        size, length = (lax.axis_size(axis), x.shape[dim])
        up = [(i, (i + 1) % size) for i in range(size - 1)]
        down = [(j, i) for i, j in up]
        last = lax.slice_in_dim(x, length - width, length, axis=dim)
        leading = lax.slice_in_dim(x, 0, width, axis=dim)
        before = lax.ppermute(last, axis, up)
        after = lax.ppermute(leading, axis, down)
        x = jnp.concatenate([before, x, after], axis=dim)
    return x


def shifted(values, step_along, step_cross, margin):
    row_count = values.shape[-2] - 2 * margin
    col_count = values.shape[-1] - 2 * margin
    return values[
        ...,
        margin + step_along : margin + step_along + row_count,
        margin + step_cross : margin + step_cross + col_count,
    ]


def depth_of(bathy_class, depth_table):
    result = jnp.zeros(bathy_class.shape, jnp.float32)
    for number in range(CLASSES):
        result = jnp.where(bathy_class == number, depth_table[number], result)
    return result


def hull_heads(hull_ranges, hull_pressure, along_first, along_count, cross_first, cross_count):
    along_index = along_first + jnp.arange(along_count, dtype=jnp.int32)
    cross_index = cross_first + jnp.arange(cross_count, dtype=jnp.int32)
    inside_along = jnp.logical_and(
        along_index[None, :] >= hull_ranges[:, 0:1], along_index[None, :] < hull_ranges[:, 1:2]
    ).astype(jnp.float32)
    inside_cross = jnp.logical_and(
        cross_index[None, :] >= hull_ranges[:, 2:3], cross_index[None, :] < hull_ranges[:, 3:4]
    ).astype(jnp.float32)
    return jnp.einsum(
        "si,sj->ij",
        inside_along * hull_pressure[:, None],
        inside_cross,
        precision=lax.Precision.HIGHEST,
    )


def predict(fields_ext, heads_ext, layer_thick, wet_cells):
    potential = gravity * (fields_ext[4] + heads_ext)
    grad_along = 0.5 * (shifted(potential, 1, 0, 2) - shifted(potential, -1, 0, 2))
    grad_cross = 0.5 * (shifted(potential, 0, 1, 2) - shifted(potential, 0, -1, 2))
    along_vel = fields_ext[0:2]
    cross_vel = fields_ext[2:4]
    centre_u = shifted(along_vel, 0, 0, 2)
    centre_v = shifted(cross_vel, 0, 0, 2)
    layer_mask = jnp.array([0.0, 1.0], jnp.float32)[:, None, None]

    def tendency(values, gradient):
        center = shifted(values, 0, 0, 2)
        back_a = 0.5 * (3.0 * center - 4.0 * shifted(values, -1, 0, 2) + shifted(values, -2, 0, 2))
        fore_a = 0.5 * (-3.0 * center + 4.0 * shifted(values, 1, 0, 2) - shifted(values, 2, 0, 2))
        back_c = 0.5 * (3.0 * center - 4.0 * shifted(values, 0, -1, 2) + shifted(values, 0, -2, 2))
        fore_c = 0.5 * (-3.0 * center + 4.0 * shifted(values, 0, 1, 2) - shifted(values, 0, 2, 2))
        advect = (
            jnp.maximum(centre_u, 0.0) * back_a
            + jnp.minimum(centre_u, 0.0) * fore_a
            + jnp.maximum(centre_v, 0.0) * back_c
            + jnp.minimum(centre_v, 0.0) * fore_c
        )
        spread = (
            shifted(values, 1, 0, 2)
            + shifted(values, -1, 0, 2)
            + shifted(values, 0, 1, 2)
            + shifted(values, 0, -1, 2)
            - 4.0 * center
        )
        coupling = (center[::-1] - center) / layer_thick
        change = (
            -gradient
            - advect
            + viscosity * spread
            + layer_drag * coupling
            - bottom_drag * layer_mask * center / layer_thick
        )
        return wet_cells * (center + time_step * change)

    return jnp.concatenate(
        [tendency(along_vel, grad_along), tendency(cross_vel, grad_cross)], axis=0
    )


def divergence(ustar_ext, conduct_ext):
    flux_a = conduct_ext * ustar_ext[0:2]
    flux_c = conduct_ext * ustar_ext[2:4]
    return -(
        shifted(flux_a, 1, 0, 1)
        - shifted(flux_a, -1, 0, 1)
        + (shifted(flux_c, 0, 1, 1) - shifted(flux_c, 0, -1, 1))
    ) / (2.0 * time_step)


def diagonal_of(conduct_ext, layer_thick):
    conduct_mid = shifted(conduct_ext, 0, 0, 1)
    result = storage * layer_thick + vertical / layer_thick
    for step_along, step_cross, weight in link_table:
        result = result + weight * 0.5 * (
            conduct_mid + shifted(conduct_ext, step_along, step_cross, 1)
        )
    return result


def extend(search):
    result = padded(search, (("along", 1), ("cross", 2)), 1)
    return result


def apply_links(values_ext, conduct_ext, layer_thick):
    middle = shifted(values_ext, 0, 0, 1)
    conduct_mid = shifted(conduct_ext, 0, 0, 1)
    result = vertical / layer_thick * middle[::-1]
    for step_along, step_cross, weight in link_table:
        link_coef = weight * 0.5 * (conduct_mid + shifted(conduct_ext, step_along, step_cross, 1))
        result = result + link_coef * shifted(values_ext, step_along, step_cross, 1)
    return result


def summed(partial):
    count = lax.axis_size("along") * lax.axis_size("cross")
    spread = jnp.broadcast_to(partial[None, :], (count, partial.shape[0]))
    return jnp.sum(lax.all_to_all(spread, ("along", "cross"), 0, 0, tiled=True), axis=0)


def coefficients(mu):
    def norm(c):
        return sum(c[i] * c[j] * mu[i + j] for i in range(len(c)) for j in range(len(c)))

    def energy(c):
        return sum(
            c[i] * c[j] * (mu[i + j] - mu[i + j + 1]) for i in range(len(c)) for j in range(len(c))
        )

    floor = 2e-7 * mu[0]
    z = [jnp.float32(1.0)]
    search = [jnp.float32(1.0)]
    total = [jnp.float32(0.0)] * ITERS
    norm_now = mu[0]
    for iteration in range(ITERS):
        step = norm_now / energy(search)
        if iteration:
            step = jnp.where(norm_now > floor, step, 0.0)
        for i, c in enumerate(search):
            total[i] = total[i] + step * c
        if iteration + 1 < ITERS:
            applied = [
                (search[i] if i < len(search) else 0.0) - (search[i - 1] if i else 0.0)
                for i in range(len(search) + 1)
            ]
            z = [(z[i] if i < len(z) else 0.0) - step * applied[i] for i in range(len(applied))]
            norm_next = norm(z)
            ratio = norm_next / norm_now
            if iteration:
                ratio = jnp.where(norm_now > floor, ratio, 0.0)
            search = [z[i] + (ratio * search[i] if i < len(search) else 0.0) for i in range(len(z))]
            norm_now = norm_next
    return total


def solve(source, conduct_ext, diagonal, layer_thick):
    inverse = 1.0 / diagonal
    y0 = source * inverse
    n0 = apply_links(extend(y0), conduct_ext, layer_thick)
    y1 = n0 * inverse
    n1 = apply_links(extend(y1), conduct_ext, layer_thick)
    y2 = n1 * inverse
    n2 = apply_links(extend(y2), conduct_ext, layer_thick)
    partial = jnp.stack(
        [
            jnp.sum(source * y0),
            jnp.sum(y0 * n0),
            jnp.sum(y1 * n0),
            jnp.sum(y1 * n1),
            jnp.sum(y2 * n1),
            jnp.sum(y2 * n2),
        ]
    )
    mu = summed(jnp.pad(partial, (0, 2)))
    c = coefficients([mu[i] for i in range(2 * ITERS)])
    return c[0] * y0 + c[1] * y1 + c[2] * y2


def correct(surface_now, ustar_ext, pressure_ext, conduct_ext, wet_cells):
    slope_a = 0.5 * (shifted(pressure_ext, 1, 0, 1) - shifted(pressure_ext, -1, 0, 1))
    slope_c = 0.5 * (shifted(pressure_ext, 0, 1, 1) - shifted(pressure_ext, 0, -1, 1))
    moved_a = ustar_ext[0:2] - time_step * slope_a
    moved_c = ustar_ext[2:4] - time_step * slope_c
    flux_a = jnp.sum(conduct_ext * moved_a, axis=0)
    flux_c = jnp.sum(conduct_ext * moved_c, axis=0)
    new_surface = surface_now - time_step * 0.5 * (
        shifted(flux_a, 1, 0, 1)
        - shifted(flux_a, -1, 0, 1)
        + (shifted(flux_c, 0, 1, 1) - shifted(flux_c, 0, -1, 1))
    )
    new_vel = wet_cells * jnp.concatenate(
        [shifted(moved_a, 0, 0, 1), shifted(moved_c, 0, 0, 1)], axis=0
    )
    return jnp.concatenate([new_vel, new_surface[None]], axis=0)


def shards(velocity, surface, wet_mask, bathy_class, depth_table, hull_ranges, hull_pressure):
    span_a = surface.shape[0]
    span_c = surface.shape[1]
    wet_cells = wet_mask.astype(jnp.float32)
    layer_thick = 0.5 * depth_of(bathy_class, depth_table)
    wet_ext, thick_ext = (
        padded(wet_cells, (("along", 0), ("cross", 1)), 1),
        padded(layer_thick, (("along", 0), ("cross", 1)), 1),
    )
    conduct_ext = wet_ext * thick_ext
    diagonal = diagonal_of(conduct_ext, layer_thick)
    along_first = lax.axis_index("along") * span_a
    cross_first = lax.axis_index("cross") * span_c
    heads_ext = hull_heads(
        hull_ranges, hull_pressure, along_first - 2, span_a + 4, cross_first - 2, span_c + 4
    )
    fields = jnp.concatenate([velocity * wet_cells, surface[None]], axis=0)
    pressure = jnp.zeros((LAYERS, span_a, span_c), jnp.float32)
    for step_number in range(STEPS):
        fields_ext = padded(fields, (("along", 1), ("cross", 2)), 2)
        predicted = predict(fields_ext, heads_ext, layer_thick, wet_cells)
        ustar_ext = padded(predicted, (("along", 1), ("cross", 2)), 1)
        source = divergence(ustar_ext, conduct_ext)
        pressure = solve(source, conduct_ext, diagonal, layer_thick)
        pressure_ext = padded(pressure, (("along", 1), ("cross", 2)), 2)
        fields = correct(fields[4], ustar_ext, pressure_ext, conduct_ext, wet_cells)
    return (fields[0:4], fields[4], pressure)


def solution(mesh):
    in_specs = (
        P(None, "along", "cross"),
        P("along", "cross"),
        P("along", "cross"),
        P("along", "cross"),
        P(),
        P(),
        P(),
    )
    out_specs = (P(None, "along", "cross"), P("along", "cross"), P(None, "along", "cross"))
    return jax.shard_map(shards, mesh=mesh, in_specs=in_specs, out_specs=out_specs, check_vma=False)
```

```python
import functools

import jax
import jax.numpy as jnp
from jax import lax
from jax.experimental import pallas as pl
from jax.experimental.pallas import tpu as pltpu
from jax.sharding import PartitionSpec as P

ITERS = 3
CLASSES = 16
SHIPS = 8

gravity = 9.81
time_step = 0.1
storage = 0.1
corner_weight = 0.25

LANES = 128
TILE = 8
GUARD = 8
HALO = 16
VMEM_BYTES = 56 * 1024 * 1024


class Shape:
    def __init__(self, rows, cols):
        self.rows = rows
        self.own = cols // LANES
        self.chunks = self.own + 1
        self.first = GUARD + HALO
        self.total = rows + 2 * (GUARD + HALO)


class Ring:
    def __init__(self, make, chunks, lane):
        self.make = make
        self.chunks = chunks
        self.lane = lane
        self.held = {}

    def at(self, chunk):
        entry = self.held.setdefault(chunk, {})
        if 0 not in entry:
            entry[0] = self.make(chunk)
        return entry[0]

    def rolled(self, chunk, amount):
        value = self.at(chunk)
        entry = self.held[chunk]
        if amount not in entry:
            entry[amount] = pltpu.roll(value, amount, 1)
        return entry[amount]

    def before(self, chunk, step):
        other = (chunk - 1) % self.chunks
        return jnp.where(self.lane < step, self.rolled(other, step), self.rolled(chunk, step))

    def after(self, chunk, step):
        other = (chunk + 1) % self.chunks
        amount = LANES - step
        return jnp.where(self.lane >= amount, self.rolled(other, amount), self.rolled(chunk, amount))

    def done(self, chunk):
        self.held.pop((chunk - 1) % self.chunks, None)


def lanes_of():
    return lax.broadcasted_iota(jnp.int32, (TILE, LANES), 1)


def sweep(first, tiles, body):
    def turn(number, carry):
        body(first + number * TILE)
        return carry

    lax.fori_loop(0, tiles, turn, 0)


def load(ref, index, chunk, row):
    return ref[index, chunk, pl.ds(row, TILE), :]


def store(ref, index, chunk, row, value):
    ref[index, chunk, pl.ds(row, TILE), :] = value


CONDUCT, HALF_RATE, INVERSE, HEAD, DIAGONAL = range(5)


def predict_rows(shape, vel, head_pressure, static, moved, row):
    lane = lanes_of()
    rings = [
        Ring(lambda c, k=k: load(vel, k, c, row), shape.chunks, lane) for k in range(4)
    ]
    potential = Ring(lambda c: load(head_pressure, 0, c, row), shape.chunks, lane)
    for c in range(shape.chunks):
        wet = load(static, CONDUCT, c, row) > 0.0
        rate = time_step * load(static, HALF_RATE, c, row)
        slope_a = (0.5 * time_step) * (
            load(head_pressure, 0, c, row + 1) - load(head_pressure, 0, c, row - 1)
        )
        slope_c = (0.5 * time_step) * (potential.after(c, 1) - potential.before(c, 1))
        for layer in range(2):
            along = rings[layer].at(c)
            cross = rings[2 + layer].at(c)
            up_a = (0.5 * time_step) * jnp.maximum(along, 0.0)
            dn_a = (0.5 * time_step) * jnp.minimum(along, 0.0)
            up_c = (0.5 * time_step) * jnp.maximum(cross, 0.0)
            dn_c = (0.5 * time_step) * jnp.minimum(cross, 0.0)
            centre = (
                0.8 - 3.0 * ((up_a - dn_a) + (up_c - dn_c)) - (rate if layer == 0 else 2.0 * rate)
            )
            back_a = 0.05 + 4.0 * up_a
            fore_a = 0.05 - 4.0 * dn_a
            back_c = 0.05 + 4.0 * up_c
            fore_c = 0.05 - 4.0 * dn_c
            for part, slope in ((layer, slope_a), (2 + layer, slope_c)):
                ring = rings[part]
                other = rings[part + 1 - 2 * layer].at(c)
                value = centre * ring.at(c) + rate * other - slope
                value = value + (
                    back_a * load(vel, part, c, row - 1) - up_a * load(vel, part, c, row - 2)
                )
                value = value + (
                    fore_a * load(vel, part, c, row + 1) + dn_a * load(vel, part, c, row + 2)
                )
                value = value + (back_c * ring.before(c, 1) - up_c * ring.before(c, 2))
                value = value + (fore_c * ring.after(c, 1) + dn_c * ring.after(c, 2))
                store(moved, part, c, row, jnp.where(wet, value, 0.0))
        for ring in rings:
            ring.done(c)
        potential.done(c)


def source_rows(shape, moved, static, krylov, row):
    lane = lanes_of()
    rings = [
        Ring(
            lambda c, k=k: load(static, CONDUCT, c, row) * load(moved, 2 + k, c, row),
            shape.chunks,
            lane,
        )
        for k in range(2)
    ]
    for c in range(shape.chunks):
        above = load(static, CONDUCT, c, row - 1)
        below = load(static, CONDUCT, c, row + 1)
        scale = (-0.5 / time_step) * load(static, INVERSE, c, row)
        for layer in range(2):
            flow = (
                below * load(moved, layer, c, row + 1)
                - above * load(moved, layer, c, row - 1)
                + (rings[layer].after(c, 1) - rings[layer].before(c, 1))
            )
            store(krylov, layer, c, row, scale * flow)
            rings[layer].done(c)


def link_rows(shape, krylov, static, level, row, own_only):
    lane = lanes_of()

    def plain(layer, c):
        values = [load(krylov, 2 * level + layer, c, row + d) for d in (-1, 0, 1)]
        return values[1], values[0] + values[2]

    def weighted(layer, c):
        values = [
            load(static, CONDUCT, c, row + d) * load(krylov, 2 * level + layer, c, row + d)
            for d in (-1, 0, 1)
        ]
        return values[1], values[0] + values[2]

    sides = {}

    def ring_of(kind, layer):
        def make(c):
            middle, sums = kind(layer, c)
            sides[kind, layer, c] = sums
            return middle + corner_weight * sums

        return Ring(make, shape.chunks, lane)

    rings = [(ring_of(plain, layer), ring_of(weighted, layer)) for layer in range(2)]
    for c in range(shape.own if own_only else shape.chunks):
        conduct = load(static, CONDUCT, c, row)
        rate = load(static, HALF_RATE, c, row)
        centre = [load(krylov, 2 * level + layer, c, row) for layer in range(2)]
        results = []
        for layer in range(2):
            ring, scaled = rings[layer]
            around = (ring.before(c, 1) + ring.after(c, 1)) + sides[plain, layer, c]
            flows = (scaled.before(c, 1) + scaled.after(c, 1)) + sides[weighted, layer, c]
            results.append(0.5 * (conduct * around + flows) + rate * centre[1 - layer])
            ring.done(c)
            scaled.done(c)
        yield c, centre, results


def krylov_rows(shape, krylov, static, level, row):
    for c, _, results in link_rows(shape, krylov, static, level, row, False):
        inverse = load(static, INVERSE, c, row)
        for layer in range(2):
            store(krylov, 2 * level + 2 + layer, c, row, inverse * results[layer])


def moments_of(shape, krylov, static):
    zeros = (jnp.zeros((TILE, LANES), jnp.float32),) * (2 * ITERS)

    def turn(number, sums):
        row = shape.first + number * TILE
        sums = list(sums)
        for c, top, results in link_rows(shape, krylov, static, 2, row, True):
            diagonal = load(static, DIAGONAL, c, row)
            for layer in range(2):
                low = load(krylov, layer, c, row)
                mid = load(krylov, 2 + layer, c, row)
                low_d, mid_d, top_d = diagonal * low, diagonal * mid, diagonal * top[layer]
                terms = (
                    low * low_d,
                    low * mid_d,
                    mid * mid_d,
                    mid * top_d,
                    top[layer] * top_d,
                    top[layer] * results[layer],
                )
                sums = [a + b for a, b in zip(sums, terms)]
        return tuple(sums)

    return lax.fori_loop(0, shape.rows // TILE, turn, zeros)


def put_moments(out, sums):
    lane = lanes_of()
    result = jnp.zeros((TILE, LANES), jnp.float32)
    for number, part in enumerate(sums):
        result = jnp.where(lane == number, jnp.sum(part), result)
    out[...] = result


def project(shape, vel, potential, static, moved, krylov, moments, first, tiles):
    sweep(first[0], tiles[0], functools.partial(predict_rows, shape, vel, potential, static, moved))
    sweep(first[1], tiles[1], functools.partial(source_rows, shape, moved, static, krylov))
    for level in range(2):
        sweep(
            first[2 + level],
            tiles[2 + level],
            functools.partial(krylov_rows, shape, krylov, static, level),
        )
    put_moments(moments, moments_of(shape, krylov, static))


def pack_kernel(shape, vel, surface, wet, bathy, table, lo, hi, side, clo, chi):
    half = lax.axis_index("cross")
    lane = lanes_of()
    for t in range(shape.rows // TILE):
        rows = pl.ds(t * TILE, TILE)
        target, corner = (lo, clo) if t * TILE < HALO else (hi, chi)
        at = pl.ds(t * TILE % HALO, TILE)
        edges = []
        for c in range(shape.own):
            cols = pl.ds(c * LANES, LANES)
            flag = wet[rows, cols]
            number = bathy[rows, cols]
            thick = jnp.zeros((TILE, LANES), jnp.float32)
            for entry in range(CLASSES):
                thick = jnp.where(number == entry, 0.5 * table[entry], thick)
            values = [jnp.where(flag > 0, vel[k, rows, cols], 0.0) for k in range(4)]
            values += [surface[rows, cols], flag.astype(jnp.float32), thick]
            for k, value in enumerate(values):
                target[k, at, cols] = value
            if c in (0, shape.own - 1):
                edges.append(values)
        for k in range(7):
            value = jnp.where(
                half == 0,
                jnp.where(lane >= LANES // 2, edges[1][k], 0.0),
                jnp.where(lane < LANES // 2, edges[0][k], 0.0),
            )
            side[k, rows, :] = value
            corner[k, at, :] = value


def first_kernel(
    shape, lo, hi, top, bot, side, ctop, cbot, ranges, heads,
    moved, static, surface, krylov, moments,
    vel, potential, thick, columns,
):
    along = lax.axis_index("along")
    half = lax.axis_index("cross")
    lane = lanes_of()
    line = lax.broadcasted_iota(jnp.int32, (TILE, LANES), 0)
    for c in range(shape.chunks):
        if c < shape.own:
            index = half * (shape.own * LANES) + c * LANES + lane
        else:
            index = jnp.where(half == 0, shape.own * LANES, (shape.own - 1) * LANES) + lane
        for s in range(SHIPS):
            inside = jnp.logical_and(index >= ranges[s, 2], index < ranges[s, 3])
            columns[s, c] = jnp.where(inside, gravity * heads[s], 0.0)
    pieces = [(GUARD, top, ctop, 0), (shape.first, lo, side, 0)]
    pieces += [(shape.first + HALO, hi, side, HALO), (shape.first + shape.rows, bot, cbot, 0)]
    for base, wide, narrow, offset in pieces:

        def turn(number, carry, base=base, wide=wide, narrow=narrow, offset=offset):
            at = pl.multiple_of(number * TILE, TILE)
            row = base + number * TILE
            global_row = along * shape.rows + (row - shape.first) + line
            covered = [
                jnp.logical_and(global_row >= ranges[s, 0], global_row < ranges[s, 1])
                for s in range(SHIPS)
            ]
            for c in range(shape.chunks):
                if c < shape.own:
                    values = [
                        wide[k, pl.ds(at, TILE), pl.ds(c * LANES, LANES)] for k in range(7)
                    ]
                else:
                    values = [narrow[k, pl.ds(offset + at, TILE), :] for k in range(7)]
                for k in range(4):
                    store(vel, k, c, row, values[k])
                depth = values[6]
                inside = depth > 0.0
                depth = jnp.where(inside, depth, 1.0)
                head = jnp.zeros((TILE, LANES), jnp.float32)
                for s in range(SHIPS):
                    head = head + jnp.where(covered[s], columns[s, c], 0.0)
                head = jnp.where(inside, head, 0.0)
                store(surface, 0, c, row, values[4])
                store(potential, 0, c, row, gravity * values[4] + head)
                store(thick, 0, c, row, values[6])
                store(static, CONDUCT, c, row, values[5] * values[6])
                store(static, HALF_RATE, c, row, 0.5 / depth)
                store(static, HEAD, c, row, head)
            return carry

        lax.fori_loop(0, HALO // TILE, turn, 0)

    def diagonal_rows(row):
        sides = {}

        def make(c):
            sums = load(static, CONDUCT, c, row - 1) + load(static, CONDUCT, c, row + 1)
            sides[c] = sums
            return load(static, CONDUCT, c, row) + corner_weight * sums

        ring = Ring(make, shape.chunks, lane)
        for c in range(shape.chunks):
            around = ring.before(c, 1) + ring.after(c, 1) + sides[c]
            depth = load(thick, 0, c, row)
            diagonal = (
                0.5 * (around + 5.0 * load(static, CONDUCT, c, row))
                + storage * depth
                + load(static, HALF_RATE, c, row)
            )
            store(static, DIAGONAL, c, row, diagonal)
            store(static, INVERSE, c, row, jnp.where(depth > 0.0, 1.0 / diagonal, 0.0))
            ring.done(c)

    start = GUARD
    sweep(start + 4, 7, diagonal_rows)
    project(
        shape, vel, potential, static, moved, krylov, moments,
        (start + 4, start + 5, start + 6, start + 7), (7, 7, 7, 7),
    )


def coefficients(shares):
    total = jnp.sum(shares[...], axis=0, keepdims=True)
    mu = [jnp.broadcast_to(total[:, k : k + 1], (TILE, LANES)) for k in range(2 * ITERS)]

    def norm(c):
        return sum(c[i] * c[j] * mu[i + j] for i in range(len(c)) for j in range(len(c)))

    def energy(c):
        return sum(
            c[i] * c[j] * (mu[i + j] - mu[i + j + 1]) for i in range(len(c)) for j in range(len(c))
        )

    floor = 2e-7 * mu[0]
    one = jnp.ones((TILE, LANES), jnp.float32)
    z = [one]
    search = [one]
    result = [jnp.zeros((TILE, LANES), jnp.float32)] * ITERS
    norm_now = mu[0]
    for iteration in range(ITERS):
        step = norm_now / energy(search)
        if iteration:
            step = jnp.where(norm_now > floor, step, 0.0)
        for i, c in enumerate(search):
            result[i] = result[i] + step * c
        if iteration + 1 < ITERS:
            applied = [
                (search[i] if i < len(search) else 0.0) - (search[i - 1] if i else 0.0)
                for i in range(len(search) + 1)
            ]
            z = [(z[i] if i < len(z) else 0.0) - step * applied[i] for i in range(len(applied))]
            norm_next = norm(z)
            ratio = norm_next / norm_now
            if iteration:
                ratio = jnp.where(norm_now > floor, ratio, 0.0)
            search = [z[i] + (ratio * search[i] if i < len(search) else 0.0) for i in range(len(z))]
            norm_now = norm_next
    return result


def pressure_rows(shape, factors, krylov, pressure, row):
    for c in range(shape.chunks):
        for layer in range(2):
            value = factors[0] * load(krylov, layer, c, row)
            value = value + factors[1] * load(krylov, 2 + layer, c, row)
            value = value + factors[2] * load(krylov, 4 + layer, c, row)
            store(pressure, layer, c, row, value)


def along_moved(moved, pressure, layer, c, row):
    return load(moved, layer, c, row) - (0.5 * time_step) * (
        load(pressure, layer, c, row + 1) - load(pressure, layer, c, row - 1)
    )


def move_rows(shape, moved, pressure, static, flux, put, row):
    lane = lanes_of()
    rings = [
        Ring(lambda c, k=k: load(pressure, k, c, row), shape.chunks, lane) for k in range(2)
    ]
    for c in range(shape.chunks):
        conduct = load(static, CONDUCT, c, row)
        wet = conduct > 0.0
        along = [along_moved(moved, pressure, layer, c, row) for layer in range(2)]
        cross = [
            load(moved, 2 + layer, c, row)
            - (0.5 * time_step) * (rings[layer].after(c, 1) - rings[layer].before(c, 1))
            for layer in range(2)
        ]
        for part, value in enumerate(along + cross):
            put(part, c, row, jnp.where(wet, value, 0.0))
        store(flux, 0, c, row, conduct * (along[0] + along[1]))
        store(flux, 1, c, row, conduct * (cross[0] + cross[1]))
        for ring in rings:
            ring.done(c)


def surface_rows(shape, surface, flux, chunks, put, row):
    ring = Ring(lambda c: load(flux, 1, c, row), shape.chunks, lanes_of())
    for c in range(chunks):
        value = load(surface, 0, c, row) - (0.5 * time_step) * (
            load(flux, 0, c, row + 1)
            - load(flux, 0, c, row - 1)
            + (ring.after(c, 1) - ring.before(c, 1))
        )
        put(c, row, value)
        ring.done(c)


def second_kernel(
    shape, shares, moved_in, static, surface_in, krylov_in,
    moved, surface, krylov, moments,
    vel, potential, pressure, flux,
):
    factors = coefficients(shares)
    start = GUARD
    sweep(start + 7, 7, functools.partial(pressure_rows, shape, factors, krylov_in, pressure))
    sweep(
        start + 8,
        6,
        functools.partial(
            move_rows, shape, moved_in, pressure, static, flux, functools.partial(store, vel)
        ),
    )

    def put(c, row, value):
        value = jnp.where(load(static, INVERSE, c, row) > 0.0, value, 0.0)
        store(surface, 0, c, row, value)
        store(potential, 0, c, row, gravity * value + load(static, HEAD, c, row))

    sweep(
        start + 9,
        6,
        functools.partial(surface_rows, shape, surface_in, flux, shape.chunks, put),
    )
    project(
        shape, vel, potential, static, moved, krylov, moments,
        (start + 11, start + 12, start + 13, start + 14), (6, 5, 5, 5),
    )


def last_kernel(
    shape, shares, moved, static, surface, krylov,
    new_vel, new_surface, new_pressure,
    pressure, flux,
):
    factors = coefficients(shares)
    start = shape.first
    sweep(start - 2, 5, functools.partial(pressure_rows, shape, factors, krylov, pressure))

    def put_vel(part, c, row, value):
        if c < shape.own:
            at = pl.multiple_of(row - start, TILE)
            new_vel[part, pl.ds(at, TILE), pl.ds(c * LANES, LANES)] = value
            if part < 2:
                new_pressure[part, pl.ds(at, TILE), pl.ds(c * LANES, LANES)] = load(
                    pressure, part, c, row
                )

    sweep(
        start,
        shape.rows // TILE,
        functools.partial(move_rows, shape, moved, pressure, static, flux, put_vel),
    )
    for row in (start - 1, start + shape.rows):
        for c in range(shape.own):
            one = slice(row, row + 1)
            total = jnp.zeros((1, LANES), jnp.float32)
            for layer in range(2):
                total = total + (
                    moved[layer, c, one, :]
                    - (0.5 * time_step)
                    * (
                        pressure[layer, c, row + 1 : row + 2, :]
                        - pressure[layer, c, row - 1 : row, :]
                    )
                )
            flux[0, c, one, :] = static[CONDUCT, c, one, :] * total

    def put(c, row, value):
        at = pl.multiple_of(row - start, TILE)
        new_surface[pl.ds(at, TILE), pl.ds(c * LANES, LANES)] = value

    sweep(
        start,
        shape.rows // TILE,
        functools.partial(surface_rows, shape, surface, flux, shape.own, put),
    )


def call(kernel, shape, kinds, outs, scratch, operands):
    f32 = jnp.float32
    return pl.pallas_call(
        functools.partial(kernel, shape),
        out_shape=[jax.ShapeDtypeStruct(s, f32) for s in outs],
        in_specs=[pl.BlockSpec(memory_space=kind) for kind in kinds],
        out_specs=[pl.BlockSpec(memory_space=pltpu.VMEM)] * len(outs),
        scratch_shapes=[pltpu.VMEM(s, f32) for s in scratch],
        compiler_params=pltpu.CompilerParams(vmem_limit_bytes=VMEM_BYTES),
    )(*operands)


def shared(moments):
    count = lax.axis_size("along") * lax.axis_size("cross")
    spread = jnp.broadcast_to(moments[0:1, 0:8], (count, 8))
    return lax.all_to_all(spread, ("along", "cross"), 0, 0, tiled=True)


def shards(velocity, surface, wet_mask, bathy_class, depth_table, hull_ranges, hull_pressure):
    shape = Shape(*surface.shape)
    vmem, smem = pltpu.VMEM, pltpu.SMEM
    cols = surface.shape[1]
    wide, narrow = (7, HALO, cols), (7, HALO, LANES)
    lo, hi, side, clo, chi = call(
        pack_kernel, shape, [vmem] * 4 + [smem],
        [wide, wide, (7, shape.rows, LANES), narrow, narrow], [],
        (velocity, surface, wet_mask, bathy_class, depth_table),
    )
    size = lax.axis_size("along")
    both = ("along", "cross")
    up = [(i, i + 1) for i in range(size - 1)]
    down = [(j, i) for i, j in up]
    turned = [(0, 1), (1, 0)]
    top = lax.ppermute(hi, "along", up)
    bot = lax.ppermute(lo, "along", down)
    far = lax.ppermute(side, "cross", turned)
    ctop = lax.ppermute(chi, both, [(2 * i + a, 2 * j + b) for i, j in up for a, b in turned])
    cbot = lax.ppermute(clo, both, [(2 * i + a, 2 * j + b) for i, j in down for a, b in turned])

    field = (shape.chunks, shape.total, LANES)
    fields = lambda count: (count,) + field
    sums = (TILE, LANES)
    moved, static, level, krylov, moments = call(
        first_kernel, shape, [vmem] * 7 + [smem] * 2,
        [fields(4), fields(5), fields(1), fields(6), sums],
        [fields(4), fields(1), fields(1), (SHIPS, shape.chunks, TILE, LANES)],
        (lo, hi, top, bot, far, ctop, cbot, hull_ranges, hull_pressure),
    )
    moved, level, krylov, moments = call(
        second_kernel, shape, [vmem] * 5,
        [fields(4), fields(1), fields(6), sums],
        [fields(4), fields(1), fields(2), fields(2)],
        (shared(moments), moved, static, level, krylov),
    )
    return tuple(
        call(
            last_kernel, shape, [vmem] * 5,
            [velocity.shape, surface.shape, (2,) + surface.shape],
            [fields(2), fields(2)],
            (shared(moments), moved, static, level, krylov),
        )
    )


def solution(mesh):
    cell = P("along", "cross")
    layered = P(None, "along", "cross")
    in_specs = (layered, cell, cell, cell, P(), P(), P())
    return jax.shard_map(
        shards, mesh=mesh, in_specs=in_specs, out_specs=(layered, cell, layered), check_vma=False
    )
```

```python
import functools

import jax
import jax.numpy as jnp
from jax import lax
from jax.experimental import pallas as pl
from jax.experimental.pallas import tpu as pltpu
from jax.sharding import PartitionSpec as P

ITERS = 3
CLASSES = 16
SHIPS = 8

gravity = 9.81
time_step = 0.1
storage = 0.1
corner_weight = 0.25

LANES = 128
TILE = 8
GUARD = 8
HALO = 16
VMEM_BYTES = 24 * 1024 * 1024


class Shape:
    def __init__(self, rows, cols):
        self.rows = rows
        self.own = cols // LANES
        self.chunks = self.own + 1
        self.first = GUARD + HALO
        self.total = rows + 2 * (GUARD + HALO)


class Ring:
    def __init__(self, make, chunks, lane):
        self.make = make
        self.chunks = chunks
        self.lane = lane
        self.held = {}

    def at(self, chunk):
        entry = self.held.setdefault(chunk, {})
        if 0 not in entry:
            entry[0] = self.make(chunk)
        return entry[0]

    def rolled(self, chunk, amount):
        value = self.at(chunk)
        entry = self.held[chunk]
        if amount not in entry:
            entry[amount] = pltpu.roll(value, amount, 1)
        return entry[amount]

    def before(self, chunk, step):
        other = (chunk - 1) % self.chunks
        return jnp.where(self.lane < step, self.rolled(other, step), self.rolled(chunk, step))

    def after(self, chunk, step):
        other = (chunk + 1) % self.chunks
        amount = LANES - step
        return jnp.where(self.lane >= amount, self.rolled(other, amount), self.rolled(chunk, amount))

    def done(self, chunk):
        self.held.pop((chunk - 1) % self.chunks, None)


def lanes_of():
    return lax.broadcasted_iota(jnp.int32, (TILE, LANES), 1)


def sweep(first, tiles, body):
    def turn(number, carry):
        body(first + number * TILE)
        return carry

    lax.fori_loop(0, tiles, turn, 0)


def load(ref, index, chunk, row):
    return ref[index, chunk, pl.ds(row, TILE), :]


def store(ref, index, chunk, row, value):
    ref[index, chunk, pl.ds(row, TILE), :] = value


CONDUCT, HALF_RATE, INVERSE, HEAD, DIAGONAL = range(5)


def predict_rows(shape, vel, head_pressure, static, moved, row):
    lane = lanes_of()
    rings = [
        Ring(lambda c, k=k: load(vel, k, c, row), shape.chunks, lane) for k in range(4)
    ]
    potential = Ring(lambda c: load(head_pressure, 0, c, row), shape.chunks, lane)
    for c in range(shape.chunks):
        wet = load(static, CONDUCT, c, row) > 0.0
        rate = time_step * load(static, HALF_RATE, c, row)
        slope_a = (0.5 * time_step) * (
            load(head_pressure, 0, c, row + 1) - load(head_pressure, 0, c, row - 1)
        )
        slope_c = (0.5 * time_step) * (potential.after(c, 1) - potential.before(c, 1))
        for layer in range(2):
            along = rings[layer].at(c)
            cross = rings[2 + layer].at(c)
            up_a = (0.5 * time_step) * jnp.maximum(along, 0.0)
            dn_a = (0.5 * time_step) * jnp.minimum(along, 0.0)
            up_c = (0.5 * time_step) * jnp.maximum(cross, 0.0)
            dn_c = (0.5 * time_step) * jnp.minimum(cross, 0.0)
            centre = (
                0.8 - 3.0 * ((up_a - dn_a) + (up_c - dn_c)) - (rate if layer == 0 else 2.0 * rate)
            )
            back_a = 0.05 + 4.0 * up_a
            fore_a = 0.05 - 4.0 * dn_a
            back_c = 0.05 + 4.0 * up_c
            fore_c = 0.05 - 4.0 * dn_c
            for part, slope in ((layer, slope_a), (2 + layer, slope_c)):
                ring = rings[part]
                other = rings[part + 1 - 2 * layer].at(c)
                value = centre * ring.at(c) + rate * other - slope
                value = value + (
                    back_a * load(vel, part, c, row - 1) - up_a * load(vel, part, c, row - 2)
                )
                value = value + (
                    fore_a * load(vel, part, c, row + 1) + dn_a * load(vel, part, c, row + 2)
                )
                value = value + (back_c * ring.before(c, 1) - up_c * ring.before(c, 2))
                value = value + (fore_c * ring.after(c, 1) + dn_c * ring.after(c, 2))
                store(moved, part, c, row, jnp.where(wet, value, 0.0))
        for ring in rings:
            ring.done(c)
        potential.done(c)


def source_rows(shape, moved, static, krylov, row):
    lane = lanes_of()
    rings = [
        Ring(
            lambda c, k=k: load(static, CONDUCT, c, row) * load(moved, 2 + k, c, row),
            shape.chunks,
            lane,
        )
        for k in range(2)
    ]
    for c in range(shape.chunks):
        above = load(static, CONDUCT, c, row - 1)
        below = load(static, CONDUCT, c, row + 1)
        scale = (-0.5 / time_step) * load(static, INVERSE, c, row)
        for layer in range(2):
            flow = (
                below * load(moved, layer, c, row + 1)
                - above * load(moved, layer, c, row - 1)
                + (rings[layer].after(c, 1) - rings[layer].before(c, 1))
            )
            store(krylov, layer, c, row, scale * flow)
            rings[layer].done(c)


def link_rows(shape, krylov, static, level, row, own_only):
    lane = lanes_of()

    def plain(layer, c):
        values = [load(krylov, 2 * level + layer, c, row + d) for d in (-1, 0, 1)]
        return values[1], values[0] + values[2]

    def weighted(layer, c):
        values = [
            load(static, CONDUCT, c, row + d) * load(krylov, 2 * level + layer, c, row + d)
            for d in (-1, 0, 1)
        ]
        return values[1], values[0] + values[2]

    sides = {}

    def ring_of(kind, layer):
        def make(c):
            middle, sums = kind(layer, c)
            sides[kind, layer, c] = sums
            return middle + corner_weight * sums

        return Ring(make, shape.chunks, lane)

    rings = [(ring_of(plain, layer), ring_of(weighted, layer)) for layer in range(2)]
    for c in range(shape.own if own_only else shape.chunks):
        conduct = load(static, CONDUCT, c, row)
        rate = load(static, HALF_RATE, c, row)
        centre = [load(krylov, 2 * level + layer, c, row) for layer in range(2)]
        results = []
        for layer in range(2):
            ring, scaled = rings[layer]
            around = (ring.before(c, 1) + ring.after(c, 1)) + sides[plain, layer, c]
            flows = (scaled.before(c, 1) + scaled.after(c, 1)) + sides[weighted, layer, c]
            results.append(0.5 * (conduct * around + flows) + rate * centre[1 - layer])
            ring.done(c)
            scaled.done(c)
        yield c, centre, results


def krylov_rows(shape, krylov, static, level, row):
    for c, _, results in link_rows(shape, krylov, static, level, row, False):
        inverse = load(static, INVERSE, c, row)
        for layer in range(2):
            store(krylov, 2 * level + 2 + layer, c, row, inverse * results[layer])


def moments_of(shape, krylov, static):
    zeros = (jnp.zeros((TILE, LANES), jnp.float32),) * (2 * ITERS)

    def turn(number, sums):
        row = shape.first + number * TILE
        sums = list(sums)
        for c, top, results in link_rows(shape, krylov, static, 2, row, True):
            diagonal = load(static, DIAGONAL, c, row)
            for layer in range(2):
                low = load(krylov, layer, c, row)
                mid = load(krylov, 2 + layer, c, row)
                low_d, mid_d, top_d = diagonal * low, diagonal * mid, diagonal * top[layer]
                terms = (
                    low * low_d,
                    low * mid_d,
                    mid * mid_d,
                    mid * top_d,
                    top[layer] * top_d,
                    top[layer] * results[layer],
                )
                sums = [a + b for a, b in zip(sums, terms)]
        return tuple(sums)

    return lax.fori_loop(0, shape.rows // TILE, turn, zeros)


def put_moments(out, sums):
    lane = lanes_of()
    result = jnp.zeros((TILE, LANES), jnp.float32)
    for number, part in enumerate(sums):
        result = jnp.where(lane == number, jnp.sum(part), result)
    out[...] = jnp.broadcast_to(result[0:1, None, 0 : out.shape[2]], out.shape)


def project(shape, vel, potential, static, moved, krylov, moments, first, tiles):
    sweep(first[0], tiles[0], functools.partial(predict_rows, shape, vel, potential, static, moved))
    sweep(first[1], tiles[1], functools.partial(source_rows, shape, moved, static, krylov))
    for level in range(2):
        sweep(
            first[2 + level],
            tiles[2 + level],
            functools.partial(krylov_rows, shape, krylov, static, level),
        )
    put_moments(moments, moments_of(shape, krylov, static))


def pack_kernel(shape, vel, surface, wet, bathy, table, lo, hi, side, clo, chi):
    half = lax.axis_index("cross")
    lane = lanes_of()
    for t in range(shape.rows // TILE):
        rows = pl.ds(t * TILE, TILE)
        target, corner = (lo, clo) if t * TILE < HALO else (hi, chi)
        at = pl.ds(t * TILE % HALO, TILE)
        edges = []
        for c in range(shape.own):
            cols = pl.ds(c * LANES, LANES)
            flag = wet[rows, cols]
            number = bathy[rows, cols]
            thick = jnp.zeros((TILE, LANES), jnp.float32)
            for entry in range(CLASSES):
                thick = jnp.where(number == entry, 0.5 * table[entry], thick)
            values = [jnp.where(flag > 0, vel[k, rows, cols], 0.0) for k in range(4)]
            values += [surface[rows, cols], flag.astype(jnp.float32), thick]
            for k, value in enumerate(values):
                target[k, at, cols] = value
            if c in (0, shape.own - 1):
                edges.append(values)
        for k in range(7):
            value = jnp.where(
                half == 0,
                jnp.where(lane >= LANES // 2, edges[1][k], 0.0),
                jnp.where(lane < LANES // 2, edges[0][k], 0.0),
            )
            side[k, rows, :] = value
            corner[k, at, :] = value


def first_kernel(
    shape, lo, hi, top, bot, side, ctop, cbot, ranges, heads,
    moved, static, surface, krylov, moments,
    vel, potential, thick, columns,
):
    along = lax.axis_index("along")
    half = lax.axis_index("cross")
    lane = lanes_of()
    line = lax.broadcasted_iota(jnp.int32, (TILE, LANES), 0)
    for c in range(shape.chunks):
        if c < shape.own:
            index = half * (shape.own * LANES) + c * LANES + lane
        else:
            index = jnp.where(half == 0, shape.own * LANES, (shape.own - 1) * LANES) + lane
        for s in range(SHIPS):
            inside = jnp.logical_and(index >= ranges[2, s], index < ranges[3, s])
            columns[s, c] = jnp.where(inside, gravity * heads[s], 0.0)
    pieces = [(GUARD, top, ctop, 0), (shape.first, lo, side, 0)]
    pieces += [(shape.first + HALO, hi, side, HALO), (shape.first + shape.rows, bot, cbot, 0)]
    for base, wide, narrow, offset in pieces:

        def turn(number, carry, base=base, wide=wide, narrow=narrow, offset=offset):
            at = pl.multiple_of(number * TILE, TILE)
            row = base + number * TILE
            global_row = along * shape.rows + (row - shape.first) + line
            covered = [
                jnp.logical_and(global_row >= ranges[0, s], global_row < ranges[1, s])
                for s in range(SHIPS)
            ]
            for c in range(shape.chunks):
                if c < shape.own:
                    values = [
                        wide[k, pl.ds(at, TILE), pl.ds(c * LANES, LANES)] for k in range(7)
                    ]
                else:
                    values = [narrow[k, pl.ds(offset + at, TILE), :] for k in range(7)]
                for k in range(4):
                    store(vel, k, c, row, values[k])
                depth = values[6]
                inside = depth > 0.0
                depth = jnp.where(inside, depth, 1.0)
                head = jnp.zeros((TILE, LANES), jnp.float32)
                for s in range(SHIPS):
                    head = head + jnp.where(covered[s], columns[s, c], 0.0)
                head = jnp.where(inside, head, 0.0)
                store(surface, 0, c, row, values[4])
                store(potential, 0, c, row, gravity * values[4] + head)
                store(thick, 0, c, row, values[6])
                store(static, CONDUCT, c, row, values[5] * values[6])
                store(static, HALF_RATE, c, row, 0.5 / depth)
                store(static, HEAD, c, row, head)
            return carry

        lax.fori_loop(0, HALO // TILE, turn, 0)

    def diagonal_rows(row):
        sides = {}

        def make(c):
            sums = load(static, CONDUCT, c, row - 1) + load(static, CONDUCT, c, row + 1)
            sides[c] = sums
            return load(static, CONDUCT, c, row) + corner_weight * sums

        ring = Ring(make, shape.chunks, lane)
        for c in range(shape.chunks):
            around = ring.before(c, 1) + ring.after(c, 1) + sides[c]
            depth = load(thick, 0, c, row)
            diagonal = (
                0.5 * (around + 5.0 * load(static, CONDUCT, c, row))
                + storage * depth
                + load(static, HALF_RATE, c, row)
            )
            store(static, DIAGONAL, c, row, diagonal)
            store(static, INVERSE, c, row, jnp.where(depth > 0.0, 1.0 / diagonal, 0.0))
            ring.done(c)

    start = GUARD
    sweep(start + 4, 7, diagonal_rows)
    project(
        shape, vel, potential, static, moved, krylov, moments,
        (start + 4, start + 5, start + 6, start + 7), (7, 7, 7, 7),
    )


def coefficients(shares):
    total = jnp.sum(shares[...], axis=0)
    mu = [jnp.broadcast_to(total[:, k : k + 1], (TILE, LANES)) for k in range(2 * ITERS)]

    def norm(c):
        return sum(c[i] * c[j] * mu[i + j] for i in range(len(c)) for j in range(len(c)))

    def energy(c):
        return sum(
            c[i] * c[j] * (mu[i + j] - mu[i + j + 1]) for i in range(len(c)) for j in range(len(c))
        )

    floor = 2e-7 * mu[0]
    one = jnp.ones((TILE, LANES), jnp.float32)
    z = [one]
    search = [one]
    result = [jnp.zeros((TILE, LANES), jnp.float32)] * ITERS
    norm_now = mu[0]
    for iteration in range(ITERS):
        step = norm_now / energy(search)
        if iteration:
            step = jnp.where(norm_now > floor, step, 0.0)
        for i, c in enumerate(search):
            result[i] = result[i] + step * c
        if iteration + 1 < ITERS:
            applied = [
                (search[i] if i < len(search) else 0.0) - (search[i - 1] if i else 0.0)
                for i in range(len(search) + 1)
            ]
            z = [(z[i] if i < len(z) else 0.0) - step * applied[i] for i in range(len(applied))]
            norm_next = norm(z)
            ratio = norm_next / norm_now
            if iteration:
                ratio = jnp.where(norm_now > floor, ratio, 0.0)
            search = [z[i] + (ratio * search[i] if i < len(search) else 0.0) for i in range(len(z))]
            norm_now = norm_next
    return result


def pressure_rows(shape, factors, krylov, pressure, row):
    for c in range(shape.chunks):
        for layer in range(2):
            value = factors[0] * load(krylov, layer, c, row)
            value = value + factors[1] * load(krylov, 2 + layer, c, row)
            value = value + factors[2] * load(krylov, 4 + layer, c, row)
            store(pressure, layer, c, row, value)


def along_moved(moved, pressure, layer, c, row):
    return load(moved, layer, c, row) - (0.5 * time_step) * (
        load(pressure, layer, c, row + 1) - load(pressure, layer, c, row - 1)
    )


def move_rows(shape, moved, pressure, static, flux, put, row):
    lane = lanes_of()
    rings = [
        Ring(lambda c, k=k: load(pressure, k, c, row), shape.chunks, lane) for k in range(2)
    ]
    for c in range(shape.chunks):
        conduct = load(static, CONDUCT, c, row)
        wet = conduct > 0.0
        along = [along_moved(moved, pressure, layer, c, row) for layer in range(2)]
        cross = [
            load(moved, 2 + layer, c, row)
            - (0.5 * time_step) * (rings[layer].after(c, 1) - rings[layer].before(c, 1))
            for layer in range(2)
        ]
        for part, value in enumerate(along + cross):
            put(part, c, row, jnp.where(wet, value, 0.0))
        store(flux, 0, c, row, conduct * (along[0] + along[1]))
        store(flux, 1, c, row, conduct * (cross[0] + cross[1]))
        for ring in rings:
            ring.done(c)


def surface_rows(shape, surface, flux, chunks, put, row):
    ring = Ring(lambda c: load(flux, 1, c, row), shape.chunks, lanes_of())
    for c in range(chunks):
        value = load(surface, 0, c, row) - (0.5 * time_step) * (
            load(flux, 0, c, row + 1)
            - load(flux, 0, c, row - 1)
            + (ring.after(c, 1) - ring.before(c, 1))
        )
        put(c, row, value)
        ring.done(c)


def second_kernel(
    shape, shares, moved_in, static, surface_in, krylov_in,
    moved, surface, krylov, moments,
    vel, potential, pressure, flux,
):
    factors = coefficients(shares)
    start = GUARD
    sweep(start + 7, 7, functools.partial(pressure_rows, shape, factors, krylov_in, pressure))
    sweep(
        start + 8,
        6,
        functools.partial(
            move_rows, shape, moved_in, pressure, static, flux, functools.partial(store, vel)
        ),
    )

    def put(c, row, value):
        value = jnp.where(load(static, INVERSE, c, row) > 0.0, value, 0.0)
        store(surface, 0, c, row, value)
        store(potential, 0, c, row, gravity * value + load(static, HEAD, c, row))

    sweep(
        start + 9,
        6,
        functools.partial(surface_rows, shape, surface_in, flux, shape.chunks, put),
    )
    project(
        shape, vel, potential, static, moved, krylov, moments,
        (start + 11, start + 12, start + 13, start + 14), (6, 5, 5, 5),
    )


def last_kernel(
    shape, shares, moved, static, surface, krylov,
    new_vel, new_surface, new_pressure,
    pressure, flux,
):
    factors = coefficients(shares)
    start = shape.first
    sweep(start - 2, 5, functools.partial(pressure_rows, shape, factors, krylov, pressure))

    def put_vel(part, c, row, value):
        if c < shape.own:
            at = pl.multiple_of(row - start, TILE)
            new_vel[part, pl.ds(at, TILE), pl.ds(c * LANES, LANES)] = value
            if part < 2:
                new_pressure[part, pl.ds(at, TILE), pl.ds(c * LANES, LANES)] = load(
                    pressure, part, c, row
                )

    sweep(
        start,
        shape.rows // TILE,
        functools.partial(move_rows, shape, moved, pressure, static, flux, put_vel),
    )
    for row in (start - 1, start + shape.rows):
        for c in range(shape.own):
            one = slice(row, row + 1)
            total = jnp.zeros((1, LANES), jnp.float32)
            for layer in range(2):
                total = total + (
                    moved[layer, c, one, :]
                    - (0.5 * time_step)
                    * (
                        pressure[layer, c, row + 1 : row + 2, :]
                        - pressure[layer, c, row - 1 : row, :]
                    )
                )
            flux[0, c, one, :] = static[CONDUCT, c, one, :] * total

    def put(c, row, value):
        at = pl.multiple_of(row - start, TILE)
        new_surface[pl.ds(at, TILE), pl.ds(c * LANES, LANES)] = value

    sweep(
        start,
        shape.rows // TILE,
        functools.partial(surface_rows, shape, surface, flux, shape.own, put),
    )


def call(kernel, shape, kinds, outs, scratch, operands):
    f32 = jnp.float32
    return pl.pallas_call(
        functools.partial(kernel, shape),
        out_shape=outs,
        in_specs=[pl.BlockSpec(memory_space=kind) for kind in kinds],
        out_specs=[pl.BlockSpec(memory_space=pltpu.VMEM)] * len(outs),
        scratch_shapes=[pltpu.VMEM(s, f32) for s in scratch],
        compiler_params=pltpu.CompilerParams(vmem_limit_bytes=VMEM_BYTES),
    )(*operands)


def held(*arrays):
    return tuple(pltpu.with_memory_space_constraint(x, pltpu.VMEM) for x in arrays)


def shared(moments):
    return lax.all_to_all(moments, ("along", "cross"), 0, 0, tiled=True)


def shards(velocity, surface, wet_mask, bathy_class, depth_table, hull_ranges, hull_pressure):
    shape = Shape(*surface.shape)
    vmem, smem = pltpu.VMEM, pltpu.SMEM
    cols = surface.shape[1]
    wide, narrow = (7, HALO, cols), (7, HALO, LANES)
    lo, hi, side, clo, chi = call(
        pack_kernel, shape, [vmem] * 4 + [smem],
        [pltpu.VMEM(each, jnp.float32) for each in (wide, wide, (7, shape.rows, LANES), narrow, narrow)],
        [],
        (velocity, surface, wet_mask, bathy_class, depth_table),
    )
    size = lax.axis_size("along")
    both = ("along", "cross")
    up = [(i, i + 1) for i in range(size - 1)]
    down = [(j, i) for i, j in up]
    turned = [(0, 1), (1, 0)]
    top = lax.ppermute(hi, "along", up)
    bot = lax.ppermute(lo, "along", down)
    far = lax.ppermute(side, "cross", turned)
    ctop = lax.ppermute(chi, both, [(2 * i + a, 2 * j + b) for i, j in up for a, b in turned])
    cbot = lax.ppermute(clo, both, [(2 * i + a, 2 * j + b) for i, j in down for a, b in turned])

    field = (shape.chunks, shape.total, LANES)
    f32 = jnp.float32
    fields = lambda count: (count,) + field
    kept = lambda count: pltpu.VMEM(fields(count), f32)
    sums = jax.ShapeDtypeStruct((2 * size, 1, 8), f32)
    moved, static, level, krylov, moments = call(
        first_kernel, shape, [vmem] * 7 + [smem] * 2,
        [kept(4), kept(5), kept(1), kept(6), sums],
        [fields(4), fields(1), fields(1), (SHIPS, shape.chunks, TILE, LANES)],
        held(lo, hi, top, bot, far, ctop, cbot) + (hull_ranges.T, hull_pressure),
    )
    moved, level, krylov, moments = call(
        second_kernel, shape, [vmem] * 5,
        [kept(4), kept(1), kept(6), sums],
        [fields(4), fields(1), fields(2), fields(2)],
        (shared(moments),) + held(moved, static, level, krylov),
    )
    whole = lambda like: jax.ShapeDtypeStruct(like, f32)
    return tuple(
        call(
            last_kernel, shape, [vmem] * 5,
            [whole(velocity.shape), whole(surface.shape), whole((2,) + surface.shape)],
            [fields(2), fields(2)],
            (shared(moments),) + held(moved, static, level, krylov),
        )
    )


def solution(mesh):
    cell = P("along", "cross")
    layered = P(None, "along", "cross")
    in_specs = (layered, cell, cell, cell, P(), P(), P())
    return jax.shard_map(
        shards, mesh=mesh, in_specs=in_specs, out_specs=(layered, cell, layered), check_vma=False
    )
```

```python
import functools

import jax
import jax.numpy as jnp
from jax import lax
from jax.experimental import pallas as pl
from jax.experimental.pallas import tpu as pltpu
from jax.sharding import PartitionSpec as P

ITERS = 3
CLASSES = 16
SHIPS = 8

gravity = 9.81
time_step = 0.1
storage = 0.1
corner_weight = 0.25

LANES = 128
TILE = 8
GUARD = 8
HALO = 16
FIELDS = 7
SENT = (13, 13, 13, 13, 12, 11, 11)
OFFSETS = (0, 13, 26, 39, 52, 64, 75)
SENT_ROWS = 88
VMEM_BYTES = 24 * 1024 * 1024


class Shape:
    def __init__(self, rows, cols):
        self.rows = rows
        self.own = cols // LANES
        self.chunks = self.own + 1
        self.first = GUARD + HALO
        self.total = rows + 2 * (GUARD + HALO)


class Ring:
    def __init__(self, make, chunks, lane):
        self.make = make
        self.chunks = chunks
        self.lane = lane
        self.held = {}

    def at(self, chunk):
        entry = self.held.setdefault(chunk, {})
        if 0 not in entry:
            entry[0] = self.make(chunk)
        return entry[0]

    def rolled(self, chunk, amount):
        value = self.at(chunk)
        entry = self.held[chunk]
        if amount not in entry:
            entry[amount] = pltpu.roll(value, amount, 1)
        return entry[amount]

    def before(self, chunk, step):
        other = (chunk - 1) % self.chunks
        return jnp.where(self.lane < step, self.rolled(other, step), self.rolled(chunk, step))

    def after(self, chunk, step):
        other = (chunk + 1) % self.chunks
        amount = LANES - step
        return jnp.where(self.lane >= amount, self.rolled(other, amount), self.rolled(chunk, amount))

    def done(self, chunk):
        self.held.pop((chunk - 1) % self.chunks, None)


def lanes_of():
    return lax.broadcasted_iota(jnp.int32, (TILE, LANES), 1)


def sweep(first, tiles, body):
    def turn(number, carry):
        body(first + number * TILE)
        return carry

    lax.fori_loop(0, tiles, turn, 0)


def load(ref, index, chunk, row):
    return ref[index, chunk, pl.ds(row, TILE), :]


def store(ref, index, chunk, row, value):
    ref[index, chunk, pl.ds(row, TILE), :] = value


CONDUCT, HALF_RATE, INVERSE, HEAD, DIAGONAL = range(5)


def predict_rows(shape, vel, head_pressure, static, moved, row):
    lane = lanes_of()
    rings = [
        Ring(lambda c, k=k: load(vel, k, c, row), shape.chunks, lane) for k in range(4)
    ]
    potential = Ring(lambda c: load(head_pressure, 0, c, row), shape.chunks, lane)
    for c in range(shape.chunks):
        wet = load(static, CONDUCT, c, row) > 0.0
        rate = time_step * load(static, HALF_RATE, c, row)
        slope_a = (0.5 * time_step) * (
            load(head_pressure, 0, c, row + 1) - load(head_pressure, 0, c, row - 1)
        )
        slope_c = (0.5 * time_step) * (potential.after(c, 1) - potential.before(c, 1))
        for layer in range(2):
            along = rings[layer].at(c)
            cross = rings[2 + layer].at(c)
            up_a = (0.5 * time_step) * jnp.maximum(along, 0.0)
            dn_a = (0.5 * time_step) * jnp.minimum(along, 0.0)
            up_c = (0.5 * time_step) * jnp.maximum(cross, 0.0)
            dn_c = (0.5 * time_step) * jnp.minimum(cross, 0.0)
            centre = (
                0.8 - 3.0 * ((up_a - dn_a) + (up_c - dn_c)) - (rate if layer == 0 else 2.0 * rate)
            )
            back_a = 0.05 + 4.0 * up_a
            fore_a = 0.05 - 4.0 * dn_a
            back_c = 0.05 + 4.0 * up_c
            fore_c = 0.05 - 4.0 * dn_c
            for part, slope in ((layer, slope_a), (2 + layer, slope_c)):
                ring = rings[part]
                other = rings[part + 1 - 2 * layer].at(c)
                value = centre * ring.at(c) + rate * other - slope
                value = value + (
                    back_a * load(vel, part, c, row - 1) - up_a * load(vel, part, c, row - 2)
                )
                value = value + (
                    fore_a * load(vel, part, c, row + 1) + dn_a * load(vel, part, c, row + 2)
                )
                value = value + (back_c * ring.before(c, 1) - up_c * ring.before(c, 2))
                value = value + (fore_c * ring.after(c, 1) + dn_c * ring.after(c, 2))
                store(moved, part, c, row, jnp.where(wet, value, 0.0))
        for ring in rings:
            ring.done(c)
        potential.done(c)


def source_rows(shape, moved, static, krylov, row):
    lane = lanes_of()
    rings = [
        Ring(
            lambda c, k=k: load(static, CONDUCT, c, row) * load(moved, 2 + k, c, row),
            shape.chunks,
            lane,
        )
        for k in range(2)
    ]
    for c in range(shape.chunks):
        above = load(static, CONDUCT, c, row - 1)
        below = load(static, CONDUCT, c, row + 1)
        scale = (-0.5 / time_step) * load(static, INVERSE, c, row)
        for layer in range(2):
            flow = (
                below * load(moved, layer, c, row + 1)
                - above * load(moved, layer, c, row - 1)
                + (rings[layer].after(c, 1) - rings[layer].before(c, 1))
            )
            store(krylov, layer, c, row, scale * flow)
            rings[layer].done(c)


def link_rows(shape, krylov, static, level, row, own_only):
    lane = lanes_of()

    def plain(layer, c):
        values = [load(krylov, 2 * level + layer, c, row + d) for d in (-1, 0, 1)]
        return values[1], values[0] + values[2]

    def weighted(layer, c):
        values = [
            load(static, CONDUCT, c, row + d) * load(krylov, 2 * level + layer, c, row + d)
            for d in (-1, 0, 1)
        ]
        return values[1], values[0] + values[2]

    sides = {}

    def ring_of(kind, layer):
        def make(c):
            middle, sums = kind(layer, c)
            sides[kind, layer, c] = sums
            return middle + corner_weight * sums

        return Ring(make, shape.chunks, lane)

    rings = [(ring_of(plain, layer), ring_of(weighted, layer)) for layer in range(2)]
    for c in range(shape.own if own_only else shape.chunks):
        conduct = load(static, CONDUCT, c, row)
        rate = load(static, HALF_RATE, c, row)
        centre = [load(krylov, 2 * level + layer, c, row) for layer in range(2)]
        results = []
        for layer in range(2):
            ring, scaled = rings[layer]
            around = (ring.before(c, 1) + ring.after(c, 1)) + sides[plain, layer, c]
            flows = (scaled.before(c, 1) + scaled.after(c, 1)) + sides[weighted, layer, c]
            results.append(0.5 * (conduct * around + flows) + rate * centre[1 - layer])
            ring.done(c)
            scaled.done(c)
        yield c, centre, results


def krylov_rows(shape, krylov, static, level, row):
    for c, _, results in link_rows(shape, krylov, static, level, row, False):
        inverse = load(static, INVERSE, c, row)
        for layer in range(2):
            store(krylov, 2 * level + 2 + layer, c, row, inverse * results[layer])


def moments_of(shape, krylov, static):
    zeros = (jnp.zeros((TILE, LANES), jnp.float32),) * (2 * ITERS)

    def turn(number, sums):
        row = shape.first + number * TILE
        sums = list(sums)
        for c, top, results in link_rows(shape, krylov, static, 2, row, True):
            diagonal = load(static, DIAGONAL, c, row)
            for layer in range(2):
                low = load(krylov, layer, c, row)
                mid = load(krylov, 2 + layer, c, row)
                low_d, mid_d, top_d = diagonal * low, diagonal * mid, diagonal * top[layer]
                terms = (
                    low * low_d,
                    low * mid_d,
                    mid * mid_d,
                    mid * top_d,
                    top[layer] * top_d,
                    top[layer] * results[layer],
                )
                sums = [a + b for a, b in zip(sums, terms)]
        return tuple(sums)

    return lax.fori_loop(0, shape.rows // TILE, turn, zeros)


def put_moments(out, sums):
    lane = lanes_of()
    result = jnp.zeros((TILE, LANES), jnp.float32)
    for number, part in enumerate(sums):
        result = jnp.where(lane == number, jnp.sum(part), result)
    out[...] = jnp.broadcast_to(result[0:1, None, 0 : out.shape[2]], out.shape)


def project(shape, vel, potential, static, moved, krylov, moments, first, tiles):
    sweep(first[0], tiles[0], functools.partial(predict_rows, shape, vel, potential, static, moved))
    sweep(first[1], tiles[1], functools.partial(source_rows, shape, moved, static, krylov))
    for level in range(2):
        sweep(
            first[2 + level],
            tiles[2 + level],
            functools.partial(krylov_rows, shape, krylov, static, level),
        )
    put_moments(moments, moments_of(shape, krylov, static))


def pack_kernel(
    shape, vel_in, surface_in, wet_in, bathy_in, table_in,
    own, side, lo, hi, clo, chi,
    vel, surface, wet, bathy, table, arrived,
):
    copies = [
        pltpu.make_async_copy(source, target, arrived.at[number])
        for number, (source, target) in enumerate(
            (
                (table_in, table),
                (bathy_in, bathy),
                (wet_in, wet),
                (surface_in, surface),
                (vel_in, vel),
            )
        )
    ]
    for copy in copies:
        copy.start()
    half = lax.axis_index("cross")
    lane = lanes_of()
    for copy in copies:
        copy.wait()

    def turn(number, carry):
        rows = pl.ds(pl.multiple_of(number * TILE, TILE), TILE)
        edges = []
        for c in range(shape.own):
            cols = pl.ds(c * LANES, LANES)
            flag = wet[rows, cols]
            entry = bathy[rows, cols]
            thick = jnp.zeros((TILE, LANES), jnp.float32)
            for choice in range(CLASSES):
                thick = jnp.where(entry == choice, 0.5 * table[choice], thick)
            values = [jnp.where(flag > 0, vel[k, rows, cols], 0.0) for k in range(4)]
            values += [surface[rows, cols], flag.astype(jnp.float32), thick]
            for k, value in enumerate(values):
                own[k, c, rows, :] = value
            if c in (0, shape.own - 1):
                edges.append(values)
        for k in range(FIELDS):
            side[k, 0, rows, :] = jnp.where(
                half == 0,
                jnp.where(lane >= LANES // 2, edges[1][k], 0.0),
                jnp.where(lane < LANES // 2, edges[0][k], 0.0),
            )
        return carry

    lax.fori_loop(0, shape.rows // TILE, turn, 0)
    for source, first, last, chunks in ((own, lo, hi, shape.own), (side, clo, chi, 1)):
        for c in range(chunks):
            for k in range(FIELDS):
                for part in (0, SENT[k] - TILE):
                    to = pl.ds(OFFSETS[k] + part, TILE)
                    first[c, to, :] = source[k, c, pl.ds(part, TILE), :]
                    start = shape.rows - SENT[k] + part
                    last[c, to, :] = source[k, c, pl.ds(start, TILE), :]


def head_kernel(shape, ranges, heads, head, columns):
    along = lax.axis_index("along")
    half = lax.axis_index("cross")
    lane = lanes_of()
    line = lax.broadcasted_iota(jnp.int32, (TILE, LANES), 0)
    for c in range(shape.chunks):
        if c < shape.own:
            index = half * (shape.own * LANES) + c * LANES + lane
        else:
            index = jnp.where(half == 0, shape.own * LANES, (shape.own - 1) * LANES) + lane
        for s in range(SHIPS):
            inside = jnp.logical_and(index >= ranges[2, s], index < ranges[3, s])
            columns[s, c] = jnp.where(inside, gravity * heads[s], 0.0)

    def head_rows(row):
        global_row = along * shape.rows + (row - shape.first) + line
        covered = [
            jnp.logical_and(global_row >= ranges[0, s], global_row < ranges[1, s])
            for s in range(SHIPS)
        ]
        for c in range(shape.chunks):
            value = jnp.zeros((TILE, LANES), jnp.float32)
            for s in range(SHIPS):
                value = value + jnp.where(covered[s], columns[s, c], 0.0)
            store(head, 0, c, row, value)

    sweep(GUARD, shape.total // TILE - 2, head_rows)


def first_kernel(
    shape, own, side, top, bot, ctop, cbot, head,
    moved, static, surface, krylov, moments,
    vel, potential, thick,
):
    along = lax.axis_index("along")
    lane = lanes_of()

    def place(c, row, values):
        for k in range(4):
            store(vel, k, c, row, values[k])
        depth = values[6]
        inside = depth > 0.0
        ship = jnp.where(inside, load(head, 0, c, row), 0.0)
        store(surface, 0, c, row, values[4])
        store(potential, 0, c, row, gravity * values[4] + ship)
        store(thick, 0, c, row, depth)
        store(static, CONDUCT, c, row, values[5] * depth)
        store(static, HALF_RATE, c, row, 0.5 / jnp.where(inside, depth, 1.0))
        store(static, HEAD, c, row, ship)

    def own_rows(number, carry):
        at = number * TILE
        for c in range(shape.chunks):
            source, chunk = (own, c) if c < shape.own else (side, 0)
            values = [load(source, k, chunk, at) for k in range(FIELDS)]
            place(c, shape.first + at, values)
        return carry

    lax.fori_loop(0, shape.rows // TILE, own_rows, 0)
    deepest = SENT[0]
    for wide, narrow, keep, starts in (
        (top, ctop, along > 0, (-deepest, -TILE)),
        (bot, cbot, along < lax.axis_size("along") - 1, (0, deepest - TILE)),
    ):
        for start in starts:
            for c in range(shape.chunks):
                source, chunk = (wide, c) if c < shape.own else (narrow, 0)
                values = []
                for k in range(FIELDS):
                    at = OFFSETS[k] + (start if start > 0 or starts[0] == 0 else SENT[k] + start)
                    value = source[chunk, pl.ds(at, TILE), :]
                    values.append(jnp.where(keep, value, 0.0))
                base = shape.first + (shape.rows if starts[0] == 0 else 0)
                place(c, base + start, values)

    def diagonal_rows(row):
        sides = {}

        def make(c):
            sums = load(static, CONDUCT, c, row - 1) + load(static, CONDUCT, c, row + 1)
            sides[c] = sums
            return load(static, CONDUCT, c, row) + corner_weight * sums

        ring = Ring(make, shape.chunks, lane)
        for c in range(shape.chunks):
            around = ring.before(c, 1) + ring.after(c, 1) + sides[c]
            depth = load(thick, 0, c, row)
            diagonal = (
                0.5 * (around + 5.0 * load(static, CONDUCT, c, row))
                + storage * depth
                + load(static, HALF_RATE, c, row)
            )
            store(static, DIAGONAL, c, row, diagonal)
            store(static, INVERSE, c, row, jnp.where(depth > 0.0, 1.0 / diagonal, 0.0))
            ring.done(c)

    start = GUARD
    sweep(start + 5, 7, diagonal_rows)
    project(
        shape, vel, potential, static, moved, krylov, moments,
        (start + 5, start + 6, start + 7, start + 8), (7, 7, 7, 6),
    )


def coefficients(shares):
    total = jnp.sum(shares[...], axis=0)
    mu = [jnp.broadcast_to(total[:, k : k + 1], (TILE, LANES)) for k in range(2 * ITERS)]

    def norm(c):
        return sum(c[i] * c[j] * mu[i + j] for i in range(len(c)) for j in range(len(c)))

    def energy(c):
        return sum(
            c[i] * c[j] * (mu[i + j] - mu[i + j + 1]) for i in range(len(c)) for j in range(len(c))
        )

    floor = 2e-7 * mu[0]
    one = jnp.ones((TILE, LANES), jnp.float32)
    z = [one]
    search = [one]
    result = [jnp.zeros((TILE, LANES), jnp.float32)] * ITERS
    norm_now = mu[0]
    for iteration in range(ITERS):
        step = norm_now / energy(search)
        if iteration:
            step = jnp.where(norm_now > floor, step, 0.0)
        for i, c in enumerate(search):
            result[i] = result[i] + step * c
        if iteration + 1 < ITERS:
            applied = [
                (search[i] if i < len(search) else 0.0) - (search[i - 1] if i else 0.0)
                for i in range(len(search) + 1)
            ]
            z = [(z[i] if i < len(z) else 0.0) - step * applied[i] for i in range(len(applied))]
            norm_next = norm(z)
            ratio = norm_next / norm_now
            if iteration:
                ratio = jnp.where(norm_now > floor, ratio, 0.0)
            search = [z[i] + (ratio * search[i] if i < len(search) else 0.0) for i in range(len(z))]
            norm_now = norm_next
    return result


def pressure_rows(shape, factors, krylov, pressure, row):
    for c in range(shape.chunks):
        for layer in range(2):
            value = factors[0] * load(krylov, layer, c, row)
            value = value + factors[1] * load(krylov, 2 + layer, c, row)
            value = value + factors[2] * load(krylov, 4 + layer, c, row)
            store(pressure, layer, c, row, value)


def along_moved(moved, pressure, layer, c, row):
    return load(moved, layer, c, row) - (0.5 * time_step) * (
        load(pressure, layer, c, row + 1) - load(pressure, layer, c, row - 1)
    )


def move_rows(shape, moved, pressure, static, flux, put, row):
    lane = lanes_of()
    rings = [
        Ring(lambda c, k=k: load(pressure, k, c, row), shape.chunks, lane) for k in range(2)
    ]
    for c in range(shape.chunks):
        conduct = load(static, CONDUCT, c, row)
        wet = conduct > 0.0
        along = [along_moved(moved, pressure, layer, c, row) for layer in range(2)]
        cross = [
            load(moved, 2 + layer, c, row)
            - (0.5 * time_step) * (rings[layer].after(c, 1) - rings[layer].before(c, 1))
            for layer in range(2)
        ]
        for part, value in enumerate(along + cross):
            put(part, c, row, jnp.where(wet, value, 0.0))
        store(flux, 0, c, row, conduct * (along[0] + along[1]))
        store(flux, 1, c, row, conduct * (cross[0] + cross[1]))
        for ring in rings:
            ring.done(c)


def surface_rows(shape, surface, flux, chunks, put, row):
    ring = Ring(lambda c: load(flux, 1, c, row), shape.chunks, lanes_of())
    for c in range(chunks):
        value = load(surface, 0, c, row) - (0.5 * time_step) * (
            load(flux, 0, c, row + 1)
            - load(flux, 0, c, row - 1)
            + (ring.after(c, 1) - ring.before(c, 1))
        )
        put(c, row, value)
        ring.done(c)


def second_kernel(
    shape, shares, moved_in, static, surface_in, krylov_in,
    moved, surface, krylov, moments,
    vel, potential, pressure, flux,
):
    factors = coefficients(shares)
    start = GUARD
    sweep(start + 8, 6, functools.partial(pressure_rows, shape, factors, krylov_in, pressure))
    sweep(
        start + 9,
        6,
        functools.partial(
            move_rows, shape, moved_in, pressure, static, flux, functools.partial(store, vel)
        ),
    )

    def put(c, row, value):
        value = jnp.where(load(static, INVERSE, c, row) > 0.0, value, 0.0)
        store(surface, 0, c, row, value)
        store(potential, 0, c, row, gravity * value + load(static, HEAD, c, row))

    sweep(
        start + 10,
        6,
        functools.partial(surface_rows, shape, surface_in, flux, shape.chunks, put),
    )
    project(
        shape, vel, potential, static, moved, krylov, moments,
        (start + 11, start + 12, start + 13, start + 14), (6, 5, 5, 5),
    )


def last_kernel(
    shape, shares, moved, static, surface, krylov,
    new_vel, new_surface, new_pressure,
    pressure, flux,
):
    factors = coefficients(shares)
    start = shape.first
    sweep(start - 2, 5, functools.partial(pressure_rows, shape, factors, krylov, pressure))

    def put_vel(part, c, row, value):
        if c < shape.own:
            at = pl.multiple_of(row - start, TILE)
            new_vel[part, pl.ds(at, TILE), pl.ds(c * LANES, LANES)] = value
            if part < 2:
                new_pressure[part, pl.ds(at, TILE), pl.ds(c * LANES, LANES)] = load(
                    pressure, part, c, row
                )

    sweep(
        start,
        shape.rows // TILE,
        functools.partial(move_rows, shape, moved, pressure, static, flux, put_vel),
    )
    for row in (start - 1, start + shape.rows):
        for c in range(shape.own):
            one = slice(row, row + 1)
            total = jnp.zeros((1, LANES), jnp.float32)
            for layer in range(2):
                total = total + (
                    moved[layer, c, one, :]
                    - (0.5 * time_step)
                    * (
                        pressure[layer, c, row + 1 : row + 2, :]
                        - pressure[layer, c, row - 1 : row, :]
                    )
                )
            flux[0, c, one, :] = static[CONDUCT, c, one, :] * total

    def put(c, row, value):
        at = pl.multiple_of(row - start, TILE)
        new_surface[pl.ds(at, TILE), pl.ds(c * LANES, LANES)] = value

    sweep(
        start,
        shape.rows // TILE,
        functools.partial(surface_rows, shape, surface, flux, shape.own, put),
    )


def call(kernel, shape, kinds, outs, scratch, operands, cost=None):
    return pl.pallas_call(
        functools.partial(kernel, shape),
        out_shape=outs,
        in_specs=[pl.BlockSpec(memory_space=kind) for kind in kinds],
        out_specs=[pl.BlockSpec(memory_space=pltpu.VMEM)] * len(outs),
        scratch_shapes=scratch,
        cost_estimate=cost,
        compiler_params=pltpu.CompilerParams(vmem_limit_bytes=VMEM_BYTES),
    )(*operands)


def held(*arrays):
    return tuple(pltpu.with_memory_space_constraint(x, pltpu.VMEM) for x in arrays)


def shared(moments):
    return lax.all_to_all(moments, ("along", "cross"), 0, 0, tiled=True)


def shards(velocity, surface, wet_mask, bathy_class, depth_table, hull_ranges, hull_pressure):
    shape = Shape(*surface.shape)
    vmem, smem = pltpu.VMEM, pltpu.SMEM
    f32, i32 = jnp.float32, jnp.int32
    size = lax.axis_size("along")
    field = (shape.chunks, shape.total, LANES)
    fields = lambda count: vmem((count,) + field, f32)
    sums = jax.ShapeDtypeStruct((2 * size, 1, 8), f32)
    block = surface.shape
    wide, narrow = vmem((shape.own, SENT_ROWS, LANES), f32), vmem((1, SENT_ROWS, LANES), f32)
    own, side, lo, hi, clo, chi = call(
        pack_kernel, shape, [pl.ANY] * 5,
        [
            vmem((FIELDS, shape.own, shape.rows, LANES), f32),
            vmem((FIELDS, 1, shape.rows, LANES), f32),
            wide, wide, narrow, narrow,
        ],
        [
            vmem(velocity.shape, f32), vmem(block, f32), vmem(block, i32), vmem(block, i32),
            smem(depth_table.shape, f32), pltpu.SemaphoreType.DMA((5,)),
        ],
        tuple(
            pltpu.with_memory_space_constraint(x, pltpu.HBM)
            for x in (velocity, surface, wet_mask, bathy_class, depth_table)
        ),
    )
    both = ("along", "cross")
    up = [(i, (i + 1) % size) for i in range(size)]
    down = [(j, i) for i, j in up]
    turned = [(0, 1), (1, 0)]
    top = lax.ppermute(hi, "along", up)
    bot = lax.ppermute(lo, "along", down)
    far = lax.ppermute(side, "cross", turned)
    ctop = lax.ppermute(chi, both, [(2 * i + a, 2 * j + b) for i, j in up for a, b in turned])
    cbot = lax.ppermute(clo, both, [(2 * i + a, 2 * j + b) for i, j in down for a, b in turned])
    (head,) = call(
        head_kernel, shape, [smem] * 2, [fields(1)],
        [vmem((SHIPS, shape.chunks, TILE, LANES), f32)],
        (hull_ranges.T, hull_pressure),
        pl.CostEstimate(flops=2 * 10**6, bytes_accessed=10**6, transcendentals=0),
    )
    moved, static, level, krylov, moments = call(
        first_kernel, shape, [vmem] * 7,
        [fields(4), fields(5), fields(1), fields(6), sums],
        [fields(4), fields(1), fields(1)],
        held(own, far, top, bot, ctop, cbot, head),
    )
    moved, level, krylov, moments = call(
        second_kernel, shape, [vmem] * 5,
        [fields(4), fields(1), fields(6), sums],
        [fields(4), fields(1), fields(2), fields(2)],
        (shared(moments),) + held(moved, static, level, krylov),
    )
    whole = lambda like: jax.ShapeDtypeStruct(like, f32)
    return tuple(
        call(
            last_kernel, shape, [vmem] * 5,
            [whole(velocity.shape), whole(surface.shape), whole((2,) + surface.shape)],
            [fields(2), fields(2)],
            (shared(moments),) + held(moved, static, level, krylov),
        )
    )


def solution(mesh):
    cell = P("along", "cross")
    layered = P(None, "along", "cross")
    in_specs = (layered, cell, cell, cell, P(), P(), P())
    return jax.shard_map(
        shards, mesh=mesh, in_specs=in_specs, out_specs=(layered, cell, layered), check_vma=False
    )
```

```python
import functools

import jax
import jax.numpy as jnp
from jax import lax
from jax.experimental import pallas as pl
from jax.experimental.pallas import tpu as pltpu
from jax.sharding import PartitionSpec as P

ITERS = 3
CLASSES = 16
SHIPS = 8

gravity = 9.81
time_step = 0.1
storage = 0.1
corner_weight = 0.25

LANES = 128
TILE = 8
GUARD = 8
HALO = 16
FIELDS = 7
SENT = (13, 13, 13, 13, 12, 11, 11)
OFFSETS = (0, 13, 26, 39, 52, 64, 75)
SENT_ROWS = 88
EDGE = 16
SLOTS = LANES // EDGE
VMEM_BYTES = 24 * 1024 * 1024


class Shape:
    def __init__(self, rows, cols):
        self.rows = rows
        self.own = cols // LANES
        self.chunks = self.own + 1
        self.first = GUARD + HALO
        self.total = rows + 2 * (GUARD + HALO)


class Ring:
    def __init__(self, make, chunks, lane):
        self.make = make
        self.chunks = chunks
        self.lane = lane
        self.held = {}

    def at(self, chunk):
        entry = self.held.setdefault(chunk, {})
        if 0 not in entry:
            entry[0] = self.make(chunk)
        return entry[0]

    def rolled(self, chunk, amount):
        value = self.at(chunk)
        entry = self.held[chunk]
        if amount not in entry:
            entry[amount] = pltpu.roll(value, amount, 1)
        return entry[amount]

    def before(self, chunk, step):
        other = (chunk - 1) % self.chunks
        return jnp.where(self.lane < step, self.rolled(other, step), self.rolled(chunk, step))

    def after(self, chunk, step):
        other = (chunk + 1) % self.chunks
        amount = LANES - step
        return jnp.where(self.lane >= amount, self.rolled(other, amount), self.rolled(chunk, amount))

    def done(self, chunk):
        self.held.pop((chunk - 1) % self.chunks, None)


def lanes_of():
    return lax.broadcasted_iota(jnp.int32, (TILE, LANES), 1)


def sweep(first, tiles, body):
    def turn(number, carry):
        body(first + number * TILE)
        return carry

    lax.fori_loop(0, tiles, turn, 0)


def load(ref, index, chunk, row):
    return ref[index, chunk, pl.ds(row, TILE), :]


def store(ref, index, chunk, row, value):
    ref[index, chunk, pl.ds(row, TILE), :] = value


CONDUCT, HALF_RATE, INVERSE, HEAD, DIAGONAL = range(5)


def predict_rows(shape, vel, head_pressure, static, moved, row):
    lane = lanes_of()
    rings = [
        Ring(lambda c, k=k: load(vel, k, c, row), shape.chunks, lane) for k in range(4)
    ]
    potential = Ring(lambda c: load(head_pressure, 0, c, row), shape.chunks, lane)
    for c in range(shape.chunks):
        wet = load(static, CONDUCT, c, row) > 0.0
        rate = time_step * load(static, HALF_RATE, c, row)
        slope_a = (0.5 * time_step) * (
            load(head_pressure, 0, c, row + 1) - load(head_pressure, 0, c, row - 1)
        )
        slope_c = (0.5 * time_step) * (potential.after(c, 1) - potential.before(c, 1))
        for layer in range(2):
            along = rings[layer].at(c)
            cross = rings[2 + layer].at(c)
            up_a = (0.5 * time_step) * jnp.maximum(along, 0.0)
            dn_a = (0.5 * time_step) * jnp.minimum(along, 0.0)
            up_c = (0.5 * time_step) * jnp.maximum(cross, 0.0)
            dn_c = (0.5 * time_step) * jnp.minimum(cross, 0.0)
            centre = (
                0.8 - 3.0 * ((up_a - dn_a) + (up_c - dn_c)) - (rate if layer == 0 else 2.0 * rate)
            )
            back_a = 0.05 + 4.0 * up_a
            fore_a = 0.05 - 4.0 * dn_a
            back_c = 0.05 + 4.0 * up_c
            fore_c = 0.05 - 4.0 * dn_c
            for part, slope in ((layer, slope_a), (2 + layer, slope_c)):
                ring = rings[part]
                other = rings[part + 1 - 2 * layer].at(c)
                value = centre * ring.at(c) + rate * other - slope
                value = value + (
                    back_a * load(vel, part, c, row - 1) - up_a * load(vel, part, c, row - 2)
                )
                value = value + (
                    fore_a * load(vel, part, c, row + 1) + dn_a * load(vel, part, c, row + 2)
                )
                value = value + (back_c * ring.before(c, 1) - up_c * ring.before(c, 2))
                value = value + (fore_c * ring.after(c, 1) + dn_c * ring.after(c, 2))
                store(moved, part, c, row, jnp.where(wet, value, 0.0))
        for ring in rings:
            ring.done(c)
        potential.done(c)


def source_rows(shape, moved, static, krylov, row):
    lane = lanes_of()
    rings = [
        Ring(
            lambda c, k=k: load(static, CONDUCT, c, row) * load(moved, 2 + k, c, row),
            shape.chunks,
            lane,
        )
        for k in range(2)
    ]
    for c in range(shape.chunks):
        above = load(static, CONDUCT, c, row - 1)
        below = load(static, CONDUCT, c, row + 1)
        scale = (-0.5 / time_step) * load(static, INVERSE, c, row)
        for layer in range(2):
            flow = (
                below * load(moved, layer, c, row + 1)
                - above * load(moved, layer, c, row - 1)
                + (rings[layer].after(c, 1) - rings[layer].before(c, 1))
            )
            store(krylov, layer, c, row, scale * flow)
            rings[layer].done(c)


def link_rows(shape, krylov, static, level, row, own_only):
    lane = lanes_of()

    def plain(layer, c):
        values = [load(krylov, 2 * level + layer, c, row + d) for d in (-1, 0, 1)]
        return values[1], values[0] + values[2]

    def weighted(layer, c):
        values = [
            load(static, CONDUCT, c, row + d) * load(krylov, 2 * level + layer, c, row + d)
            for d in (-1, 0, 1)
        ]
        return values[1], values[0] + values[2]

    sides = {}

    def ring_of(kind, layer):
        def make(c):
            middle, sums = kind(layer, c)
            sides[kind, layer, c] = sums
            return middle + corner_weight * sums

        return Ring(make, shape.chunks, lane)

    rings = [(ring_of(plain, layer), ring_of(weighted, layer)) for layer in range(2)]
    for c in range(shape.own if own_only else shape.chunks):
        conduct = load(static, CONDUCT, c, row)
        rate = load(static, HALF_RATE, c, row)
        centre = [load(krylov, 2 * level + layer, c, row) for layer in range(2)]
        results = []
        for layer in range(2):
            ring, scaled = rings[layer]
            around = (ring.before(c, 1) + ring.after(c, 1)) + sides[plain, layer, c]
            flows = (scaled.before(c, 1) + scaled.after(c, 1)) + sides[weighted, layer, c]
            results.append(0.5 * (conduct * around + flows) + rate * centre[1 - layer])
            ring.done(c)
            scaled.done(c)
        yield c, centre, results


def krylov_rows(shape, krylov, static, level, row):
    for c, _, results in link_rows(shape, krylov, static, level, row, False):
        inverse = load(static, INVERSE, c, row)
        for layer in range(2):
            store(krylov, 2 * level + 2 + layer, c, row, inverse * results[layer])


def moments_of(shape, krylov, static):
    zeros = (jnp.zeros((TILE, LANES), jnp.float32),) * (2 * ITERS)

    def turn(number, sums):
        row = shape.first + number * TILE
        sums = list(sums)
        for c, top, results in link_rows(shape, krylov, static, 2, row, True):
            diagonal = load(static, DIAGONAL, c, row)
            for layer in range(2):
                low = load(krylov, layer, c, row)
                mid = load(krylov, 2 + layer, c, row)
                low_d, mid_d, top_d = diagonal * low, diagonal * mid, diagonal * top[layer]
                terms = (
                    low * low_d,
                    low * mid_d,
                    mid * mid_d,
                    mid * top_d,
                    top[layer] * top_d,
                    top[layer] * results[layer],
                )
                sums = [a + b for a, b in zip(sums, terms)]
        return tuple(sums)

    return lax.fori_loop(0, shape.rows // TILE, turn, zeros)


def put_moments(out, sums):
    lane = lanes_of()
    result = jnp.zeros((TILE, LANES), jnp.float32)
    for number, part in enumerate(sums):
        result = jnp.where(lane == number, jnp.sum(part), result)
    out[...] = jnp.broadcast_to(result[0:1, None, 0 : out.shape[2]], out.shape)


def project(shape, vel, potential, static, moved, krylov, moments, first, tiles):
    sweep(first[0], tiles[0], functools.partial(predict_rows, shape, vel, potential, static, moved))
    sweep(first[1], tiles[1], functools.partial(source_rows, shape, moved, static, krylov))
    for level in range(2):
        sweep(
            first[2 + level],
            tiles[2 + level],
            functools.partial(krylov_rows, shape, krylov, static, level),
        )
    put_moments(moments, moments_of(shape, krylov, static))


def pack_kernel(
    shape, vel_in, surface_in, wet_in, bathy_in, table_in,
    own, lo, hi, side, clo, chi,
    vel, surface, wet, bathy, table, edge, arrived,
):
    copies = [
        pltpu.make_async_copy(source, target, arrived.at[number])
        for number, (source, target) in enumerate(
            (
                (table_in, table),
                (bathy_in, bathy),
                (wet_in, wet),
                (surface_in, surface),
                (vel_in, vel),
            )
        )
    ]
    for copy in copies:
        copy.start()
    half = lax.axis_index("cross")
    lane = lanes_of()
    for copy in copies:
        copy.wait()

    def turn(number, carry):
        rows = pl.ds(pl.multiple_of(number * TILE, TILE), TILE)
        edges = []
        for c in range(shape.own):
            cols = pl.ds(c * LANES, LANES)
            flag = wet[rows, cols]
            entry = bathy[rows, cols]
            thick = jnp.zeros((TILE, LANES), jnp.float32)
            for choice in range(CLASSES):
                thick = jnp.where(entry == choice, 0.5 * table[choice], thick)
            values = [jnp.where(flag > 0, vel[k, rows, cols], 0.0) for k in range(4)]
            values += [surface[rows, cols], flag.astype(jnp.float32), thick]
            for k, value in enumerate(values):
                own[k, c, rows, :] = value
            if c in (0, shape.own - 1):
                edges.append(values)
        for k in range(FIELDS):
            edge[k, rows, :] = jnp.where(half == 0, edges[1][k], edges[0][k])
        return carry

    lax.fori_loop(0, shape.rows // TILE, turn, 0)
    for c in range(shape.own):
        for k in range(FIELDS):
            for part in (0, SENT[k] - TILE):
                to = pl.ds(OFFSETS[k] + part, TILE)
                lo[c, to, :] = own[k, c, pl.ds(part, TILE), :]
                hi[c, to, :] = own[k, c, pl.ds(shape.rows - SENT[k] + part, TILE), :]
    shift = jnp.where(half == 0, EDGE, 0)
    squeeze(side, side_tiles(shape, edge), shift)
    squeeze(clo, corner_tiles(edge, 0), shift)
    squeeze(chi, corner_tiles(edge, shape.rows), shift)


def side_tiles(shape, edge):
    return [
        edge.at[k, pl.ds(row, TILE), :] for k in range(FIELDS) for row in range(0, shape.rows, TILE)
    ]


def corner_parts():
    return [(k, part) for k in range(FIELDS) for part in (0, SENT[k] - TILE)]


def corner_tiles(edge, rows):
    return [
        edge.at[k, pl.ds(part + (rows - SENT[k] if rows else 0), TILE), :]
        for k, part in corner_parts()
    ]


def squeeze(out, tiles, shift):
    slot = lanes_of() // EDGE
    for first in range(0, len(tiles), SLOTS):
        value = jnp.zeros((TILE, LANES), jnp.float32)
        for number, tile in enumerate(tiles[first : first + SLOTS]):
            moved = pltpu.roll(tile[...], lax.rem(EDGE * number + shift, LANES), 1)
            value = jnp.where(slot == number, moved, value)
        out[pl.ds(first, TILE), :] = value


def spread(source, number, half):
    lane = lanes_of()
    tile = source[pl.ds(number // SLOTS * TILE, TILE), :]
    amount = LANES - EDGE * (number % SLOTS) - jnp.where(half == 0, 0, EDGE)
    moved = pltpu.roll(tile, lax.rem(amount + LANES, LANES), 1)
    wanted = jnp.where(half == 0, lane, LANES - 1 - lane) < EDGE
    return jnp.where(wanted, moved, 0.0)


def head_kernel(shape, ranges, heads, head, columns):
    along = lax.axis_index("along")
    half = lax.axis_index("cross")
    lane = lanes_of()
    line = lax.broadcasted_iota(jnp.int32, (TILE, LANES), 0)
    for c in range(shape.chunks):
        if c < shape.own:
            index = half * (shape.own * LANES) + c * LANES + lane
        else:
            index = jnp.where(half == 0, shape.own * LANES, (shape.own - 1) * LANES) + lane
        for s in range(SHIPS):
            inside = jnp.logical_and(index >= ranges[2, s], index < ranges[3, s])
            columns[s, c] = jnp.where(inside, gravity * heads[s], 0.0)

    def head_rows(row):
        global_row = along * shape.rows + (row - shape.first) + line
        covered = [
            jnp.logical_and(global_row >= ranges[0, s], global_row < ranges[1, s])
            for s in range(SHIPS)
        ]
        for c in range(shape.chunks):
            value = jnp.zeros((TILE, LANES), jnp.float32)
            for s in range(SHIPS):
                value = value + jnp.where(covered[s], columns[s, c], 0.0)
            store(head, 0, c, row, value)

    sweep(GUARD, shape.total // TILE - 2, head_rows)


def first_kernel(
    shape, own, side_in, top, bot, ctop_in, cbot_in, head,
    moved, static, surface, krylov, moments,
    vel, potential, thick, side, ctop, cbot,
):
    along = lax.axis_index("along")
    half = lax.axis_index("cross")
    for number, tile in enumerate(side_tiles(shape, side)):
        tile[...] = spread(side_in, number, half)
    for number, (k, part) in enumerate(corner_parts()):
        to = pl.ds(OFFSETS[k] + part, TILE)
        ctop[0, to, :] = spread(ctop_in, number, half)
        cbot[0, to, :] = spread(cbot_in, number, half)
    lane = lanes_of()

    def place(c, row, values):
        for k in range(4):
            store(vel, k, c, row, values[k])
        depth = values[6]
        inside = depth > 0.0
        ship = jnp.where(inside, load(head, 0, c, row), 0.0)
        store(surface, 0, c, row, values[4])
        store(potential, 0, c, row, gravity * values[4] + ship)
        store(thick, 0, c, row, depth)
        store(static, CONDUCT, c, row, values[5] * depth)
        store(static, HALF_RATE, c, row, 0.5 / jnp.where(inside, depth, 1.0))
        store(static, HEAD, c, row, ship)

    def own_rows(number, carry):
        at = number * TILE
        for c in range(shape.chunks):
            if c < shape.own:
                values = [load(own, k, c, at) for k in range(FIELDS)]
            else:
                values = [side[k, pl.ds(at, TILE), :] for k in range(FIELDS)]
            place(c, shape.first + at, values)
        return carry

    lax.fori_loop(0, shape.rows // TILE, own_rows, 0)
    deepest = SENT[0]
    for wide, narrow, keep, starts in (
        (top, ctop, along > 0, (-deepest, -TILE)),
        (bot, cbot, along < lax.axis_size("along") - 1, (0, deepest - TILE)),
    ):
        for start in starts:
            for c in range(shape.chunks):
                source, chunk = (wide, c) if c < shape.own else (narrow, 0)
                values = []
                for k in range(FIELDS):
                    at = OFFSETS[k] + (start if start > 0 or starts[0] == 0 else SENT[k] + start)
                    value = source[chunk, pl.ds(at, TILE), :]
                    values.append(jnp.where(keep, value, 0.0))
                base = shape.first + (shape.rows if starts[0] == 0 else 0)
                place(c, base + start, values)

    def diagonal_rows(row):
        sides = {}

        def make(c):
            sums = load(static, CONDUCT, c, row - 1) + load(static, CONDUCT, c, row + 1)
            sides[c] = sums
            return load(static, CONDUCT, c, row) + corner_weight * sums

        ring = Ring(make, shape.chunks, lane)
        for c in range(shape.chunks):
            around = ring.before(c, 1) + ring.after(c, 1) + sides[c]
            depth = load(thick, 0, c, row)
            diagonal = (
                0.5 * (around + 5.0 * load(static, CONDUCT, c, row))
                + storage * depth
                + load(static, HALF_RATE, c, row)
            )
            store(static, DIAGONAL, c, row, diagonal)
            store(static, INVERSE, c, row, jnp.where(depth > 0.0, 1.0 / diagonal, 0.0))
            ring.done(c)

    start = GUARD
    sweep(start + 5, 7, diagonal_rows)
    project(
        shape, vel, potential, static, moved, krylov, moments,
        (start + 5, start + 6, start + 7, start + 8), (7, 7, 7, 6),
    )


def coefficients(shares):
    total = jnp.sum(shares[...], axis=0)
    mu = [jnp.broadcast_to(total[:, k : k + 1], (TILE, LANES)) for k in range(2 * ITERS)]

    def norm(c):
        return sum(c[i] * c[j] * mu[i + j] for i in range(len(c)) for j in range(len(c)))

    def energy(c):
        return sum(
            c[i] * c[j] * (mu[i + j] - mu[i + j + 1]) for i in range(len(c)) for j in range(len(c))
        )

    floor = 2e-7 * mu[0]
    one = jnp.ones((TILE, LANES), jnp.float32)
    z = [one]
    search = [one]
    result = [jnp.zeros((TILE, LANES), jnp.float32)] * ITERS
    norm_now = mu[0]
    for iteration in range(ITERS):
        step = norm_now / energy(search)
        if iteration:
            step = jnp.where(norm_now > floor, step, 0.0)
        for i, c in enumerate(search):
            result[i] = result[i] + step * c
        if iteration + 1 < ITERS:
            applied = [
                (search[i] if i < len(search) else 0.0) - (search[i - 1] if i else 0.0)
                for i in range(len(search) + 1)
            ]
            z = [(z[i] if i < len(z) else 0.0) - step * applied[i] for i in range(len(applied))]
            norm_next = norm(z)
            ratio = norm_next / norm_now
            if iteration:
                ratio = jnp.where(norm_now > floor, ratio, 0.0)
            search = [z[i] + (ratio * search[i] if i < len(search) else 0.0) for i in range(len(z))]
            norm_now = norm_next
    return result


def pressure_rows(shape, factors, krylov, pressure, row):
    for c in range(shape.chunks):
        for layer in range(2):
            value = factors[0] * load(krylov, layer, c, row)
            value = value + factors[1] * load(krylov, 2 + layer, c, row)
            value = value + factors[2] * load(krylov, 4 + layer, c, row)
            store(pressure, layer, c, row, value)


def along_moved(moved, pressure, layer, c, row):
    return load(moved, layer, c, row) - (0.5 * time_step) * (
        load(pressure, layer, c, row + 1) - load(pressure, layer, c, row - 1)
    )


def move_rows(shape, moved, pressure, static, flux, put, row):
    lane = lanes_of()
    rings = [
        Ring(lambda c, k=k: load(pressure, k, c, row), shape.chunks, lane) for k in range(2)
    ]
    for c in range(shape.chunks):
        conduct = load(static, CONDUCT, c, row)
        wet = conduct > 0.0
        along = [along_moved(moved, pressure, layer, c, row) for layer in range(2)]
        cross = [
            load(moved, 2 + layer, c, row)
            - (0.5 * time_step) * (rings[layer].after(c, 1) - rings[layer].before(c, 1))
            for layer in range(2)
        ]
        for part, value in enumerate(along + cross):
            put(part, c, row, jnp.where(wet, value, 0.0))
        store(flux, 0, c, row, conduct * (along[0] + along[1]))
        store(flux, 1, c, row, conduct * (cross[0] + cross[1]))
        for ring in rings:
            ring.done(c)


def surface_rows(shape, surface, flux, chunks, put, row):
    ring = Ring(lambda c: load(flux, 1, c, row), shape.chunks, lanes_of())
    for c in range(chunks):
        value = load(surface, 0, c, row) - (0.5 * time_step) * (
            load(flux, 0, c, row + 1)
            - load(flux, 0, c, row - 1)
            + (ring.after(c, 1) - ring.before(c, 1))
        )
        put(c, row, value)
        ring.done(c)


def second_kernel(
    shape, shares, moved_in, static, surface_in, krylov_in,
    moved, surface, krylov, moments,
    vel, potential, pressure, flux,
):
    factors = coefficients(shares)
    start = GUARD
    sweep(start + 8, 6, functools.partial(pressure_rows, shape, factors, krylov_in, pressure))
    sweep(
        start + 9,
        6,
        functools.partial(
            move_rows, shape, moved_in, pressure, static, flux, functools.partial(store, vel)
        ),
    )

    def put(c, row, value):
        value = jnp.where(load(static, INVERSE, c, row) > 0.0, value, 0.0)
        store(surface, 0, c, row, value)
        store(potential, 0, c, row, gravity * value + load(static, HEAD, c, row))

    sweep(
        start + 10,
        6,
        functools.partial(surface_rows, shape, surface_in, flux, shape.chunks, put),
    )
    project(
        shape, vel, potential, static, moved, krylov, moments,
        (start + 11, start + 12, start + 13, start + 14), (6, 5, 5, 5),
    )


def last_kernel(
    shape, shares, moved, static, surface, krylov,
    new_vel, new_surface, new_pressure,
    pressure, flux,
):
    factors = coefficients(shares)
    start = shape.first
    sweep(start - 2, 5, functools.partial(pressure_rows, shape, factors, krylov, pressure))

    def put_vel(part, c, row, value):
        if c < shape.own:
            at = pl.multiple_of(row - start, TILE)
            new_vel[part, pl.ds(at, TILE), pl.ds(c * LANES, LANES)] = value
            if part < 2:
                new_pressure[part, pl.ds(at, TILE), pl.ds(c * LANES, LANES)] = load(
                    pressure, part, c, row
                )

    sweep(
        start,
        shape.rows // TILE,
        functools.partial(move_rows, shape, moved, pressure, static, flux, put_vel),
    )
    for row in (start - 1, start + shape.rows):
        for c in range(shape.own):
            one = slice(row, row + 1)
            total = jnp.zeros((1, LANES), jnp.float32)
            for layer in range(2):
                total = total + (
                    moved[layer, c, one, :]
                    - (0.5 * time_step)
                    * (
                        pressure[layer, c, row + 1 : row + 2, :]
                        - pressure[layer, c, row - 1 : row, :]
                    )
                )
            flux[0, c, one, :] = static[CONDUCT, c, one, :] * total

    def put(c, row, value):
        at = pl.multiple_of(row - start, TILE)
        new_surface[pl.ds(at, TILE), pl.ds(c * LANES, LANES)] = value

    sweep(
        start,
        shape.rows // TILE,
        functools.partial(surface_rows, shape, surface, flux, shape.own, put),
    )


def call(kernel, shape, kinds, outs, scratch, operands, cost=None):
    return pl.pallas_call(
        functools.partial(kernel, shape),
        out_shape=outs,
        in_specs=[pl.BlockSpec(memory_space=kind) for kind in kinds],
        out_specs=[pl.BlockSpec(memory_space=pltpu.VMEM)] * len(outs),
        scratch_shapes=scratch,
        cost_estimate=cost,
        compiler_params=pltpu.CompilerParams(vmem_limit_bytes=VMEM_BYTES),
    )(*operands)


def held(*arrays):
    return tuple(pltpu.with_memory_space_constraint(x, pltpu.VMEM) for x in arrays)


def shared(moments):
    return lax.all_to_all(moments, ("along", "cross"), 0, 0, tiled=True)


def shards(velocity, surface, wet_mask, bathy_class, depth_table, hull_ranges, hull_pressure):
    shape = Shape(*surface.shape)
    vmem, smem = pltpu.VMEM, pltpu.SMEM
    f32, i32 = jnp.float32, jnp.int32
    size = lax.axis_size("along")
    field = (shape.chunks, shape.total, LANES)
    fields = lambda count: vmem((count,) + field, f32)
    sums = jax.ShapeDtypeStruct((2 * size, 1, 8), f32)
    block = surface.shape
    wide = vmem((shape.own, SENT_ROWS, LANES), f32)
    packed = lambda tiles: vmem((-(-tiles // SLOTS) * TILE, LANES), f32)
    narrow = packed(2 * FIELDS)
    full = vmem((FIELDS, shape.rows, LANES), f32)
    corner = vmem((1, SENT_ROWS, LANES), f32)
    own, lo, hi, side, clo, chi = call(
        pack_kernel, shape, [pl.ANY] * 5,
        [
            vmem((FIELDS, shape.own, shape.rows, LANES), f32),
            wide, wide, packed(FIELDS * shape.rows // TILE), narrow, narrow,
        ],
        [
            vmem(velocity.shape, f32), vmem(block, f32), vmem(block, i32), vmem(block, i32),
            smem(depth_table.shape, f32), full, pltpu.SemaphoreType.DMA((5,)),
        ],
        tuple(
            pltpu.with_memory_space_constraint(x, pltpu.HBM)
            for x in (velocity, surface, wet_mask, bathy_class, depth_table)
        ),
    )
    both = ("along", "cross")
    up = [(i, (i + 1) % size) for i in range(size)]
    down = [(j, i) for i, j in up]
    turned = [(0, 1), (1, 0)]
    top = lax.ppermute(hi, "along", up)
    bot = lax.ppermute(lo, "along", down)
    far = lax.ppermute(side, "cross", turned)
    ctop = lax.ppermute(chi, both, [(2 * i + a, 2 * j + b) for i, j in up for a, b in turned])
    cbot = lax.ppermute(clo, both, [(2 * i + a, 2 * j + b) for i, j in down for a, b in turned])
    (head,) = call(
        head_kernel, shape, [smem] * 2, [fields(1)],
        [vmem((SHIPS, shape.chunks, TILE, LANES), f32)],
        (hull_ranges.T, hull_pressure),
        pl.CostEstimate(flops=2 * 10**6, bytes_accessed=10**6, transcendentals=0),
    )
    moved, static, level, krylov, moments = call(
        first_kernel, shape, [vmem] * 7,
        [fields(4), fields(5), fields(1), fields(6), sums],
        [fields(4), fields(1), fields(1), full, corner, corner],
        held(own, far, top, bot, ctop, cbot, head),
    )
    moved, level, krylov, moments = call(
        second_kernel, shape, [vmem] * 5,
        [fields(4), fields(1), fields(6), sums],
        [fields(4), fields(1), fields(2), fields(2)],
        (shared(moments),) + held(moved, static, level, krylov),
    )
    whole = lambda like: jax.ShapeDtypeStruct(like, f32)
    return tuple(
        call(
            last_kernel, shape, [vmem] * 5,
            [whole(velocity.shape), whole(surface.shape), whole((2,) + surface.shape)],
            [fields(2), fields(2)],
            (shared(moments),) + held(moved, static, level, krylov),
        )
    )


def solution(mesh):
    cell = P("along", "cross")
    layered = P(None, "along", "cross")
    in_specs = (layered, cell, cell, cell, P(), P(), P())
    return jax.shard_map(
        shards, mesh=mesh, in_specs=in_specs, out_specs=(layered, cell, layered), check_vma=False
    )
```

```python
import functools

import jax
import jax.numpy as jnp
from jax import lax
from jax.experimental import pallas as pl
from jax.experimental.pallas import tpu as pltpu
from jax.sharding import PartitionSpec as P

ITERS = 3
CLASSES = 16
SHIPS = 8

gravity = 9.81
time_step = 0.1
storage = 0.1
corner_weight = 0.25

LANES = 128
TILE = 8
GUARD = 8
HALO = 16
FIELDS = 7
SENT = (13, 13, 13, 13, 12, 11, 11)
OFFSETS = (0, 13, 26, 39, 52, 64, 75)
SENT_ROWS = 88
CORNER_ROWS = 16
EDGE = 16
SLOTS = LANES // EDGE
VMEM_BYTES = 24 * 1024 * 1024


class Shape:
    def __init__(self, rows, cols):
        self.rows = rows
        self.own = cols // LANES
        self.chunks = self.own + 1
        self.first = GUARD + HALO
        self.total = rows + 2 * (GUARD + HALO)


class Ring:
    def __init__(self, make, chunks, lane):
        self.make = make
        self.chunks = chunks
        self.lane = lane
        self.held = {}

    def at(self, chunk):
        entry = self.held.setdefault(chunk, {})
        if 0 not in entry:
            entry[0] = self.make(chunk)
        return entry[0]

    def rolled(self, chunk, amount):
        value = self.at(chunk)
        entry = self.held[chunk]
        if amount not in entry:
            entry[amount] = pltpu.roll(value, amount, 1)
        return entry[amount]

    def before(self, chunk, step):
        other = (chunk - 1) % self.chunks
        return jnp.where(self.lane < step, self.rolled(other, step), self.rolled(chunk, step))

    def after(self, chunk, step):
        other = (chunk + 1) % self.chunks
        amount = LANES - step
        return jnp.where(self.lane >= amount, self.rolled(other, amount), self.rolled(chunk, amount))

    def done(self, chunk):
        self.held.pop((chunk - 1) % self.chunks, None)


def lanes_of():
    return lax.broadcasted_iota(jnp.int32, (TILE, LANES), 1)


def sweep(first, tiles, body):
    def turn(number, carry):
        body(first + number * TILE)
        return carry

    lax.fori_loop(0, tiles, turn, 0)


def load(ref, index, chunk, row):
    return ref[index, chunk, pl.ds(row, TILE), :]


def store(ref, index, chunk, row, value):
    ref[index, chunk, pl.ds(row, TILE), :] = value


CONDUCT, HALF_RATE, INVERSE, HEAD, DIAGONAL = range(5)


def predict_rows(shape, vel, head_pressure, static, moved, row):
    lane = lanes_of()
    rings = [
        Ring(lambda c, k=k: load(vel, k, c, row), shape.chunks, lane) for k in range(4)
    ]
    potential = Ring(lambda c: load(head_pressure, 0, c, row), shape.chunks, lane)
    for c in range(shape.chunks):
        wet = load(static, CONDUCT, c, row) > 0.0
        rate = time_step * load(static, HALF_RATE, c, row)
        slope_a = (0.5 * time_step) * (
            load(head_pressure, 0, c, row + 1) - load(head_pressure, 0, c, row - 1)
        )
        slope_c = (0.5 * time_step) * (potential.after(c, 1) - potential.before(c, 1))
        for layer in range(2):
            along = rings[layer].at(c)
            cross = rings[2 + layer].at(c)
            up_a = (0.5 * time_step) * jnp.maximum(along, 0.0)
            dn_a = (0.5 * time_step) * jnp.minimum(along, 0.0)
            up_c = (0.5 * time_step) * jnp.maximum(cross, 0.0)
            dn_c = (0.5 * time_step) * jnp.minimum(cross, 0.0)
            centre = (
                0.8 - 3.0 * ((up_a - dn_a) + (up_c - dn_c)) - (rate if layer == 0 else 2.0 * rate)
            )
            back_a = 0.05 + 4.0 * up_a
            fore_a = 0.05 - 4.0 * dn_a
            back_c = 0.05 + 4.0 * up_c
            fore_c = 0.05 - 4.0 * dn_c
            for part, slope in ((layer, slope_a), (2 + layer, slope_c)):
                ring = rings[part]
                other = rings[part + 1 - 2 * layer].at(c)
                value = centre * ring.at(c) + rate * other - slope
                value = value + (
                    back_a * load(vel, part, c, row - 1) - up_a * load(vel, part, c, row - 2)
                )
                value = value + (
                    fore_a * load(vel, part, c, row + 1) + dn_a * load(vel, part, c, row + 2)
                )
                value = value + (back_c * ring.before(c, 1) - up_c * ring.before(c, 2))
                value = value + (fore_c * ring.after(c, 1) + dn_c * ring.after(c, 2))
                store(moved, part, c, row, jnp.where(wet, value, 0.0))
        for ring in rings:
            ring.done(c)
        potential.done(c)


def source_rows(shape, moved, static, krylov, row):
    lane = lanes_of()
    rings = [
        Ring(
            lambda c, k=k: load(static, CONDUCT, c, row) * load(moved, 2 + k, c, row),
            shape.chunks,
            lane,
        )
        for k in range(2)
    ]
    for c in range(shape.chunks):
        above = load(static, CONDUCT, c, row - 1)
        below = load(static, CONDUCT, c, row + 1)
        scale = (-0.5 / time_step) * load(static, INVERSE, c, row)
        for layer in range(2):
            flow = (
                below * load(moved, layer, c, row + 1)
                - above * load(moved, layer, c, row - 1)
                + (rings[layer].after(c, 1) - rings[layer].before(c, 1))
            )
            store(krylov, layer, c, row, scale * flow)
            rings[layer].done(c)


def link_rows(shape, krylov, static, level, row, own_only):
    lane = lanes_of()

    def plain(layer, c):
        values = [load(krylov, 2 * level + layer, c, row + d) for d in (-1, 0, 1)]
        return values[1], values[0] + values[2]

    def weighted(layer, c):
        values = [
            load(static, CONDUCT, c, row + d) * load(krylov, 2 * level + layer, c, row + d)
            for d in (-1, 0, 1)
        ]
        return values[1], values[0] + values[2]

    sides = {}

    def ring_of(kind, layer):
        def make(c):
            middle, sums = kind(layer, c)
            sides[kind, layer, c] = sums
            return middle + corner_weight * sums

        return Ring(make, shape.chunks, lane)

    rings = [(ring_of(plain, layer), ring_of(weighted, layer)) for layer in range(2)]
    for c in range(shape.own if own_only else shape.chunks):
        conduct = load(static, CONDUCT, c, row)
        rate = load(static, HALF_RATE, c, row)
        centre = [load(krylov, 2 * level + layer, c, row) for layer in range(2)]
        results = []
        for layer in range(2):
            ring, scaled = rings[layer]
            around = (ring.before(c, 1) + ring.after(c, 1)) + sides[plain, layer, c]
            flows = (scaled.before(c, 1) + scaled.after(c, 1)) + sides[weighted, layer, c]
            results.append(0.5 * (conduct * around + flows) + rate * centre[1 - layer])
            ring.done(c)
            scaled.done(c)
        yield c, centre, results


def krylov_rows(shape, krylov, static, level, row):
    for c, _, results in link_rows(shape, krylov, static, level, row, False):
        inverse = load(static, INVERSE, c, row)
        for layer in range(2):
            store(krylov, 2 * level + 2 + layer, c, row, inverse * results[layer])


def moments_of(shape, krylov, static):
    zeros = (jnp.zeros((TILE, LANES), jnp.float32),) * (2 * ITERS)

    def turn(number, sums):
        row = shape.first + number * TILE
        sums = list(sums)
        for c, top, results in link_rows(shape, krylov, static, 2, row, True):
            diagonal = load(static, DIAGONAL, c, row)
            for layer in range(2):
                low = load(krylov, layer, c, row)
                mid = load(krylov, 2 + layer, c, row)
                low_d, mid_d, top_d = diagonal * low, diagonal * mid, diagonal * top[layer]
                terms = (
                    low * low_d,
                    low * mid_d,
                    mid * mid_d,
                    mid * top_d,
                    top[layer] * top_d,
                    top[layer] * results[layer],
                )
                sums = [a + b for a, b in zip(sums, terms)]
        return tuple(sums)

    return lax.fori_loop(0, shape.rows // TILE, turn, zeros)


def put_moments(out, sums):
    lane = lanes_of()
    result = jnp.zeros((TILE, LANES), jnp.float32)
    for number, part in enumerate(sums):
        result = jnp.where(lane == number, jnp.sum(part), result)
    out[...] = jnp.broadcast_to(result[0:1, None, 0 : out.shape[2]], out.shape)


def project(shape, vel, potential, static, moved, krylov, moments, first, tiles):
    sweep(first[0], tiles[0], functools.partial(predict_rows, shape, vel, potential, static, moved))
    sweep(first[1], tiles[1], functools.partial(source_rows, shape, moved, static, krylov))
    for level in range(2):
        sweep(
            first[2 + level],
            tiles[2 + level],
            functools.partial(krylov_rows, shape, krylov, static, level),
        )
    put_moments(moments, moments_of(shape, krylov, static))


def fetch(pairs, arrived):
    copies = [
        pltpu.make_async_copy(source, target, arrived.at[number])
        for number, (source, target) in enumerate(pairs)
    ]
    for copy in copies:
        copy.start()
    for copy in copies:
        copy.wait()


def cell_values(vel, surface, wet, bathy, table, rows, cols):
    flag = wet[rows, cols]
    entry = bathy[rows, cols]
    thick = jnp.zeros((TILE, LANES), jnp.float32)
    for choice in range(CLASSES):
        thick = jnp.where(entry == choice, 0.5 * table[choice], thick)
    values = [jnp.where(flag > 0, vel[k, rows, cols], 0.0) for k in range(4)]
    return values + [surface[rows, cols], flag.astype(jnp.float32), thick]


def edge_kernel(
    shape, vel_in, surface_in, wet_in, bathy_in, table_in, side,
    vel, surface, wet, bathy, table, edge, arrived,
):
    half = lax.axis_index("cross")
    first = jnp.where(half == 0, (shape.own - 1) * LANES, 0)
    near = pl.ds(pl.multiple_of(first, LANES), LANES)
    fetch(
        (
            (table_in, table),
            (bathy_in.at[:, near], bathy),
            (wet_in.at[:, near], wet),
            (surface_in.at[:, near], surface),
            (vel_in.at[:, :, near], vel),
        ),
        arrived,
    )
    for t in range(shape.rows // TILE):
        rows = pl.ds(t * TILE, TILE)
        values = cell_values(vel, surface, wet, bathy, table, rows, pl.ds(0, LANES))
        for k, value in enumerate(values):
            edge[k, rows, :] = value
    squeeze(side, 0, side_tiles(shape, edge), jnp.where(half == 0, EDGE, 0))


def pack_kernel(
    shape, vel_in, surface_in, wet_in, bathy_in, table_in,
    own, lo, hi,
    vel, surface, wet, bathy, table, arrived,
):
    fetch(
        (
            (table_in, table),
            (bathy_in, bathy),
            (wet_in, wet),
            (surface_in, surface),
            (vel_in, vel),
        ),
        arrived,
    )

    def turn(number, carry):
        rows = pl.ds(pl.multiple_of(number * TILE, TILE), TILE)
        for c in range(shape.own):
            cols = pl.ds(c * LANES, LANES)
            values = cell_values(vel, surface, wet, bathy, table, rows, cols)
            for k, value in enumerate(values):
                own[k, c, rows, :] = value
        return carry

    lax.fori_loop(0, shape.rows // TILE, turn, 0)
    for c in range(shape.own):
        for k in range(FIELDS):
            for part in (0, SENT[k] - TILE):
                to = pl.ds(c * SENT_ROWS + OFFSETS[k] + part, TILE)
                lo[to, :] = own[k, c, pl.ds(part, TILE), :]
                hi[to, :] = own[k, c, pl.ds(shape.rows - SENT[k] + part, TILE), :]


def corner_kernel(shape, far, lo_in, hi_in, lo, hi, side):
    half = lax.axis_index("cross")
    for number, tile in enumerate(side_tiles(shape, side)):
        tile[...] = spread(far, 0, number, half)
    shift = jnp.where(half == 0, 0, EDGE)
    squeeze(lo, shape.own * SENT_ROWS, corner_tiles(side, 0), shift)
    squeeze(hi, shape.own * SENT_ROWS, corner_tiles(side, shape.rows), shift)


def side_tiles(shape, edge):
    return [
        edge.at[k, pl.ds(row, TILE), :] for k in range(FIELDS) for row in range(0, shape.rows, TILE)
    ]


def corner_parts():
    return [(k, part) for k in range(FIELDS) for part in (0, SENT[k] - TILE)]


def corner_tiles(edge, rows):
    return [
        edge.at[k, pl.ds(part + (rows - SENT[k] if rows else 0), TILE), :]
        for k, part in corner_parts()
    ]


def squeeze(out, base, tiles, shift):
    slot = lanes_of() // EDGE
    for first in range(0, len(tiles), SLOTS):
        value = jnp.zeros((TILE, LANES), jnp.float32)
        for number, tile in enumerate(tiles[first : first + SLOTS]):
            moved = pltpu.roll(tile[...], lax.rem(EDGE * number + shift, LANES), 1)
            value = jnp.where(slot == number, moved, value)
        out[pl.ds(base + first, TILE), :] = value


def spread(source, base, number, half):
    lane = lanes_of()
    tile = source[pl.ds(base + number // SLOTS * TILE, TILE), :]
    amount = LANES - EDGE * (number % SLOTS) - jnp.where(half == 0, 0, EDGE)
    moved = pltpu.roll(tile, lax.rem(amount + LANES, LANES), 1)
    wanted = jnp.where(half == 0, lane, LANES - 1 - lane) < EDGE
    return jnp.where(wanted, moved, 0.0)


def head_kernel(shape, ranges, heads, side, head, columns):
    along = lax.axis_index("along")
    half = lax.axis_index("cross")
    lane = lanes_of()
    line = lax.broadcasted_iota(jnp.int32, (TILE, LANES), 0)
    for c in range(shape.chunks):
        if c < shape.own:
            index = half * (shape.own * LANES) + c * LANES + lane
        else:
            index = jnp.where(half == 0, shape.own * LANES, (shape.own - 1) * LANES) + lane
        for s in range(SHIPS):
            inside = jnp.logical_and(index >= ranges[2, s], index < ranges[3, s])
            columns[s, c] = jnp.where(inside, gravity * heads[s], 0.0)

    def head_rows(row):
        global_row = along * shape.rows + (row - shape.first) + line
        covered = [
            jnp.logical_and(global_row >= ranges[0, s], global_row < ranges[1, s])
            for s in range(SHIPS)
        ]
        for c in range(shape.chunks):
            value = jnp.zeros((TILE, LANES), jnp.float32)
            for s in range(SHIPS):
                value = value + jnp.where(covered[s], columns[s, c], 0.0)
            store(head, 0, c, row, value)

    sweep(GUARD, shape.total // TILE - 2, head_rows)


def first_kernel(
    shape, own, side, top, bot, head,
    moved, static, surface, krylov, moments,
    vel, potential, thick, ctop, cbot,
):
    along = lax.axis_index("along")
    half = lax.axis_index("cross")
    for number, (k, part) in enumerate(corner_parts()):
        to = pl.ds(OFFSETS[k] + part, TILE)
        ctop[to, :] = spread(top, shape.own * SENT_ROWS, number, half)
        cbot[to, :] = spread(bot, shape.own * SENT_ROWS, number, half)
    lane = lanes_of()

    def place(c, row, values):
        for k in range(4):
            store(vel, k, c, row, values[k])
        depth = values[6]
        inside = depth > 0.0
        ship = jnp.where(inside, load(head, 0, c, row), 0.0)
        store(surface, 0, c, row, values[4])
        store(potential, 0, c, row, gravity * values[4] + ship)
        store(thick, 0, c, row, depth)
        store(static, CONDUCT, c, row, values[5] * depth)
        store(static, HALF_RATE, c, row, 0.5 / jnp.where(inside, depth, 1.0))
        store(static, HEAD, c, row, ship)

    def own_rows(number, carry):
        at = number * TILE
        for c in range(shape.chunks):
            if c < shape.own:
                values = [load(own, k, c, at) for k in range(FIELDS)]
            else:
                values = [side[k, pl.ds(at, TILE), :] for k in range(FIELDS)]
            place(c, shape.first + at, values)
        return carry

    lax.fori_loop(0, shape.rows // TILE, own_rows, 0)
    deepest = SENT[0]
    for wide, narrow, keep, starts in (
        (top, ctop, along > 0, (-deepest, -TILE)),
        (bot, cbot, along < lax.axis_size("along") - 1, (0, deepest - TILE)),
    ):
        for start in starts:
            for c in range(shape.chunks):
                source, skip = (wide, c * SENT_ROWS) if c < shape.own else (narrow, 0)
                values = []
                for k in range(FIELDS):
                    at = OFFSETS[k] + (start if start > 0 or starts[0] == 0 else SENT[k] + start)
                    value = source[pl.ds(skip + at, TILE), :]
                    values.append(jnp.where(keep, value, 0.0))
                base = shape.first + (shape.rows if starts[0] == 0 else 0)
                place(c, base + start, values)

    def diagonal_rows(row):
        sides = {}

        def make(c):
            sums = load(static, CONDUCT, c, row - 1) + load(static, CONDUCT, c, row + 1)
            sides[c] = sums
            return load(static, CONDUCT, c, row) + corner_weight * sums

        ring = Ring(make, shape.chunks, lane)
        for c in range(shape.chunks):
            around = ring.before(c, 1) + ring.after(c, 1) + sides[c]
            depth = load(thick, 0, c, row)
            diagonal = (
                0.5 * (around + 5.0 * load(static, CONDUCT, c, row))
                + storage * depth
                + load(static, HALF_RATE, c, row)
            )
            store(static, DIAGONAL, c, row, diagonal)
            store(static, INVERSE, c, row, jnp.where(depth > 0.0, 1.0 / diagonal, 0.0))
            ring.done(c)

    start = GUARD
    sweep(start + 5, 7, diagonal_rows)
    project(
        shape, vel, potential, static, moved, krylov, moments,
        (start + 5, start + 6, start + 7, start + 8), (7, 7, 7, 6),
    )


def coefficients(shares):
    total = jnp.sum(shares[...], axis=0)
    mu = [jnp.broadcast_to(total[:, k : k + 1], (TILE, LANES)) for k in range(2 * ITERS)]

    def norm(c):
        return sum(c[i] * c[j] * mu[i + j] for i in range(len(c)) for j in range(len(c)))

    def energy(c):
        return sum(
            c[i] * c[j] * (mu[i + j] - mu[i + j + 1]) for i in range(len(c)) for j in range(len(c))
        )

    floor = 2e-7 * mu[0]
    one = jnp.ones((TILE, LANES), jnp.float32)
    z = [one]
    search = [one]
    result = [jnp.zeros((TILE, LANES), jnp.float32)] * ITERS
    norm_now = mu[0]
    for iteration in range(ITERS):
        step = norm_now / energy(search)
        if iteration:
            step = jnp.where(norm_now > floor, step, 0.0)
        for i, c in enumerate(search):
            result[i] = result[i] + step * c
        if iteration + 1 < ITERS:
            applied = [
                (search[i] if i < len(search) else 0.0) - (search[i - 1] if i else 0.0)
                for i in range(len(search) + 1)
            ]
            z = [(z[i] if i < len(z) else 0.0) - step * applied[i] for i in range(len(applied))]
            norm_next = norm(z)
            ratio = norm_next / norm_now
            if iteration:
                ratio = jnp.where(norm_now > floor, ratio, 0.0)
            search = [z[i] + (ratio * search[i] if i < len(search) else 0.0) for i in range(len(z))]
            norm_now = norm_next
    return result


def pressure_rows(shape, factors, krylov, pressure, row):
    for c in range(shape.chunks):
        for layer in range(2):
            value = factors[0] * load(krylov, layer, c, row)
            value = value + factors[1] * load(krylov, 2 + layer, c, row)
            value = value + factors[2] * load(krylov, 4 + layer, c, row)
            store(pressure, layer, c, row, value)


def along_moved(moved, pressure, layer, c, row):
    return load(moved, layer, c, row) - (0.5 * time_step) * (
        load(pressure, layer, c, row + 1) - load(pressure, layer, c, row - 1)
    )


def move_rows(shape, moved, pressure, static, flux, put, row):
    lane = lanes_of()
    rings = [
        Ring(lambda c, k=k: load(pressure, k, c, row), shape.chunks, lane) for k in range(2)
    ]
    for c in range(shape.chunks):
        conduct = load(static, CONDUCT, c, row)
        wet = conduct > 0.0
        along = [along_moved(moved, pressure, layer, c, row) for layer in range(2)]
        cross = [
            load(moved, 2 + layer, c, row)
            - (0.5 * time_step) * (rings[layer].after(c, 1) - rings[layer].before(c, 1))
            for layer in range(2)
        ]
        for part, value in enumerate(along + cross):
            put(part, c, row, jnp.where(wet, value, 0.0))
        store(flux, 0, c, row, conduct * (along[0] + along[1]))
        store(flux, 1, c, row, conduct * (cross[0] + cross[1]))
        for ring in rings:
            ring.done(c)


def surface_rows(shape, surface, flux, chunks, put, row):
    ring = Ring(lambda c: load(flux, 1, c, row), shape.chunks, lanes_of())
    for c in range(chunks):
        value = load(surface, 0, c, row) - (0.5 * time_step) * (
            load(flux, 0, c, row + 1)
            - load(flux, 0, c, row - 1)
            + (ring.after(c, 1) - ring.before(c, 1))
        )
        put(c, row, value)
        ring.done(c)


def second_kernel(
    shape, shares, moved_in, static, surface_in, krylov_in,
    moved, surface, krylov, moments,
    vel, potential, pressure, flux,
):
    factors = coefficients(shares)
    start = GUARD
    sweep(start + 8, 6, functools.partial(pressure_rows, shape, factors, krylov_in, pressure))
    sweep(
        start + 9,
        6,
        functools.partial(
            move_rows, shape, moved_in, pressure, static, flux, functools.partial(store, vel)
        ),
    )

    def put(c, row, value):
        value = jnp.where(load(static, INVERSE, c, row) > 0.0, value, 0.0)
        store(surface, 0, c, row, value)
        store(potential, 0, c, row, gravity * value + load(static, HEAD, c, row))

    sweep(
        start + 10,
        6,
        functools.partial(surface_rows, shape, surface_in, flux, shape.chunks, put),
    )
    project(
        shape, vel, potential, static, moved, krylov, moments,
        (start + 11, start + 12, start + 13, start + 14), (6, 5, 5, 5),
    )


def last_kernel(
    shape, shares, moved, static, surface, krylov,
    new_vel, new_surface, new_pressure,
    pressure, flux,
):
    factors = coefficients(shares)
    start = shape.first
    sweep(start - 2, 5, functools.partial(pressure_rows, shape, factors, krylov, pressure))

    def put_vel(part, c, row, value):
        if c < shape.own:
            at = pl.multiple_of(row - start, TILE)
            new_vel[part, pl.ds(at, TILE), pl.ds(c * LANES, LANES)] = value
            if part < 2:
                new_pressure[part, pl.ds(at, TILE), pl.ds(c * LANES, LANES)] = load(
                    pressure, part, c, row
                )

    sweep(
        start,
        shape.rows // TILE,
        functools.partial(move_rows, shape, moved, pressure, static, flux, put_vel),
    )
    for row in (start - 1, start + shape.rows):
        for c in range(shape.own):
            one = slice(row, row + 1)
            total = jnp.zeros((1, LANES), jnp.float32)
            for layer in range(2):
                total = total + (
                    moved[layer, c, one, :]
                    - (0.5 * time_step)
                    * (
                        pressure[layer, c, row + 1 : row + 2, :]
                        - pressure[layer, c, row - 1 : row, :]
                    )
                )
            flux[0, c, one, :] = static[CONDUCT, c, one, :] * total

    def put(c, row, value):
        at = pl.multiple_of(row - start, TILE)
        new_surface[pl.ds(at, TILE), pl.ds(c * LANES, LANES)] = value

    sweep(
        start,
        shape.rows // TILE,
        functools.partial(surface_rows, shape, surface, flux, shape.own, put),
    )


def cost(flops):
    return pl.CostEstimate(flops=flops, bytes_accessed=flops, transcendentals=0)


def call(kernel, shape, kinds, outs, scratch, operands, estimate=None, aliases={}):
    return pl.pallas_call(
        functools.partial(kernel, shape),
        out_shape=outs,
        in_specs=[pl.BlockSpec(memory_space=kind) for kind in kinds],
        out_specs=[pl.BlockSpec(memory_space=pltpu.VMEM)] * len(outs),
        scratch_shapes=scratch,
        cost_estimate=estimate,
        input_output_aliases=aliases,
        compiler_params=pltpu.CompilerParams(vmem_limit_bytes=VMEM_BYTES),
    )(*operands)


def held(*arrays):
    return tuple(pltpu.with_memory_space_constraint(x, pltpu.VMEM) for x in arrays)


def shared(moments):
    return lax.all_to_all(moments, ("along", "cross"), 0, 0, tiled=True)


def shards(velocity, surface, wet_mask, bathy_class, depth_table, hull_ranges, hull_pressure):
    shape = Shape(*surface.shape)
    vmem, smem = pltpu.VMEM, pltpu.SMEM
    f32, i32 = jnp.float32, jnp.int32
    size = lax.axis_size("along")
    field = (shape.chunks, shape.total, LANES)
    fields = lambda count: vmem((count,) + field, f32)
    sums = jax.ShapeDtypeStruct((2 * size, 1, 8), f32)
    block = surface.shape
    wide = vmem((shape.own * SENT_ROWS + CORNER_ROWS, LANES), f32)
    full = vmem((FIELDS, shape.rows, LANES), f32)
    corner = vmem((SENT_ROWS, LANES), f32)
    tiles = FIELDS * shape.rows // TILE
    table = [smem(depth_table.shape, f32)]
    arrived = [pltpu.SemaphoreType.DMA((5,))]
    near = (shape.rows, LANES)
    inputs = tuple(
        pltpu.with_memory_space_constraint(x, pltpu.HBM)
        for x in (velocity, surface, wet_mask, bathy_class, depth_table)
    )
    (side,) = call(
        edge_kernel, shape, [pl.ANY] * 5,
        [vmem((-(-tiles // SLOTS) * TILE, LANES), f32)],
        [vmem((4,) + near, f32), vmem(near, f32), vmem(near, i32), vmem(near, i32)]
        + table + [full] + arrived,
        inputs,
        cost(10**5),
    )
    far = lax.ppermute(side, "cross", [(0, 1), (1, 0)])
    own, lo, hi = call(
        pack_kernel, shape, [pl.ANY] * 5,
        [vmem((FIELDS, shape.own, shape.rows, LANES), f32), wide, wide],
        [vmem(velocity.shape, f32), vmem(block, f32), vmem(block, i32), vmem(block, i32)]
        + table + arrived,
        inputs,
        cost(4 * 10**6),
    )
    lo, hi, side = call(
        corner_kernel, shape, [vmem] * 3, [wide, wide, full], [], held(far, lo, hi),
        cost(10**5), {1: 0, 2: 1},
    )
    up = [(i, (i + 1) % size) for i in range(size)]
    down = [(j, i) for i, j in up]
    top = lax.ppermute(hi, "along", up)
    bot = lax.ppermute(lo, "along", down)
    (head,) = call(
        head_kernel, shape, [smem] * 2 + [vmem], [fields(1)],
        [vmem((SHIPS, shape.chunks, TILE, LANES), f32)],
        (hull_ranges.T, hull_pressure) + held(side),
        cost(2 * 10**6),
    )
    moved, static, level, krylov, moments = call(
        first_kernel, shape, [vmem] * 5,
        [fields(4), fields(5), fields(1), fields(6), sums],
        [fields(4), fields(1), fields(1), corner, corner],
        held(own, side, top, bot, head),
    )
    moved, level, krylov, moments = call(
        second_kernel, shape, [vmem] * 5,
        [fields(4), fields(1), fields(6), sums],
        [fields(4), fields(1), fields(2), fields(2)],
        (shared(moments),) + held(moved, static, level, krylov),
    )
    whole = lambda like: jax.ShapeDtypeStruct(like, f32)
    return tuple(
        call(
            last_kernel, shape, [vmem] * 5,
            [whole(velocity.shape), whole(surface.shape), whole((2,) + surface.shape)],
            [fields(2), fields(2)],
            (shared(moments),) + held(moved, static, level, krylov),
        )
    )


def solution(mesh):
    cell = P("along", "cross")
    layered = P(None, "along", "cross")
    in_specs = (layered, cell, cell, cell, P(), P(), P())
    return jax.shard_map(
        shards, mesh=mesh, in_specs=in_specs, out_specs=(layered, cell, layered), check_vma=False
    )
```

```python
import functools

import jax
import jax.numpy as jnp
from jax import lax
from jax.experimental import pallas as pl
from jax.experimental.pallas import tpu as pltpu
from jax.sharding import PartitionSpec as P

ITERS = 3
CLASSES = 16
SHIPS = 8

gravity = 9.81
time_step = 0.1
storage = 0.1
corner_weight = 0.25

LANES = 128
TILE = 8
GUARD = 8
HALO = 16
FIELDS = 7
SENT = (13, 13, 13, 13, 12, 11, 11)
OFFSETS = (0, 13, 26, 39, 52, 64, 75)
SENT_ROWS = 88
CORNER_ROWS = 16
EDGE = 16
SLOTS = LANES // EDGE
VMEM_BYTES = 24 * 1024 * 1024


class Shape:
    def __init__(self, rows, cols):
        self.rows = rows
        self.own = cols // LANES
        self.chunks = self.own + 1
        self.first = GUARD + HALO
        self.total = rows + 2 * (GUARD + HALO)


class Ring:
    def __init__(self, make, chunks, lane):
        self.make = make
        self.chunks = chunks
        self.lane = lane
        self.held = {}

    def at(self, chunk):
        entry = self.held.setdefault(chunk, {})
        if 0 not in entry:
            entry[0] = self.make(chunk)
        return entry[0]

    def rolled(self, chunk, amount):
        value = self.at(chunk)
        entry = self.held[chunk]
        if amount not in entry:
            entry[amount] = pltpu.roll(value, amount, 1)
        return entry[amount]

    def before(self, chunk, step):
        other = (chunk - 1) % self.chunks
        return jnp.where(self.lane < step, self.rolled(other, step), self.rolled(chunk, step))

    def after(self, chunk, step):
        other = (chunk + 1) % self.chunks
        amount = LANES - step
        return jnp.where(self.lane >= amount, self.rolled(other, amount), self.rolled(chunk, amount))

    def done(self, chunk):
        self.held.pop((chunk - 1) % self.chunks, None)


def lanes_of():
    return lax.broadcasted_iota(jnp.int32, (TILE, LANES), 1)


def sweep(first, tiles, body):
    def turn(number, carry):
        body(first + number * TILE)
        return carry

    lax.fori_loop(0, tiles, turn, 0)


def load(ref, index, chunk, row):
    return ref[index, chunk, pl.ds(row, TILE), :]


def store(ref, index, chunk, row, value):
    ref[index, chunk, pl.ds(row, TILE), :] = value


CONDUCT, HALF_RATE, INVERSE, HEAD, DIAGONAL = range(5)


def predict_rows(shape, vel, head_pressure, static, moved, row):
    lane = lanes_of()
    rings = [
        Ring(lambda c, k=k: load(vel, k, c, row), shape.chunks, lane) for k in range(4)
    ]
    potential = Ring(lambda c: load(head_pressure, 0, c, row), shape.chunks, lane)
    for c in range(shape.chunks):
        wet = load(static, CONDUCT, c, row) > 0.0
        rate = time_step * load(static, HALF_RATE, c, row)
        slope_a = (0.5 * time_step) * (
            load(head_pressure, 0, c, row + 1) - load(head_pressure, 0, c, row - 1)
        )
        slope_c = (0.5 * time_step) * (potential.after(c, 1) - potential.before(c, 1))
        for layer in range(2):
            along = rings[layer].at(c)
            cross = rings[2 + layer].at(c)
            up_a = (0.5 * time_step) * jnp.maximum(along, 0.0)
            dn_a = (0.5 * time_step) * jnp.minimum(along, 0.0)
            up_c = (0.5 * time_step) * jnp.maximum(cross, 0.0)
            dn_c = (0.5 * time_step) * jnp.minimum(cross, 0.0)
            centre = (
                0.8 - 3.0 * ((up_a - dn_a) + (up_c - dn_c)) - (rate if layer == 0 else 2.0 * rate)
            )
            back_a = 0.05 + 4.0 * up_a
            fore_a = 0.05 - 4.0 * dn_a
            back_c = 0.05 + 4.0 * up_c
            fore_c = 0.05 - 4.0 * dn_c
            for part, slope in ((layer, slope_a), (2 + layer, slope_c)):
                ring = rings[part]
                other = rings[part + 1 - 2 * layer].at(c)
                value = centre * ring.at(c) + rate * other - slope
                value = value + (
                    back_a * load(vel, part, c, row - 1) - up_a * load(vel, part, c, row - 2)
                )
                value = value + (
                    fore_a * load(vel, part, c, row + 1) + dn_a * load(vel, part, c, row + 2)
                )
                value = value + (back_c * ring.before(c, 1) - up_c * ring.before(c, 2))
                value = value + (fore_c * ring.after(c, 1) + dn_c * ring.after(c, 2))
                store(moved, part, c, row, jnp.where(wet, value, 0.0))
        for ring in rings:
            ring.done(c)
        potential.done(c)


def source_rows(shape, moved, static, krylov, row):
    lane = lanes_of()
    rings = [
        Ring(
            lambda c, k=k: load(static, CONDUCT, c, row) * load(moved, 2 + k, c, row),
            shape.chunks,
            lane,
        )
        for k in range(2)
    ]
    for c in range(shape.chunks):
        above = load(static, CONDUCT, c, row - 1)
        below = load(static, CONDUCT, c, row + 1)
        scale = (-0.5 / time_step) * load(static, INVERSE, c, row)
        for layer in range(2):
            flow = (
                below * load(moved, layer, c, row + 1)
                - above * load(moved, layer, c, row - 1)
                + (rings[layer].after(c, 1) - rings[layer].before(c, 1))
            )
            store(krylov, layer, c, row, scale * flow)
            rings[layer].done(c)


def link_rows(shape, krylov, static, level, row, own_only):
    lane = lanes_of()

    def plain(layer, c):
        values = [load(krylov, 2 * level + layer, c, row + d) for d in (-1, 0, 1)]
        return values[1], values[0] + values[2]

    def weighted(layer, c):
        values = [
            load(static, CONDUCT, c, row + d) * load(krylov, 2 * level + layer, c, row + d)
            for d in (-1, 0, 1)
        ]
        return values[1], values[0] + values[2]

    sides = {}

    def ring_of(kind, layer):
        def make(c):
            middle, sums = kind(layer, c)
            sides[kind, layer, c] = sums
            return middle + corner_weight * sums

        return Ring(make, shape.chunks, lane)

    rings = [(ring_of(plain, layer), ring_of(weighted, layer)) for layer in range(2)]
    for c in range(shape.own if own_only else shape.chunks):
        conduct = load(static, CONDUCT, c, row)
        rate = load(static, HALF_RATE, c, row)
        centre = [load(krylov, 2 * level + layer, c, row) for layer in range(2)]
        results = []
        for layer in range(2):
            ring, scaled = rings[layer]
            around = (ring.before(c, 1) + ring.after(c, 1)) + sides[plain, layer, c]
            flows = (scaled.before(c, 1) + scaled.after(c, 1)) + sides[weighted, layer, c]
            results.append(0.5 * (conduct * around + flows) + rate * centre[1 - layer])
            ring.done(c)
            scaled.done(c)
        yield c, centre, results


def krylov_rows(shape, krylov, static, level, row):
    for c, _, results in link_rows(shape, krylov, static, level, row, False):
        inverse = load(static, INVERSE, c, row)
        for layer in range(2):
            store(krylov, 2 * level + 2 + layer, c, row, inverse * results[layer])


def moments_of(shape, krylov, static):
    zeros = (jnp.zeros((TILE, LANES), jnp.float32),) * (2 * ITERS)

    def turn(number, sums):
        row = shape.first + number * TILE
        sums = list(sums)
        for c, top, results in link_rows(shape, krylov, static, 2, row, True):
            diagonal = load(static, DIAGONAL, c, row)
            for layer in range(2):
                low = load(krylov, layer, c, row)
                mid = load(krylov, 2 + layer, c, row)
                low_d, mid_d, top_d = diagonal * low, diagonal * mid, diagonal * top[layer]
                terms = (
                    low * low_d,
                    low * mid_d,
                    mid * mid_d,
                    mid * top_d,
                    top[layer] * top_d,
                    top[layer] * results[layer],
                )
                sums = [a + b for a, b in zip(sums, terms)]
        return tuple(sums)

    return lax.fori_loop(0, shape.rows // TILE, turn, zeros)


def put_moments(out, sums):
    lane = lanes_of()
    result = jnp.zeros((TILE, LANES), jnp.float32)
    for number, part in enumerate(sums):
        result = jnp.where(lane == number, jnp.sum(part), result)
    out[...] = jnp.broadcast_to(result[0:1, None, 0 : out.shape[2]], out.shape)


def project(shape, vel, potential, static, moved, krylov, moments, first, tiles):
    sweep(first[0], tiles[0], functools.partial(predict_rows, shape, vel, potential, static, moved))
    sweep(first[1], tiles[1], functools.partial(source_rows, shape, moved, static, krylov))
    for level in range(2):
        sweep(
            first[2 + level],
            tiles[2 + level],
            functools.partial(krylov_rows, shape, krylov, static, level),
        )
    put_moments(moments, moments_of(shape, krylov, static))


def fetch(pairs, arrived):
    copies = [
        pltpu.make_async_copy(source, target, arrived.at[number])
        for number, (source, target) in enumerate(pairs)
    ]
    for copy in copies:
        copy.start()
    for copy in copies:
        copy.wait()


def cell_values(vel, surface, wet, bathy, table, rows, cols):
    flag = wet[rows, cols]
    entry = bathy[rows, cols]
    thick = jnp.zeros((TILE, LANES), jnp.float32)
    for choice in range(CLASSES):
        thick = jnp.where(entry == choice, 0.5 * table[choice], thick)
    values = [jnp.where(flag > 0, vel[k, rows, cols], 0.0) for k in range(4)]
    return values + [surface[rows, cols], flag.astype(jnp.float32), thick]


def edge_kernel(
    shape, vel_in, surface_in, wet_in, bathy_in, table_in, side,
    vel, surface, wet, bathy, table, edge, arrived,
):
    half = lax.axis_index("cross")
    first = jnp.where(half == 0, (shape.own - 1) * LANES, 0)
    near = pl.ds(pl.multiple_of(first, LANES), LANES)
    fetch(
        (
            (table_in, table),
            (bathy_in.at[:, near], bathy),
            (wet_in.at[:, near], wet),
            (surface_in.at[:, near], surface),
            (vel_in.at[:, :, near], vel),
        ),
        arrived,
    )
    for t in range(shape.rows // TILE):
        rows = pl.ds(t * TILE, TILE)
        values = cell_values(vel, surface, wet, bathy, table, rows, pl.ds(0, LANES))
        for k, value in enumerate(values):
            edge[k, rows, :] = value
    squeeze(side, 0, side_tiles(shape, edge), jnp.where(half == 0, EDGE, 0))


def pack_kernel(
    shape, vel_in, surface_in, wet_in, bathy_in, table_in,
    own, out_chip, in_chip,
    vel, surface, wet, bathy, table, arrived,
):
    fetch(
        (
            (table_in, table),
            (bathy_in, bathy),
            (wet_in, wet),
            (surface_in, surface),
            (vel_in, vel),
        ),
        arrived,
    )

    def turn(number, carry):
        rows = pl.ds(pl.multiple_of(number * TILE, TILE), TILE)
        for c in range(shape.own):
            cols = pl.ds(c * LANES, LANES)
            values = cell_values(vel, surface, wet, bathy, table, rows, cols)
            for k, value in enumerate(values):
                own[k, c, rows, :] = value
        return carry

    lax.fori_loop(0, shape.rows // TILE, turn, 0)
    core = lax.rem(lax.axis_index("along"), 2)
    for c in range(shape.own):
        for k in range(FIELDS):
            for part in (0, SENT[k] - TILE):
                to = pl.ds(c * SENT_ROWS + OFFSETS[k] + part, TILE)
                last = shape.rows - SENT[k]
                out_chip[to, :] = own[k, c, pl.ds(part + core * last, TILE), :]
                in_chip[to, :] = own[k, c, pl.ds(part + (1 - core) * last, TILE), :]


def corner_kernel(shape, far, out_in, in_in, out_chip, in_chip, side):
    half = lax.axis_index("cross")
    core = lax.rem(lax.axis_index("along"), 2)
    for number, tile in enumerate(side_tiles(shape, side)):
        tile[...] = spread(far, 0, number, half)
    shift = jnp.where(half == 0, 0, EDGE)
    squeeze(out_chip, shape.own * SENT_ROWS, corner_tiles(shape, side, core), shift)
    squeeze(in_chip, shape.own * SENT_ROWS, corner_tiles(shape, side, 1 - core), shift)


def side_tiles(shape, edge):
    return [
        edge.at[k, pl.ds(row, TILE), :] for k in range(FIELDS) for row in range(0, shape.rows, TILE)
    ]


def corner_parts():
    return [(k, part) for k in range(FIELDS) for part in (0, SENT[k] - TILE)]


def corner_tiles(shape, edge, last):
    return [
        edge.at[k, pl.ds(part + last * (shape.rows - SENT[k]), TILE), :]
        for k, part in corner_parts()
    ]


def squeeze(out, base, tiles, shift):
    slot = lanes_of() // EDGE
    for first in range(0, len(tiles), SLOTS):
        value = jnp.zeros((TILE, LANES), jnp.float32)
        for number, tile in enumerate(tiles[first : first + SLOTS]):
            moved = pltpu.roll(tile[...], lax.rem(EDGE * number + shift, LANES), 1)
            value = jnp.where(slot == number, moved, value)
        out[pl.ds(base + first, TILE), :] = value


def spread(source, base, number, half):
    lane = lanes_of()
    tile = source[pl.ds(base + number // SLOTS * TILE, TILE), :]
    amount = LANES - EDGE * (number % SLOTS) - jnp.where(half == 0, 0, EDGE)
    moved = pltpu.roll(tile, lax.rem(amount + LANES, LANES), 1)
    wanted = jnp.where(half == 0, lane, LANES - 1 - lane) < EDGE
    return jnp.where(wanted, moved, 0.0)


def head_kernel(shape, ranges, heads, side, head, columns):
    along = lax.axis_index("along")
    half = lax.axis_index("cross")
    lane = lanes_of()
    line = lax.broadcasted_iota(jnp.int32, (TILE, LANES), 0)
    for c in range(shape.chunks):
        if c < shape.own:
            index = half * (shape.own * LANES) + c * LANES + lane
        else:
            index = jnp.where(half == 0, shape.own * LANES, (shape.own - 1) * LANES) + lane
        for s in range(SHIPS):
            inside = jnp.logical_and(index >= ranges[2, s], index < ranges[3, s])
            columns[s, c] = jnp.where(inside, gravity * heads[s], 0.0)

    def head_rows(row):
        global_row = along * shape.rows + (row - shape.first) + line
        covered = [
            jnp.logical_and(global_row >= ranges[0, s], global_row < ranges[1, s])
            for s in range(SHIPS)
        ]
        for c in range(shape.chunks):
            value = jnp.zeros((TILE, LANES), jnp.float32)
            for s in range(SHIPS):
                value = value + jnp.where(covered[s], columns[s, c], 0.0)
            store(head, 0, c, row, value)

    sweep(GUARD, shape.total // TILE - 2, head_rows)


def first_kernel(
    shape, own, side, out_chip, in_chip, head,
    moved, static, surface, krylov, moments,
    vel, potential, thick, out_corner, in_corner,
):
    along = lax.axis_index("along")
    half = lax.axis_index("cross")
    for number, (k, part) in enumerate(corner_parts()):
        to = pl.ds(OFFSETS[k] + part, TILE)
        out_corner[to, :] = spread(out_chip, shape.own * SENT_ROWS, number, half)
        in_corner[to, :] = spread(in_chip, shape.own * SENT_ROWS, number, half)
    lane = lanes_of()

    def place(c, row, values):
        for k in range(4):
            store(vel, k, c, row, values[k])
        depth = values[6]
        inside = depth > 0.0
        ship = jnp.where(inside, load(head, 0, c, row), 0.0)
        store(surface, 0, c, row, values[4])
        store(potential, 0, c, row, gravity * values[4] + ship)
        store(thick, 0, c, row, depth)
        store(static, CONDUCT, c, row, values[5] * depth)
        store(static, HALF_RATE, c, row, 0.5 / jnp.where(inside, depth, 1.0))
        store(static, HEAD, c, row, ship)

    def own_rows(number, carry):
        at = number * TILE
        for c in range(shape.chunks):
            if c < shape.own:
                values = [load(own, k, c, at) for k in range(FIELDS)]
            else:
                values = [side[k, pl.ds(at, TILE), :] for k in range(FIELDS)]
            place(c, shape.first + at, values)
        return carry

    lax.fori_loop(0, shape.rows // TILE, own_rows, 0)
    core = lax.rem(along, 2)
    deepest = SENT[0]
    last = lax.axis_size("along") - 1
    for wide, narrow, below in ((out_chip, out_corner, core), (in_chip, in_corner, 1 - core)):
        keep = jnp.where(below == 1, last - along, along) > 0
        for over, under in ((-deepest, 0), (-TILE, deepest - TILE)):
            row = shape.first + jnp.where(below == 1, shape.rows + under, over)
            for c in range(shape.chunks):
                source, skip = (wide, c * SENT_ROWS) if c < shape.own else (narrow, 0)
                values = []
                for k in range(FIELDS):
                    at = skip + OFFSETS[k] + jnp.where(below == 1, under, SENT[k] + over)
                    values.append(jnp.where(keep, source[pl.ds(at, TILE), :], 0.0))
                place(c, row, values)

    def diagonal_rows(row):
        sides = {}

        def make(c):
            sums = load(static, CONDUCT, c, row - 1) + load(static, CONDUCT, c, row + 1)
            sides[c] = sums
            return load(static, CONDUCT, c, row) + corner_weight * sums

        ring = Ring(make, shape.chunks, lane)
        for c in range(shape.chunks):
            around = ring.before(c, 1) + ring.after(c, 1) + sides[c]
            depth = load(thick, 0, c, row)
            diagonal = (
                0.5 * (around + 5.0 * load(static, CONDUCT, c, row))
                + storage * depth
                + load(static, HALF_RATE, c, row)
            )
            store(static, DIAGONAL, c, row, diagonal)
            store(static, INVERSE, c, row, jnp.where(depth > 0.0, 1.0 / diagonal, 0.0))
            ring.done(c)

    start = GUARD
    sweep(start + 5, 7, diagonal_rows)
    project(
        shape, vel, potential, static, moved, krylov, moments,
        (start + 5, start + 6, start + 7, start + 8), (7, 7, 7, 6),
    )


def coefficients(shares):
    total = jnp.sum(shares[...], axis=0)
    mu = [jnp.broadcast_to(total[:, k : k + 1], (TILE, LANES)) for k in range(2 * ITERS)]

    def norm(c):
        return sum(c[i] * c[j] * mu[i + j] for i in range(len(c)) for j in range(len(c)))

    def energy(c):
        return sum(
            c[i] * c[j] * (mu[i + j] - mu[i + j + 1]) for i in range(len(c)) for j in range(len(c))
        )

    floor = 2e-7 * mu[0]
    one = jnp.ones((TILE, LANES), jnp.float32)
    z = [one]
    search = [one]
    result = [jnp.zeros((TILE, LANES), jnp.float32)] * ITERS
    norm_now = mu[0]
    for iteration in range(ITERS):
        step = norm_now / energy(search)
        if iteration:
            step = jnp.where(norm_now > floor, step, 0.0)
        for i, c in enumerate(search):
            result[i] = result[i] + step * c
        if iteration + 1 < ITERS:
            applied = [
                (search[i] if i < len(search) else 0.0) - (search[i - 1] if i else 0.0)
                for i in range(len(search) + 1)
            ]
            z = [(z[i] if i < len(z) else 0.0) - step * applied[i] for i in range(len(applied))]
            norm_next = norm(z)
            ratio = norm_next / norm_now
            if iteration:
                ratio = jnp.where(norm_now > floor, ratio, 0.0)
            search = [z[i] + (ratio * search[i] if i < len(search) else 0.0) for i in range(len(z))]
            norm_now = norm_next
    return result


def pressure_rows(shape, factors, krylov, pressure, row):
    for c in range(shape.chunks):
        for layer in range(2):
            value = factors[0] * load(krylov, layer, c, row)
            value = value + factors[1] * load(krylov, 2 + layer, c, row)
            value = value + factors[2] * load(krylov, 4 + layer, c, row)
            store(pressure, layer, c, row, value)


def along_moved(moved, pressure, layer, c, row):
    return load(moved, layer, c, row) - (0.5 * time_step) * (
        load(pressure, layer, c, row + 1) - load(pressure, layer, c, row - 1)
    )


def move_rows(shape, moved, pressure, static, flux, put, row):
    lane = lanes_of()
    rings = [
        Ring(lambda c, k=k: load(pressure, k, c, row), shape.chunks, lane) for k in range(2)
    ]
    for c in range(shape.chunks):
        conduct = load(static, CONDUCT, c, row)
        wet = conduct > 0.0
        along = [along_moved(moved, pressure, layer, c, row) for layer in range(2)]
        cross = [
            load(moved, 2 + layer, c, row)
            - (0.5 * time_step) * (rings[layer].after(c, 1) - rings[layer].before(c, 1))
            for layer in range(2)
        ]
        for part, value in enumerate(along + cross):
            put(part, c, row, jnp.where(wet, value, 0.0))
        store(flux, 0, c, row, conduct * (along[0] + along[1]))
        store(flux, 1, c, row, conduct * (cross[0] + cross[1]))
        for ring in rings:
            ring.done(c)


def surface_rows(shape, surface, flux, chunks, put, row):
    ring = Ring(lambda c: load(flux, 1, c, row), shape.chunks, lanes_of())
    for c in range(chunks):
        value = load(surface, 0, c, row) - (0.5 * time_step) * (
            load(flux, 0, c, row + 1)
            - load(flux, 0, c, row - 1)
            + (ring.after(c, 1) - ring.before(c, 1))
        )
        put(c, row, value)
        ring.done(c)


def second_kernel(
    shape, shares, moved_in, static, surface_in, krylov_in,
    moved, surface, krylov, moments,
    vel, potential, pressure, flux,
):
    factors = coefficients(shares)
    start = GUARD
    sweep(start + 8, 6, functools.partial(pressure_rows, shape, factors, krylov_in, pressure))
    sweep(
        start + 9,
        6,
        functools.partial(
            move_rows, shape, moved_in, pressure, static, flux, functools.partial(store, vel)
        ),
    )

    def put(c, row, value):
        value = jnp.where(load(static, INVERSE, c, row) > 0.0, value, 0.0)
        store(surface, 0, c, row, value)
        store(potential, 0, c, row, gravity * value + load(static, HEAD, c, row))

    sweep(
        start + 10,
        6,
        functools.partial(surface_rows, shape, surface_in, flux, shape.chunks, put),
    )
    project(
        shape, vel, potential, static, moved, krylov, moments,
        (start + 11, start + 12, start + 13, start + 14), (6, 5, 5, 5),
    )


def last_kernel(
    shape, shares, moved, static, surface, krylov,
    new_vel, new_surface, new_pressure,
    pressure, flux,
):
    factors = coefficients(shares)
    start = shape.first
    sweep(start - 2, 5, functools.partial(pressure_rows, shape, factors, krylov, pressure))

    def put_vel(part, c, row, value):
        if c < shape.own:
            at = pl.multiple_of(row - start, TILE)
            new_vel[part, pl.ds(at, TILE), pl.ds(c * LANES, LANES)] = value
            if part < 2:
                new_pressure[part, pl.ds(at, TILE), pl.ds(c * LANES, LANES)] = load(
                    pressure, part, c, row
                )

    sweep(
        start,
        shape.rows // TILE,
        functools.partial(move_rows, shape, moved, pressure, static, flux, put_vel),
    )
    for row in (start - 1, start + shape.rows):
        for c in range(shape.own):
            one = slice(row, row + 1)
            total = jnp.zeros((1, LANES), jnp.float32)
            for layer in range(2):
                total = total + (
                    moved[layer, c, one, :]
                    - (0.5 * time_step)
                    * (
                        pressure[layer, c, row + 1 : row + 2, :]
                        - pressure[layer, c, row - 1 : row, :]
                    )
                )
            flux[0, c, one, :] = static[CONDUCT, c, one, :] * total

    def put(c, row, value):
        at = pl.multiple_of(row - start, TILE)
        new_surface[pl.ds(at, TILE), pl.ds(c * LANES, LANES)] = value

    sweep(
        start,
        shape.rows // TILE,
        functools.partial(surface_rows, shape, surface, flux, shape.own, put),
    )


def cost(flops):
    return pl.CostEstimate(flops=flops, bytes_accessed=flops, transcendentals=0)


def call(kernel, shape, kinds, outs, scratch, operands, estimate=None, aliases={}):
    return pl.pallas_call(
        functools.partial(kernel, shape),
        out_shape=outs,
        in_specs=[pl.BlockSpec(memory_space=kind) for kind in kinds],
        out_specs=[pl.BlockSpec(memory_space=pltpu.VMEM)] * len(outs),
        scratch_shapes=scratch,
        cost_estimate=estimate,
        input_output_aliases=aliases,
        compiler_params=pltpu.CompilerParams(vmem_limit_bytes=VMEM_BYTES),
    )(*operands)


def held(*arrays):
    return tuple(pltpu.with_memory_space_constraint(x, pltpu.VMEM) for x in arrays)


def shared(moments):
    return lax.all_to_all(moments, ("along", "cross"), 0, 0, tiled=True)


def shards(velocity, surface, wet_mask, bathy_class, depth_table, hull_ranges, hull_pressure):
    shape = Shape(*surface.shape)
    vmem, smem = pltpu.VMEM, pltpu.SMEM
    f32, i32 = jnp.float32, jnp.int32
    size = lax.axis_size("along")
    field = (shape.chunks, shape.total, LANES)
    fields = lambda count: vmem((count,) + field, f32)
    sums = jax.ShapeDtypeStruct((2 * size, 1, 8), f32)
    block = surface.shape
    wide = vmem((shape.own * SENT_ROWS + CORNER_ROWS, LANES), f32)
    full = vmem((FIELDS, shape.rows, LANES), f32)
    corner = vmem((SENT_ROWS, LANES), f32)
    tiles = FIELDS * shape.rows // TILE
    table = [smem(depth_table.shape, f32)]
    arrived = [pltpu.SemaphoreType.DMA((5,))]
    near = (shape.rows, LANES)
    inputs = tuple(
        pltpu.with_memory_space_constraint(x, pltpu.HBM)
        for x in (velocity, surface, wet_mask, bathy_class, depth_table)
    )
    (side,) = call(
        edge_kernel, shape, [pl.ANY] * 5,
        [vmem((-(-tiles // SLOTS) * TILE, LANES), f32)],
        [vmem((4,) + near, f32), vmem(near, f32), vmem(near, i32), vmem(near, i32)]
        + table + [full] + arrived,
        inputs,
        cost(10**5),
    )
    far = lax.ppermute(side, "cross", [(0, 1), (1, 0)])
    own, out_chip, in_chip = call(
        pack_kernel, shape, [pl.ANY] * 5,
        [vmem((FIELDS, shape.own, shape.rows, LANES), f32), wide, wide],
        [vmem(velocity.shape, f32), vmem(block, f32), vmem(block, i32), vmem(block, i32)]
        + table + arrived,
        inputs,
        cost(4 * 10**6),
    )
    out_chip, in_chip, side = call(
        corner_kernel, shape, [vmem] * 3, [wide, wide, full], [], held(far, out_chip, in_chip),
        cost(10**5), {1: 0, 2: 1},
    )
    firsts = [i for i in range(1, size, 2)]
    trades = lambda pairs: pairs + [(j, i) for i, j in pairs]
    from_out = lax.ppermute(out_chip, "along", trades([(i, (i + 1) % size) for i in firsts]))
    from_in = lax.ppermute(in_chip, "along", trades([(i - 1, i) for i in firsts]))
    (head,) = call(
        head_kernel, shape, [smem] * 2 + [vmem], [fields(1)],
        [vmem((SHIPS, shape.chunks, TILE, LANES), f32)],
        (hull_ranges.T, hull_pressure) + held(side),
        cost(2 * 10**6),
    )
    moved, static, level, krylov, moments = call(
        first_kernel, shape, [vmem] * 5,
        [fields(4), fields(5), fields(1), fields(6), sums],
        [fields(4), fields(1), fields(1), corner, corner],
        held(own, side, from_out, from_in, head),
    )
    moved, level, krylov, moments = call(
        second_kernel, shape, [vmem] * 5,
        [fields(4), fields(1), fields(6), sums],
        [fields(4), fields(1), fields(2), fields(2)],
        (shared(moments),) + held(moved, static, level, krylov),
    )
    whole = lambda like: jax.ShapeDtypeStruct(like, f32)
    return tuple(
        call(
            last_kernel, shape, [vmem] * 5,
            [whole(velocity.shape), whole(surface.shape), whole((2,) + surface.shape)],
            [fields(2), fields(2)],
            (shared(moments),) + held(moved, static, level, krylov),
        )
    )


def solution(mesh):
    cell = P("along", "cross")
    layered = P(None, "along", "cross")
    in_specs = (layered, cell, cell, cell, P(), P(), P())
    return jax.shard_map(
        shards, mesh=mesh, in_specs=in_specs, out_specs=(layered, cell, layered), check_vma=False
    )
```

```python
import functools

import jax
import jax.numpy as jnp
from jax import lax
from jax.experimental import pallas as pl
from jax.experimental.pallas import tpu as pltpu
from jax.sharding import PartitionSpec as P

ITERS = 3
CLASSES = 16
SHIPS = 8

gravity = 9.81
time_step = 0.1
storage = 0.1
corner_weight = 0.25

LANES = 128
TILE = 8
GUARD = 8
HALO = 16
FIELDS = 7
SENT = (13, 13, 13, 13, 12, 11, 11)
OFFSETS = (0, 13, 26, 39, 52, 64, 75)
SENT_ROWS = 88
CORNER_ROWS = 16
EDGE = 16
SLOTS = LANES // EDGE
VMEM_BYTES = 24 * 1024 * 1024


class Shape:
    def __init__(self, rows, cols):
        self.rows = rows
        self.own = cols // LANES
        self.chunks = self.own + 1
        self.first = GUARD + HALO
        self.total = rows + 2 * (GUARD + HALO)


class Ring:
    def __init__(self, make, chunks, lane):
        self.make = make
        self.chunks = chunks
        self.lane = lane
        self.held = {}

    def at(self, chunk):
        entry = self.held.setdefault(chunk, {})
        if 0 not in entry:
            entry[0] = self.make(chunk)
        return entry[0]

    def rolled(self, chunk, amount):
        value = self.at(chunk)
        entry = self.held[chunk]
        if amount not in entry:
            entry[amount] = pltpu.roll(value, amount, 1)
        return entry[amount]

    def before(self, chunk, step):
        other = (chunk - 1) % self.chunks
        return jnp.where(self.lane < step, self.rolled(other, step), self.rolled(chunk, step))

    def after(self, chunk, step):
        other = (chunk + 1) % self.chunks
        amount = LANES - step
        return jnp.where(self.lane >= amount, self.rolled(other, amount), self.rolled(chunk, amount))

    def done(self, chunk):
        self.held.pop((chunk - 1) % self.chunks, None)


def lanes_of():
    return lax.broadcasted_iota(jnp.int32, (TILE, LANES), 1)


def sweep(span, body, carry=None):
    first, tiles, split, gap = span if len(span) == 4 else span + (span[1], 0)

    def turn(number, carry):
        row = first + number * TILE
        if split < tiles:
            row = row + jnp.where(number >= split, gap, 0)
        if carry is None:
            body(row)
            return None
        return body(row, carry)

    return lax.fori_loop(0, tiles, turn, carry)


def load(ref, index, chunk, row):
    return ref[index, chunk, pl.ds(row, TILE), :]


def store(ref, index, chunk, row, value):
    ref[index, chunk, pl.ds(row, TILE), :] = value


CONDUCT, HALF_RATE, INVERSE, HEAD, DIAGONAL = range(5)


def predict_rows(shape, vel, head_pressure, static, moved, row):
    lane = lanes_of()
    rings = [
        Ring(lambda c, k=k: load(vel, k, c, row), shape.chunks, lane) for k in range(4)
    ]
    potential = Ring(lambda c: load(head_pressure, 0, c, row), shape.chunks, lane)
    for c in range(shape.chunks):
        wet = load(static, CONDUCT, c, row) > 0.0
        rate = time_step * load(static, HALF_RATE, c, row)
        slope_a = (0.5 * time_step) * (
            load(head_pressure, 0, c, row + 1) - load(head_pressure, 0, c, row - 1)
        )
        slope_c = (0.5 * time_step) * (potential.after(c, 1) - potential.before(c, 1))
        for layer in range(2):
            along = rings[layer].at(c)
            cross = rings[2 + layer].at(c)
            up_a = (0.5 * time_step) * jnp.maximum(along, 0.0)
            dn_a = (0.5 * time_step) * jnp.minimum(along, 0.0)
            up_c = (0.5 * time_step) * jnp.maximum(cross, 0.0)
            dn_c = (0.5 * time_step) * jnp.minimum(cross, 0.0)
            centre = (
                0.8 - 3.0 * ((up_a - dn_a) + (up_c - dn_c)) - (rate if layer == 0 else 2.0 * rate)
            )
            back_a = 0.05 + 4.0 * up_a
            fore_a = 0.05 - 4.0 * dn_a
            back_c = 0.05 + 4.0 * up_c
            fore_c = 0.05 - 4.0 * dn_c
            for part, slope in ((layer, slope_a), (2 + layer, slope_c)):
                ring = rings[part]
                other = rings[part + 1 - 2 * layer].at(c)
                value = centre * ring.at(c) + rate * other - slope
                value = value + (
                    back_a * load(vel, part, c, row - 1) - up_a * load(vel, part, c, row - 2)
                )
                value = value + (
                    fore_a * load(vel, part, c, row + 1) + dn_a * load(vel, part, c, row + 2)
                )
                value = value + (back_c * ring.before(c, 1) - up_c * ring.before(c, 2))
                value = value + (fore_c * ring.after(c, 1) + dn_c * ring.after(c, 2))
                store(moved, part, c, row, jnp.where(wet, value, 0.0))
        for ring in rings:
            ring.done(c)
        potential.done(c)


def source_rows(shape, moved, static, krylov, row):
    lane = lanes_of()
    rings = [
        Ring(
            lambda c, k=k: load(static, CONDUCT, c, row) * load(moved, 2 + k, c, row),
            shape.chunks,
            lane,
        )
        for k in range(2)
    ]
    for c in range(shape.chunks):
        above = load(static, CONDUCT, c, row - 1)
        below = load(static, CONDUCT, c, row + 1)
        scale = (-0.5 / time_step) * load(static, INVERSE, c, row)
        for layer in range(2):
            flow = (
                below * load(moved, layer, c, row + 1)
                - above * load(moved, layer, c, row - 1)
                + (rings[layer].after(c, 1) - rings[layer].before(c, 1))
            )
            store(krylov, layer, c, row, scale * flow)
            rings[layer].done(c)


def link_rows(shape, krylov, static, level, row, own_only):
    lane = lanes_of()

    def plain(layer, c):
        values = [load(krylov, 2 * level + layer, c, row + d) for d in (-1, 0, 1)]
        return values[1], values[0] + values[2]

    def weighted(layer, c):
        values = [
            load(static, CONDUCT, c, row + d) * load(krylov, 2 * level + layer, c, row + d)
            for d in (-1, 0, 1)
        ]
        return values[1], values[0] + values[2]

    sides = {}

    def ring_of(kind, layer):
        def make(c):
            middle, sums = kind(layer, c)
            sides[kind, layer, c] = sums
            return middle + corner_weight * sums

        return Ring(make, shape.chunks, lane)

    rings = [(ring_of(plain, layer), ring_of(weighted, layer)) for layer in range(2)]
    for c in range(shape.own if own_only else shape.chunks):
        conduct = load(static, CONDUCT, c, row)
        rate = load(static, HALF_RATE, c, row)
        centre = [load(krylov, 2 * level + layer, c, row) for layer in range(2)]
        results = []
        for layer in range(2):
            ring, scaled = rings[layer]
            around = (ring.before(c, 1) + ring.after(c, 1)) + sides[plain, layer, c]
            flows = (scaled.before(c, 1) + scaled.after(c, 1)) + sides[weighted, layer, c]
            results.append(0.5 * (conduct * around + flows) + rate * centre[1 - layer])
            ring.done(c)
            scaled.done(c)
        yield c, centre, results


def krylov_rows(shape, krylov, static, level, row):
    for c, _, results in link_rows(shape, krylov, static, level, row, False):
        inverse = load(static, INVERSE, c, row)
        for layer in range(2):
            store(krylov, 2 * level + 2 + layer, c, row, inverse * results[layer])


def moments_of(shape, krylov, static, span, sums):
    def turn(row, sums):
        sums = list(sums)
        for c, top, results in link_rows(shape, krylov, static, 2, row, True):
            diagonal = load(static, DIAGONAL, c, row)
            for layer in range(2):
                low = load(krylov, layer, c, row)
                mid = load(krylov, 2 + layer, c, row)
                low_d, mid_d, top_d = diagonal * low, diagonal * mid, diagonal * top[layer]
                terms = (
                    low * low_d,
                    low * mid_d,
                    mid * mid_d,
                    mid * top_d,
                    top[layer] * top_d,
                    top[layer] * results[layer],
                )
                sums = [a + b for a, b in zip(sums, terms)]
        return tuple(sums)

    return sweep(span, turn, tuple(sums))


def no_moments():
    return (jnp.zeros((TILE, LANES), jnp.float32),) * (2 * ITERS)


def put_moments(out, sums):
    lane = lanes_of()
    result = jnp.zeros((TILE, LANES), jnp.float32)
    for number, part in enumerate(sums):
        result = jnp.where(lane == number, jnp.sum(part), result)
    out[...] = jnp.broadcast_to(result[0:1, None, 0 : out.shape[2]], out.shape)


def project(shape, vel, potential, static, moved, krylov, spans, sums):
    sweep(spans[0], functools.partial(predict_rows, shape, vel, potential, static, moved))
    sweep(spans[1], functools.partial(source_rows, shape, moved, static, krylov))
    for level in range(2):
        sweep(spans[2 + level], functools.partial(krylov_rows, shape, krylov, static, level))
    return moments_of(shape, krylov, static, spans[4], sums)


def fetch(pairs, arrived):
    copies = [
        pltpu.make_async_copy(source, target, arrived.at[number])
        for number, (source, target) in enumerate(pairs)
    ]
    for copy in copies:
        copy.start()
    for copy in copies:
        copy.wait()


def cell_values(vel, surface, wet, bathy, table, rows, cols):
    flag = wet[rows, cols]
    entry = bathy[rows, cols]
    thick = jnp.zeros((TILE, LANES), jnp.float32)
    for choice in range(CLASSES):
        thick = jnp.where(entry == choice, 0.5 * table[choice], thick)
    values = [jnp.where(flag > 0, vel[k, rows, cols], 0.0) for k in range(4)]
    return values + [surface[rows, cols], flag.astype(jnp.float32), thick]


def edge_kernel(
    shape, vel_in, surface_in, wet_in, bathy_in, table_in, side,
    vel, surface, wet, bathy, table, edge, arrived,
):
    half = lax.axis_index("cross")
    first = jnp.where(half == 0, (shape.own - 1) * LANES, 0)
    near = pl.ds(pl.multiple_of(first, LANES), LANES)
    fetch(
        (
            (table_in, table),
            (bathy_in.at[:, near], bathy),
            (wet_in.at[:, near], wet),
            (surface_in.at[:, near], surface),
            (vel_in.at[:, :, near], vel),
        ),
        arrived,
    )
    for t in range(shape.rows // TILE):
        rows = pl.ds(t * TILE, TILE)
        values = cell_values(vel, surface, wet, bathy, table, rows, pl.ds(0, LANES))
        for k, value in enumerate(values):
            edge[k, rows, :] = value
    squeeze(side, 0, side_tiles(shape, edge), jnp.where(half == 0, EDGE, 0))


def pack_kernel(
    shape, vel_in, surface_in, wet_in, bathy_in, table_in,
    own, out_chip, in_chip,
    vel, surface, wet, bathy, table, arrived,
):
    fetch(
        (
            (table_in, table),
            (bathy_in, bathy),
            (wet_in, wet),
            (surface_in, surface),
            (vel_in, vel),
        ),
        arrived,
    )

    def turn(number, carry):
        rows = pl.ds(pl.multiple_of(number * TILE, TILE), TILE)
        for c in range(shape.own):
            cols = pl.ds(c * LANES, LANES)
            values = cell_values(vel, surface, wet, bathy, table, rows, cols)
            for k, value in enumerate(values):
                own[k, c, rows, :] = value
        return carry

    lax.fori_loop(0, shape.rows // TILE, turn, 0)
    core = lax.rem(lax.axis_index("along"), 2)
    for c in range(shape.own):
        for k in range(FIELDS):
            for part in (0, SENT[k] - TILE):
                to = pl.ds(c * SENT_ROWS + OFFSETS[k] + part, TILE)
                last = shape.rows - SENT[k]
                out_chip[to, :] = own[k, c, pl.ds(part + core * last, TILE), :]
                in_chip[to, :] = own[k, c, pl.ds(part + (1 - core) * last, TILE), :]


def corner_kernel(shape, far, out_in, in_in, out_chip, in_chip, side):
    half = lax.axis_index("cross")
    core = lax.rem(lax.axis_index("along"), 2)
    for number, tile in enumerate(side_tiles(shape, side)):
        tile[...] = spread(far, 0, number, half)
    shift = jnp.where(half == 0, 0, EDGE)
    squeeze(out_chip, shape.own * SENT_ROWS, corner_tiles(shape, side, core), shift)
    squeeze(in_chip, shape.own * SENT_ROWS, corner_tiles(shape, side, 1 - core), shift)


def side_tiles(shape, edge):
    return [
        edge.at[k, pl.ds(row, TILE), :] for k in range(FIELDS) for row in range(0, shape.rows, TILE)
    ]


def corner_parts():
    return [(k, part) for k in range(FIELDS) for part in (0, SENT[k] - TILE)]


def corner_tiles(shape, edge, last):
    return [
        edge.at[k, pl.ds(part + last * (shape.rows - SENT[k]), TILE), :]
        for k, part in corner_parts()
    ]


def squeeze(out, base, tiles, shift):
    slot = lanes_of() // EDGE
    for first in range(0, len(tiles), SLOTS):
        value = jnp.zeros((TILE, LANES), jnp.float32)
        for number, tile in enumerate(tiles[first : first + SLOTS]):
            moved = pltpu.roll(tile[...], lax.rem(EDGE * number + shift, LANES), 1)
            value = jnp.where(slot == number, moved, value)
        out[pl.ds(base + first, TILE), :] = value


def spread(source, base, number, half):
    lane = lanes_of()
    tile = source[pl.ds(base + number // SLOTS * TILE, TILE), :]
    amount = LANES - EDGE * (number % SLOTS) - jnp.where(half == 0, 0, EDGE)
    moved = pltpu.roll(tile, lax.rem(amount + LANES, LANES), 1)
    wanted = jnp.where(half == 0, lane, LANES - 1 - lane) < EDGE
    return jnp.where(wanted, moved, 0.0)


def head_kernel(shape, ranges, heads, side, head, columns):
    along = lax.axis_index("along")
    half = lax.axis_index("cross")
    lane = lanes_of()
    line = lax.broadcasted_iota(jnp.int32, (TILE, LANES), 0)
    for c in range(shape.chunks):
        if c < shape.own:
            index = half * (shape.own * LANES) + c * LANES + lane
        else:
            index = jnp.where(half == 0, shape.own * LANES, (shape.own - 1) * LANES) + lane
        for s in range(SHIPS):
            inside = jnp.logical_and(index >= ranges[2, s], index < ranges[3, s])
            columns[s, c] = jnp.where(inside, gravity * heads[s], 0.0)

    def head_rows(row):
        global_row = along * shape.rows + (row - shape.first) + line
        covered = [
            jnp.logical_and(global_row >= ranges[0, s], global_row < ranges[1, s])
            for s in range(SHIPS)
        ]
        for c in range(shape.chunks):
            value = jnp.zeros((TILE, LANES), jnp.float32)
            for s in range(SHIPS):
                value = value + jnp.where(covered[s], columns[s, c], 0.0)
            store(head, 0, c, row, value)

    sweep((GUARD, shape.total // TILE - 2), head_rows)


def place(refs, head, c, row, values):
    moved, static, surface, krylov, vel, potential, thick = refs
    for k in range(4):
        store(vel, k, c, row, values[k])
    depth = values[6]
    inside = depth > 0.0
    ship = jnp.where(inside, load(head, 0, c, row), 0.0)
    store(surface, 0, c, row, values[4])
    store(potential, 0, c, row, gravity * values[4] + ship)
    store(thick, 0, c, row, depth)
    store(static, CONDUCT, c, row, values[5] * depth)
    store(static, HALF_RATE, c, row, 0.5 / jnp.where(inside, depth, 1.0))
    store(static, HEAD, c, row, ship)


def diagonal_rows(shape, static, thick, row):
    sides = {}

    def make(c):
        sums = load(static, CONDUCT, c, row - 1) + load(static, CONDUCT, c, row + 1)
        sides[c] = sums
        return load(static, CONDUCT, c, row) + corner_weight * sums

    ring = Ring(make, shape.chunks, lanes_of())
    for c in range(shape.chunks):
        around = ring.before(c, 1) + ring.after(c, 1) + sides[c]
        depth = load(thick, 0, c, row)
        diagonal = (
            0.5 * (around + 5.0 * load(static, CONDUCT, c, row))
            + storage * depth
            + load(static, HALF_RATE, c, row)
        )
        store(static, DIAGONAL, c, row, diagonal)
        store(static, INVERSE, c, row, jnp.where(depth > 0.0, 1.0 / diagonal, 0.0))
        ring.done(c)


def inner_kernel(shape, own, side, head, *refs):
    refs, partial = refs[:7], refs[7]
    moved, static, surface, krylov, vel, potential, thick = refs

    def own_rows(row):
        at = row - shape.first
        for c in range(shape.chunks):
            if c < shape.own:
                values = [load(own, k, c, at) for k in range(FIELDS)]
            else:
                values = [side[k, pl.ds(at, TILE), :] for k in range(FIELDS)]
            place(refs, head, c, row, values)

    sweep((shape.first, shape.rows // TILE), own_rows)
    middle = (shape.first + 4, shape.rows // TILE - 1)
    sweep(middle, functools.partial(diagonal_rows, shape, static, thick))
    spans = (middle,) * 4 + ((shape.first + 8, shape.rows // TILE - 2),)
    sums = project(shape, vel, potential, static, moved, krylov, spans, no_moments())
    for number, value in enumerate(sums):
        partial[number] = value


def outer_kernel(shape, out_chip, in_chip, head, partial, *refs):
    refs = refs[7:]
    moments, out_corner, in_corner = refs[7:]
    refs = refs[:7]
    moved, static, surface, krylov, vel, potential, thick = refs
    along = lax.axis_index("along")
    half = lax.axis_index("cross")
    for number, (k, part) in enumerate(corner_parts()):
        to = pl.ds(OFFSETS[k] + part, TILE)
        out_corner[to, :] = spread(out_chip, shape.own * SENT_ROWS, number, half)
        in_corner[to, :] = spread(in_chip, shape.own * SENT_ROWS, number, half)
    core = lax.rem(along, 2)
    deepest = SENT[0]
    last = lax.axis_size("along") - 1
    for wide, narrow, below in ((out_chip, out_corner, core), (in_chip, in_corner, 1 - core)):
        keep = jnp.where(below == 1, last - along, along) > 0
        for over, under in ((-deepest, 0), (-TILE, deepest - TILE)):
            row = shape.first + jnp.where(below == 1, shape.rows + under, over)
            for c in range(shape.chunks):
                source, skip = (wide, c * SENT_ROWS) if c < shape.own else (narrow, 0)
                values = []
                for k in range(FIELDS):
                    at = skip + OFFSETS[k] + jnp.where(below == 1, under, SENT[k] + over)
                    values.append(jnp.where(keep, source[pl.ds(at, TILE), :], 0.0))
                place(refs, head, c, row, values)

    def both(halo):
        return (shape.first - halo, 4, 2, shape.rows + 2 * halo - 4 * TILE)

    sweep(both(11), functools.partial(diagonal_rows, shape, static, thick))
    spans = tuple(both(halo) for halo in (11, 10, 9, 8))
    spans += ((shape.first, 2, 1, shape.rows - 2 * TILE),)
    sums = [partial[number] for number in range(2 * ITERS)]
    put_moments(moments, project(shape, vel, potential, static, moved, krylov, spans, sums))


def coefficients(shares):
    total = jnp.sum(shares[...], axis=0)
    mu = [jnp.broadcast_to(total[:, k : k + 1], (TILE, LANES)) for k in range(2 * ITERS)]

    def norm(c):
        return sum(c[i] * c[j] * mu[i + j] for i in range(len(c)) for j in range(len(c)))

    def energy(c):
        return sum(
            c[i] * c[j] * (mu[i + j] - mu[i + j + 1]) for i in range(len(c)) for j in range(len(c))
        )

    floor = 2e-7 * mu[0]
    one = jnp.ones((TILE, LANES), jnp.float32)
    z = [one]
    search = [one]
    result = [jnp.zeros((TILE, LANES), jnp.float32)] * ITERS
    norm_now = mu[0]
    for iteration in range(ITERS):
        step = norm_now / energy(search)
        if iteration:
            step = jnp.where(norm_now > floor, step, 0.0)
        for i, c in enumerate(search):
            result[i] = result[i] + step * c
        if iteration + 1 < ITERS:
            applied = [
                (search[i] if i < len(search) else 0.0) - (search[i - 1] if i else 0.0)
                for i in range(len(search) + 1)
            ]
            z = [(z[i] if i < len(z) else 0.0) - step * applied[i] for i in range(len(applied))]
            norm_next = norm(z)
            ratio = norm_next / norm_now
            if iteration:
                ratio = jnp.where(norm_now > floor, ratio, 0.0)
            search = [z[i] + (ratio * search[i] if i < len(search) else 0.0) for i in range(len(z))]
            norm_now = norm_next
    return result


def pressure_rows(shape, factors, krylov, pressure, row):
    for c in range(shape.chunks):
        for layer in range(2):
            value = factors[0] * load(krylov, layer, c, row)
            value = value + factors[1] * load(krylov, 2 + layer, c, row)
            value = value + factors[2] * load(krylov, 4 + layer, c, row)
            store(pressure, layer, c, row, value)


def along_moved(moved, pressure, layer, c, row):
    return load(moved, layer, c, row) - (0.5 * time_step) * (
        load(pressure, layer, c, row + 1) - load(pressure, layer, c, row - 1)
    )


def move_rows(shape, moved, pressure, static, flux, put, row):
    lane = lanes_of()
    rings = [
        Ring(lambda c, k=k: load(pressure, k, c, row), shape.chunks, lane) for k in range(2)
    ]
    for c in range(shape.chunks):
        conduct = load(static, CONDUCT, c, row)
        wet = conduct > 0.0
        along = [along_moved(moved, pressure, layer, c, row) for layer in range(2)]
        cross = [
            load(moved, 2 + layer, c, row)
            - (0.5 * time_step) * (rings[layer].after(c, 1) - rings[layer].before(c, 1))
            for layer in range(2)
        ]
        for part, value in enumerate(along + cross):
            put(part, c, row, jnp.where(wet, value, 0.0))
        store(flux, 0, c, row, conduct * (along[0] + along[1]))
        store(flux, 1, c, row, conduct * (cross[0] + cross[1]))
        for ring in rings:
            ring.done(c)


def surface_rows(shape, surface, flux, chunks, put, row):
    ring = Ring(lambda c: load(flux, 1, c, row), shape.chunks, lanes_of())
    for c in range(chunks):
        value = load(surface, 0, c, row) - (0.5 * time_step) * (
            load(flux, 0, c, row + 1)
            - load(flux, 0, c, row - 1)
            + (ring.after(c, 1) - ring.before(c, 1))
        )
        put(c, row, value)
        ring.done(c)


def second_kernel(
    shape, shares, moved_in, static, surface_in, krylov_in,
    moved, surface, krylov, moments,
    vel, potential, pressure, flux,
):
    factors = coefficients(shares)
    start = GUARD
    sweep((start + 8, 6), functools.partial(pressure_rows, shape, factors, krylov_in, pressure))
    put_vel = functools.partial(store, vel)
    sweep(
        (start + 9, 6),
        functools.partial(move_rows, shape, moved_in, pressure, static, flux, put_vel),
    )

    def put(c, row, value):
        value = jnp.where(load(static, INVERSE, c, row) > 0.0, value, 0.0)
        store(surface, 0, c, row, value)
        store(potential, 0, c, row, gravity * value + load(static, HEAD, c, row))

    sweep(
        (start + 10, 6),
        functools.partial(surface_rows, shape, surface_in, flux, shape.chunks, put),
    )
    spans = ((start + 11, 6), (start + 12, 5), (start + 13, 5), (start + 14, 5))
    spans += ((shape.first, shape.rows // TILE),)
    put_moments(
        moments, project(shape, vel, potential, static, moved, krylov, spans, no_moments())
    )


def last_kernel(
    shape, shares, moved, static, surface, krylov,
    new_vel, new_surface, new_pressure,
    pressure, flux,
):
    factors = coefficients(shares)
    start = shape.first
    sweep((start - 2, 5), functools.partial(pressure_rows, shape, factors, krylov, pressure))

    def put_vel(part, c, row, value):
        if c < shape.own:
            at = pl.multiple_of(row - start, TILE)
            new_vel[part, pl.ds(at, TILE), pl.ds(c * LANES, LANES)] = value
            if part < 2:
                new_pressure[part, pl.ds(at, TILE), pl.ds(c * LANES, LANES)] = load(
                    pressure, part, c, row
                )

    sweep(
        (start, shape.rows // TILE),
        functools.partial(move_rows, shape, moved, pressure, static, flux, put_vel),
    )
    for row in (start - 1, start + shape.rows):
        for c in range(shape.own):
            one = slice(row, row + 1)
            total = jnp.zeros((1, LANES), jnp.float32)
            for layer in range(2):
                total = total + (
                    moved[layer, c, one, :]
                    - (0.5 * time_step)
                    * (
                        pressure[layer, c, row + 1 : row + 2, :]
                        - pressure[layer, c, row - 1 : row, :]
                    )
                )
            flux[0, c, one, :] = static[CONDUCT, c, one, :] * total

    def put(c, row, value):
        at = pl.multiple_of(row - start, TILE)
        new_surface[pl.ds(at, TILE), pl.ds(c * LANES, LANES)] = value

    sweep(
        (start, shape.rows // TILE),
        functools.partial(surface_rows, shape, surface, flux, shape.own, put),
    )


def cost(flops):
    return pl.CostEstimate(flops=flops, bytes_accessed=flops, transcendentals=0)


def call(kernel, shape, kinds, outs, scratch, operands, estimate=None, aliases={}):
    return pl.pallas_call(
        functools.partial(kernel, shape),
        out_shape=outs,
        in_specs=[pl.BlockSpec(memory_space=kind) for kind in kinds],
        out_specs=[pl.BlockSpec(memory_space=pltpu.VMEM)] * len(outs),
        scratch_shapes=scratch,
        cost_estimate=estimate,
        input_output_aliases=aliases,
        compiler_params=pltpu.CompilerParams(vmem_limit_bytes=VMEM_BYTES),
    )(*operands)


def held(*arrays):
    return tuple(pltpu.with_memory_space_constraint(x, pltpu.VMEM) for x in arrays)


def shared(moments):
    return lax.all_to_all(moments, ("along", "cross"), 0, 0, tiled=True)


def shards(velocity, surface, wet_mask, bathy_class, depth_table, hull_ranges, hull_pressure):
    shape = Shape(*surface.shape)
    vmem, smem = pltpu.VMEM, pltpu.SMEM
    f32, i32 = jnp.float32, jnp.int32
    size = lax.axis_size("along")
    field = (shape.chunks, shape.total, LANES)
    fields = lambda count: vmem((count,) + field, f32)
    sums = jax.ShapeDtypeStruct((2 * size, 1, 8), f32)
    block = surface.shape
    wide = vmem((shape.own * SENT_ROWS + CORNER_ROWS, LANES), f32)
    full = vmem((FIELDS, shape.rows, LANES), f32)
    corner = vmem((SENT_ROWS, LANES), f32)
    tiles = FIELDS * shape.rows // TILE
    table = [smem(depth_table.shape, f32)]
    arrived = [pltpu.SemaphoreType.DMA((5,))]
    near = (shape.rows, LANES)
    inputs = tuple(
        pltpu.with_memory_space_constraint(x, pltpu.HBM)
        for x in (velocity, surface, wet_mask, bathy_class, depth_table)
    )
    (side,) = call(
        edge_kernel, shape, [pl.ANY] * 5,
        [vmem((-(-tiles // SLOTS) * TILE, LANES), f32)],
        [vmem((4,) + near, f32), vmem(near, f32), vmem(near, i32), vmem(near, i32)]
        + table + [full] + arrived,
        inputs,
        cost(10**5),
    )
    far = lax.ppermute(side, "cross", [(0, 1), (1, 0)])
    own, out_chip, in_chip = call(
        pack_kernel, shape, [pl.ANY] * 5,
        [vmem((FIELDS, shape.own, shape.rows, LANES), f32), wide, wide],
        [vmem(velocity.shape, f32), vmem(block, f32), vmem(block, i32), vmem(block, i32)]
        + table + arrived,
        inputs,
        cost(4 * 10**6),
    )
    out_chip, in_chip, side = call(
        corner_kernel, shape, [vmem] * 3, [wide, wide, full], [], held(far, out_chip, in_chip),
        cost(10**5), {1: 0, 2: 1},
    )
    firsts = [i for i in range(1, size, 2)]
    trades = lambda pairs: pairs + [(j, i) for i, j in pairs]
    out_pairs = trades([(i, i + 1) for i in firsts[:-1]]) + [(0, 0), (size - 1, size - 1)]
    from_out = lax.ppermute(out_chip, "along", out_pairs)
    from_in = lax.ppermute(in_chip, "along", trades([(i - 1, i) for i in firsts]))
    (head,) = call(
        head_kernel, shape, [smem] * 2 + [vmem], [fields(1)],
        [vmem((SHIPS, shape.chunks, TILE, LANES), f32)],
        (hull_ranges.T, hull_pressure) + held(side),
        cost(2 * 10**6),
    )
    state = [fields(count) for count in (4, 5, 1, 6, 4, 1, 1)]
    partial = vmem((2 * ITERS, TILE, LANES), f32)
    *inner, partial = call(
        inner_kernel, shape, [vmem] * 3, state + [partial], [],
        held(own, side, head),
        cost(10**7),
    )
    moved, static, level, krylov, _, _, _, moments = call(
        outer_kernel, shape, [vmem] * 11, state + [sums], [corner, corner],
        held(from_out, from_in, head, partial, *inner),
        cost(10**7), {4 + number: number for number in range(7)},
    )
    moved, level, krylov, moments = call(
        second_kernel, shape, [vmem] * 5,
        [fields(4), fields(1), fields(6), sums],
        [fields(4), fields(1), fields(2), fields(2)],
        (shared(moments),) + held(moved, static, level, krylov),
    )
    whole = lambda like: jax.ShapeDtypeStruct(like, f32)
    return tuple(
        call(
            last_kernel, shape, [vmem] * 5,
            [whole(velocity.shape), whole(surface.shape), whole((2,) + surface.shape)],
            [fields(2), fields(2)],
            (shared(moments),) + held(moved, static, level, krylov),
        )
    )


def solution(mesh):
    cell = P("along", "cross")
    layered = P(None, "along", "cross")
    in_specs = (layered, cell, cell, cell, P(), P(), P())
    return jax.shard_map(
        shards, mesh=mesh, in_specs=in_specs, out_specs=(layered, cell, layered), check_vma=False
    )
```

```python
import functools

import jax
import jax.numpy as jnp
from jax import lax
from jax.experimental import pallas as pl
from jax.experimental.pallas import tpu as pltpu
from jax.sharding import PartitionSpec as P

ITERS = 3
CLASSES = 16
SHIPS = 8

gravity = 9.81
time_step = 0.1
storage = 0.1
corner_weight = 0.25

LANES = 128
TILE = 8
GUARD = 8
HALO = 16
FIELDS = 7
SENT = (13, 13, 13, 13, 12, 11, 11)
OFFSETS = (0, 13, 26, 39, 52, 64, 75)
SENT_ROWS = 88
CORNER_ROWS = 16
EDGE = 16
SLOTS = LANES // EDGE
VMEM_BYTES = 24 * 1024 * 1024


class Shape:
    def __init__(self, rows, cols):
        self.rows = rows
        self.own = cols // LANES
        self.chunks = self.own + 1
        self.first = GUARD + HALO
        self.total = rows + 2 * (GUARD + HALO)


class Ring:
    def __init__(self, make, chunks, lane):
        self.make = make
        self.chunks = chunks
        self.lane = lane
        self.held = {}

    def at(self, chunk):
        entry = self.held.setdefault(chunk, {})
        if 0 not in entry:
            entry[0] = self.make(chunk)
        return entry[0]

    def rolled(self, chunk, amount):
        value = self.at(chunk)
        entry = self.held[chunk]
        if amount not in entry:
            entry[amount] = pltpu.roll(value, amount, 1)
        return entry[amount]

    def before(self, chunk, step):
        other = (chunk - 1) % self.chunks
        return jnp.where(self.lane < step, self.rolled(other, step), self.rolled(chunk, step))

    def after(self, chunk, step):
        other = (chunk + 1) % self.chunks
        amount = LANES - step
        return jnp.where(self.lane >= amount, self.rolled(other, amount), self.rolled(chunk, amount))

    def done(self, chunk):
        self.held.pop((chunk - 1) % self.chunks, None)


def lanes_of():
    return lax.broadcasted_iota(jnp.int32, (TILE, LANES), 1)


def sweep(spans, body, carry=None):
    for first, tiles in spans:

        def turn(number, carry, first=first):
            row = first + number * TILE
            if carry is None:
                body(row)
                return None
            return body(row, carry)

        carry = lax.fori_loop(0, tiles, turn, carry)
    return carry


def load(ref, index, chunk, row):
    return ref[index, chunk, pl.ds(row, TILE), :]


def store(ref, index, chunk, row, value):
    ref[index, chunk, pl.ds(row, TILE), :] = value


CONDUCT, HALF_RATE, INVERSE, HEAD, DIAGONAL = range(5)


def predict_rows(shape, vel, head_pressure, static, moved, row):
    lane = lanes_of()
    rings = [
        Ring(lambda c, k=k: load(vel, k, c, row), shape.chunks, lane) for k in range(4)
    ]
    potential = Ring(lambda c: load(head_pressure, 0, c, row), shape.chunks, lane)
    for c in range(shape.chunks):
        wet = load(static, CONDUCT, c, row) > 0.0
        rate = time_step * load(static, HALF_RATE, c, row)
        slope_a = (0.5 * time_step) * (
            load(head_pressure, 0, c, row + 1) - load(head_pressure, 0, c, row - 1)
        )
        slope_c = (0.5 * time_step) * (potential.after(c, 1) - potential.before(c, 1))
        for layer in range(2):
            along = rings[layer].at(c)
            cross = rings[2 + layer].at(c)
            up_a = (0.5 * time_step) * jnp.maximum(along, 0.0)
            dn_a = (0.5 * time_step) * jnp.minimum(along, 0.0)
            up_c = (0.5 * time_step) * jnp.maximum(cross, 0.0)
            dn_c = (0.5 * time_step) * jnp.minimum(cross, 0.0)
            centre = (
                0.8 - 3.0 * ((up_a - dn_a) + (up_c - dn_c)) - (rate if layer == 0 else 2.0 * rate)
            )
            back_a = 0.05 + 4.0 * up_a
            fore_a = 0.05 - 4.0 * dn_a
            back_c = 0.05 + 4.0 * up_c
            fore_c = 0.05 - 4.0 * dn_c
            for part, slope in ((layer, slope_a), (2 + layer, slope_c)):
                ring = rings[part]
                other = rings[part + 1 - 2 * layer].at(c)
                value = centre * ring.at(c) + rate * other - slope
                value = value + (
                    back_a * load(vel, part, c, row - 1) - up_a * load(vel, part, c, row - 2)
                )
                value = value + (
                    fore_a * load(vel, part, c, row + 1) + dn_a * load(vel, part, c, row + 2)
                )
                value = value + (back_c * ring.before(c, 1) - up_c * ring.before(c, 2))
                value = value + (fore_c * ring.after(c, 1) + dn_c * ring.after(c, 2))
                store(moved, part, c, row, jnp.where(wet, value, 0.0))
        for ring in rings:
            ring.done(c)
        potential.done(c)


def source_rows(shape, moved, static, krylov, row):
    lane = lanes_of()
    rings = [
        Ring(
            lambda c, k=k: load(static, CONDUCT, c, row) * load(moved, 2 + k, c, row),
            shape.chunks,
            lane,
        )
        for k in range(2)
    ]
    for c in range(shape.chunks):
        above = load(static, CONDUCT, c, row - 1)
        below = load(static, CONDUCT, c, row + 1)
        scale = (-0.5 / time_step) * load(static, INVERSE, c, row)
        for layer in range(2):
            flow = (
                below * load(moved, layer, c, row + 1)
                - above * load(moved, layer, c, row - 1)
                + (rings[layer].after(c, 1) - rings[layer].before(c, 1))
            )
            store(krylov, layer, c, row, scale * flow)
            rings[layer].done(c)


def link_rows(shape, krylov, static, level, row, own_only):
    lane = lanes_of()

    def plain(layer, c):
        values = [load(krylov, 2 * level + layer, c, row + d) for d in (-1, 0, 1)]
        return values[1], values[0] + values[2]

    def weighted(layer, c):
        values = [
            load(static, CONDUCT, c, row + d) * load(krylov, 2 * level + layer, c, row + d)
            for d in (-1, 0, 1)
        ]
        return values[1], values[0] + values[2]

    sides = {}

    def ring_of(kind, layer):
        def make(c):
            middle, sums = kind(layer, c)
            sides[kind, layer, c] = sums
            return middle + corner_weight * sums

        return Ring(make, shape.chunks, lane)

    rings = [(ring_of(plain, layer), ring_of(weighted, layer)) for layer in range(2)]
    for c in range(shape.own if own_only else shape.chunks):
        conduct = load(static, CONDUCT, c, row)
        rate = load(static, HALF_RATE, c, row)
        centre = [load(krylov, 2 * level + layer, c, row) for layer in range(2)]
        results = []
        for layer in range(2):
            ring, scaled = rings[layer]
            around = (ring.before(c, 1) + ring.after(c, 1)) + sides[plain, layer, c]
            flows = (scaled.before(c, 1) + scaled.after(c, 1)) + sides[weighted, layer, c]
            results.append(0.5 * (conduct * around + flows) + rate * centre[1 - layer])
            ring.done(c)
            scaled.done(c)
        yield c, centre, results


def krylov_rows(shape, krylov, static, level, row):
    for c, _, results in link_rows(shape, krylov, static, level, row, False):
        inverse = load(static, INVERSE, c, row)
        for layer in range(2):
            store(krylov, 2 * level + 2 + layer, c, row, inverse * results[layer])


def moments_of(shape, krylov, static, span, sums):
    def turn(row, sums):
        sums = list(sums)
        for c, top, results in link_rows(shape, krylov, static, 2, row, True):
            diagonal = load(static, DIAGONAL, c, row)
            for layer in range(2):
                low = load(krylov, layer, c, row)
                mid = load(krylov, 2 + layer, c, row)
                low_d, mid_d, top_d = diagonal * low, diagonal * mid, diagonal * top[layer]
                terms = (
                    low * low_d,
                    low * mid_d,
                    mid * mid_d,
                    mid * top_d,
                    top[layer] * top_d,
                    top[layer] * results[layer],
                )
                sums = [a + b for a, b in zip(sums, terms)]
        return tuple(sums)

    return sweep(span, turn, tuple(sums))


def no_moments():
    return (jnp.zeros((TILE, LANES), jnp.float32),) * (2 * ITERS)


def put_moments(out, sums):
    lane = lanes_of()
    result = jnp.zeros((TILE, LANES), jnp.float32)
    for number, part in enumerate(sums):
        result = jnp.where(lane == number, jnp.sum(part), result)
    out[...] = jnp.broadcast_to(result[0:1, None, 0 : out.shape[2]], out.shape)


def project(shape, vel, potential, static, moved, krylov, spans, sums):
    sweep(spans[0], functools.partial(predict_rows, shape, vel, potential, static, moved))
    sweep(spans[1], functools.partial(source_rows, shape, moved, static, krylov))
    for level in range(2):
        sweep(spans[2 + level], functools.partial(krylov_rows, shape, krylov, static, level))
    return moments_of(shape, krylov, static, spans[4], sums)


def fetch(pairs, arrived):
    copies = [
        pltpu.make_async_copy(source, target, arrived.at[number])
        for number, (source, target) in enumerate(pairs)
    ]
    for copy in copies:
        copy.start()
    for copy in copies:
        copy.wait()


def cell_values(vel, surface, wet, bathy, table, rows, cols):
    flag = wet[rows, cols]
    entry = bathy[rows, cols]
    thick = jnp.zeros((TILE, LANES), jnp.float32)
    for choice in range(CLASSES):
        thick = jnp.where(entry == choice, 0.5 * table[choice], thick)
    values = [jnp.where(flag > 0, vel[k, rows, cols], 0.0) for k in range(4)]
    return values + [surface[rows, cols], flag.astype(jnp.float32), thick]


def edge_kernel(
    shape, vel_in, surface_in, wet_in, bathy_in, table_in, side,
    vel, surface, wet, bathy, table, edge, arrived,
):
    half = lax.axis_index("cross")
    first = jnp.where(half == 0, (shape.own - 1) * LANES, 0)
    near = pl.ds(pl.multiple_of(first, LANES), LANES)
    fetch(
        (
            (table_in, table),
            (bathy_in.at[:, near], bathy),
            (wet_in.at[:, near], wet),
            (surface_in.at[:, near], surface),
            (vel_in.at[:, :, near], vel),
        ),
        arrived,
    )
    for t in range(shape.rows // TILE):
        rows = pl.ds(t * TILE, TILE)
        values = cell_values(vel, surface, wet, bathy, table, rows, pl.ds(0, LANES))
        for k, value in enumerate(values):
            edge[k, rows, :] = value
    squeeze(side, 0, side_tiles(shape, edge), jnp.where(half == 0, EDGE, 0))


def pack_kernel(
    shape, vel_in, surface_in, wet_in, bathy_in, table_in,
    own, out_chip, in_chip,
    vel, surface, wet, bathy, table, arrived,
):
    fetch(
        (
            (table_in, table),
            (bathy_in, bathy),
            (wet_in, wet),
            (surface_in, surface),
            (vel_in, vel),
        ),
        arrived,
    )

    def turn(number, carry):
        rows = pl.ds(pl.multiple_of(number * TILE, TILE), TILE)
        for c in range(shape.own):
            cols = pl.ds(c * LANES, LANES)
            values = cell_values(vel, surface, wet, bathy, table, rows, cols)
            for k, value in enumerate(values):
                own[k, c, rows, :] = value
        return carry

    lax.fori_loop(0, shape.rows // TILE, turn, 0)
    core = lax.rem(lax.axis_index("along"), 2)
    for c in range(shape.own):
        for k in range(FIELDS):
            for part in (0, SENT[k] - TILE):
                to = pl.ds(c * SENT_ROWS + OFFSETS[k] + part, TILE)
                last = shape.rows - SENT[k]
                out_chip[to, :] = own[k, c, pl.ds(part + core * last, TILE), :]
                in_chip[to, :] = own[k, c, pl.ds(part + (1 - core) * last, TILE), :]


def corner_kernel(shape, far, out_in, in_in, out_chip, in_chip, side):
    half = lax.axis_index("cross")
    core = lax.rem(lax.axis_index("along"), 2)
    for number, tile in enumerate(side_tiles(shape, side)):
        tile[...] = spread(far, 0, number, half)
    shift = jnp.where(half == 0, 0, EDGE)
    squeeze(out_chip, shape.own * SENT_ROWS, corner_tiles(shape, side, core), shift)
    squeeze(in_chip, shape.own * SENT_ROWS, corner_tiles(shape, side, 1 - core), shift)


def side_tiles(shape, edge):
    return [
        edge.at[k, pl.ds(row, TILE), :] for k in range(FIELDS) for row in range(0, shape.rows, TILE)
    ]


def corner_parts():
    return [(k, part) for k in range(FIELDS) for part in (0, SENT[k] - TILE)]


def corner_tiles(shape, edge, last):
    return [
        edge.at[k, pl.ds(part + last * (shape.rows - SENT[k]), TILE), :]
        for k, part in corner_parts()
    ]


def squeeze(out, base, tiles, shift):
    slot = lanes_of() // EDGE
    for first in range(0, len(tiles), SLOTS):
        value = jnp.zeros((TILE, LANES), jnp.float32)
        for number, tile in enumerate(tiles[first : first + SLOTS]):
            moved = pltpu.roll(tile[...], lax.rem(EDGE * number + shift, LANES), 1)
            value = jnp.where(slot == number, moved, value)
        out[pl.ds(base + first, TILE), :] = value


def spread(source, base, number, half):
    lane = lanes_of()
    tile = source[pl.ds(base + number // SLOTS * TILE, TILE), :]
    amount = LANES - EDGE * (number % SLOTS) - jnp.where(half == 0, 0, EDGE)
    moved = pltpu.roll(tile, lax.rem(amount + LANES, LANES), 1)
    wanted = jnp.where(half == 0, lane, LANES - 1 - lane) < EDGE
    return jnp.where(wanted, moved, 0.0)


def head_kernel(shape, ranges, heads, side, head, columns):
    along = lax.axis_index("along")
    half = lax.axis_index("cross")
    lane = lanes_of()
    line = lax.broadcasted_iota(jnp.int32, (TILE, LANES), 0)
    for c in range(shape.chunks):
        if c < shape.own:
            index = half * (shape.own * LANES) + c * LANES + lane
        else:
            index = jnp.where(half == 0, shape.own * LANES, (shape.own - 1) * LANES) + lane
        for s in range(SHIPS):
            inside = jnp.logical_and(index >= ranges[2, s], index < ranges[3, s])
            columns[s, c] = jnp.where(inside, gravity * heads[s], 0.0)

    def head_rows(row):
        global_row = along * shape.rows + (row - shape.first) + line
        covered = [
            jnp.logical_and(global_row >= ranges[0, s], global_row < ranges[1, s])
            for s in range(SHIPS)
        ]
        for c in range(shape.chunks):
            value = jnp.zeros((TILE, LANES), jnp.float32)
            for s in range(SHIPS):
                value = value + jnp.where(covered[s], columns[s, c], 0.0)
            store(head, 0, c, row, value)

    sweep([(GUARD, shape.total // TILE - 2)], head_rows)


def place(refs, head, c, row, values):
    moved, static, surface, krylov, vel, potential, thick = refs
    for k in range(4):
        store(vel, k, c, row, values[k])
    depth = values[6]
    inside = depth > 0.0
    ship = jnp.where(inside, load(head, 0, c, row), 0.0)
    store(surface, 0, c, row, values[4])
    store(potential, 0, c, row, gravity * values[4] + ship)
    store(thick, 0, c, row, depth)
    store(static, CONDUCT, c, row, values[5] * depth)
    store(static, HALF_RATE, c, row, 0.5 / jnp.where(inside, depth, 1.0))
    store(static, HEAD, c, row, ship)


def diagonal_rows(shape, static, thick, row):
    sides = {}

    def make(c):
        sums = load(static, CONDUCT, c, row - 1) + load(static, CONDUCT, c, row + 1)
        sides[c] = sums
        return load(static, CONDUCT, c, row) + corner_weight * sums

    ring = Ring(make, shape.chunks, lanes_of())
    for c in range(shape.chunks):
        around = ring.before(c, 1) + ring.after(c, 1) + sides[c]
        depth = load(thick, 0, c, row)
        diagonal = (
            0.5 * (around + 5.0 * load(static, CONDUCT, c, row))
            + storage * depth
            + load(static, HALF_RATE, c, row)
        )
        store(static, DIAGONAL, c, row, diagonal)
        store(static, INVERSE, c, row, jnp.where(depth > 0.0, 1.0 / diagonal, 0.0))
        ring.done(c)


def inner_kernel(shape, own, side, head, *refs):
    refs, partial = refs[:7], refs[7]
    moved, static, surface, krylov, vel, potential, thick = refs

    def own_rows(row):
        at = row - shape.first
        for c in range(shape.chunks):
            if c < shape.own:
                values = [load(own, k, c, at) for k in range(FIELDS)]
            else:
                values = [side[k, pl.ds(at, TILE), :] for k in range(FIELDS)]
            place(refs, head, c, row, values)

    sweep([(shape.first, shape.rows // TILE)], own_rows)
    middle = [(shape.first + 4, shape.rows // TILE - 1)]
    sweep(middle, functools.partial(diagonal_rows, shape, static, thick))
    spans = [middle] * 4 + [[(shape.first + 8, shape.rows // TILE - 2)]]
    sums = project(shape, vel, potential, static, moved, krylov, spans, no_moments())
    for number, value in enumerate(sums):
        partial[number] = value


def outer_kernel(shape, out_chip, in_chip, head, partial, *refs):
    refs = refs[7:]
    moments, out_corner, in_corner = refs[7:]
    refs = refs[:7]
    moved, static, surface, krylov, vel, potential, thick = refs
    along = lax.axis_index("along")
    half = lax.axis_index("cross")
    for number, (k, part) in enumerate(corner_parts()):
        to = pl.ds(OFFSETS[k] + part, TILE)
        out_corner[to, :] = spread(out_chip, shape.own * SENT_ROWS, number, half)
        in_corner[to, :] = spread(in_chip, shape.own * SENT_ROWS, number, half)
    deepest = SENT[0]
    last = lax.axis_size("along") - 1

    def place_piece(wide, narrow, below):
        keep = (last - along if below else along) > 0
        for start in (0, deepest - TILE) if below else (-deepest, -TILE):
            for c in range(shape.chunks):
                source, skip = (wide, c * SENT_ROWS) if c < shape.own else (narrow, 0)
                values = []
                for k in range(FIELDS):
                    at = skip + OFFSETS[k] + start + (0 if below else SENT[k])
                    values.append(jnp.where(keep, source[pl.ds(at, TILE), :], 0.0))
                place(refs, head, c, shape.first + start + (shape.rows if below else 0), values)

    core = lax.rem(along, 2)
    for which in range(2):

        @pl.when(core == which)
        def _(which=which):
            place_piece(out_chip, out_corner, which == 1)
            place_piece(in_chip, in_corner, which == 0)

    def both(halo):
        return [(shape.first - halo, 2), (shape.first + shape.rows + halo - 2 * TILE, 2)]

    sweep(both(11), functools.partial(diagonal_rows, shape, static, thick))
    spans = [both(halo) for halo in (11, 10, 9, 8)]
    spans += [[(shape.first, 1), (shape.first + shape.rows - TILE, 1)]]
    sums = [partial[number] for number in range(2 * ITERS)]
    put_moments(moments, project(shape, vel, potential, static, moved, krylov, spans, sums))


def coefficients(shares):
    total = jnp.sum(shares[...], axis=0)
    mu = [jnp.broadcast_to(total[:, k : k + 1], (TILE, LANES)) for k in range(2 * ITERS)]

    def norm(c):
        return sum(c[i] * c[j] * mu[i + j] for i in range(len(c)) for j in range(len(c)))

    def energy(c):
        return sum(
            c[i] * c[j] * (mu[i + j] - mu[i + j + 1]) for i in range(len(c)) for j in range(len(c))
        )

    floor = 2e-7 * mu[0]
    one = jnp.ones((TILE, LANES), jnp.float32)
    z = [one]
    search = [one]
    result = [jnp.zeros((TILE, LANES), jnp.float32)] * ITERS
    norm_now = mu[0]
    for iteration in range(ITERS):
        step = norm_now / energy(search)
        if iteration:
            step = jnp.where(norm_now > floor, step, 0.0)
        for i, c in enumerate(search):
            result[i] = result[i] + step * c
        if iteration + 1 < ITERS:
            applied = [
                (search[i] if i < len(search) else 0.0) - (search[i - 1] if i else 0.0)
                for i in range(len(search) + 1)
            ]
            z = [(z[i] if i < len(z) else 0.0) - step * applied[i] for i in range(len(applied))]
            norm_next = norm(z)
            ratio = norm_next / norm_now
            if iteration:
                ratio = jnp.where(norm_now > floor, ratio, 0.0)
            search = [z[i] + (ratio * search[i] if i < len(search) else 0.0) for i in range(len(z))]
            norm_now = norm_next
    return result


def pressure_rows(shape, factors, krylov, pressure, row):
    for c in range(shape.chunks):
        for layer in range(2):
            value = factors[0] * load(krylov, layer, c, row)
            value = value + factors[1] * load(krylov, 2 + layer, c, row)
            value = value + factors[2] * load(krylov, 4 + layer, c, row)
            store(pressure, layer, c, row, value)


def along_moved(moved, pressure, layer, c, row):
    return load(moved, layer, c, row) - (0.5 * time_step) * (
        load(pressure, layer, c, row + 1) - load(pressure, layer, c, row - 1)
    )


def move_rows(shape, moved, pressure, static, flux, put, row):
    lane = lanes_of()
    rings = [
        Ring(lambda c, k=k: load(pressure, k, c, row), shape.chunks, lane) for k in range(2)
    ]
    for c in range(shape.chunks):
        conduct = load(static, CONDUCT, c, row)
        wet = conduct > 0.0
        along = [along_moved(moved, pressure, layer, c, row) for layer in range(2)]
        cross = [
            load(moved, 2 + layer, c, row)
            - (0.5 * time_step) * (rings[layer].after(c, 1) - rings[layer].before(c, 1))
            for layer in range(2)
        ]
        for part, value in enumerate(along + cross):
            put(part, c, row, jnp.where(wet, value, 0.0))
        store(flux, 0, c, row, conduct * (along[0] + along[1]))
        store(flux, 1, c, row, conduct * (cross[0] + cross[1]))
        for ring in rings:
            ring.done(c)


def surface_rows(shape, surface, flux, chunks, put, row):
    ring = Ring(lambda c: load(flux, 1, c, row), shape.chunks, lanes_of())
    for c in range(chunks):
        value = load(surface, 0, c, row) - (0.5 * time_step) * (
            load(flux, 0, c, row + 1)
            - load(flux, 0, c, row - 1)
            + (ring.after(c, 1) - ring.before(c, 1))
        )
        put(c, row, value)
        ring.done(c)


def second_kernel(
    shape, shares, moved_in, static, surface_in, krylov_in,
    moved, surface, krylov, moments,
    vel, potential, pressure, flux,
):
    factors = coefficients(shares)
    start = GUARD
    sweep([(start + 8, 6)], functools.partial(pressure_rows, shape, factors, krylov_in, pressure))
    put_vel = functools.partial(store, vel)
    sweep(
        [(start + 9, 6)],
        functools.partial(move_rows, shape, moved_in, pressure, static, flux, put_vel),
    )

    def put(c, row, value):
        value = jnp.where(load(static, INVERSE, c, row) > 0.0, value, 0.0)
        store(surface, 0, c, row, value)
        store(potential, 0, c, row, gravity * value + load(static, HEAD, c, row))

    sweep(
        [(start + 10, 6)],
        functools.partial(surface_rows, shape, surface_in, flux, shape.chunks, put),
    )
    spans = [[(start + 11, 6)], [(start + 12, 5)], [(start + 13, 5)], [(start + 14, 5)]]
    spans += [[(shape.first, shape.rows // TILE)]]
    put_moments(
        moments, project(shape, vel, potential, static, moved, krylov, spans, no_moments())
    )


def last_kernel(
    shape, shares, moved, static, surface, krylov,
    new_vel, new_surface, new_pressure,
    pressure, flux,
):
    factors = coefficients(shares)
    start = shape.first
    sweep([(start - 2, 5)], functools.partial(pressure_rows, shape, factors, krylov, pressure))

    def put_vel(part, c, row, value):
        if c < shape.own:
            at = pl.multiple_of(row - start, TILE)
            new_vel[part, pl.ds(at, TILE), pl.ds(c * LANES, LANES)] = value
            if part < 2:
                new_pressure[part, pl.ds(at, TILE), pl.ds(c * LANES, LANES)] = load(
                    pressure, part, c, row
                )

    sweep(
        [(start, shape.rows // TILE)],
        functools.partial(move_rows, shape, moved, pressure, static, flux, put_vel),
    )
    for row in (start - 1, start + shape.rows):
        for c in range(shape.own):
            one = slice(row, row + 1)
            total = jnp.zeros((1, LANES), jnp.float32)
            for layer in range(2):
                total = total + (
                    moved[layer, c, one, :]
                    - (0.5 * time_step)
                    * (
                        pressure[layer, c, row + 1 : row + 2, :]
                        - pressure[layer, c, row - 1 : row, :]
                    )
                )
            flux[0, c, one, :] = static[CONDUCT, c, one, :] * total

    def put(c, row, value):
        at = pl.multiple_of(row - start, TILE)
        new_surface[pl.ds(at, TILE), pl.ds(c * LANES, LANES)] = value

    sweep(
        [(start, shape.rows // TILE)],
        functools.partial(surface_rows, shape, surface, flux, shape.own, put),
    )


def cost(flops):
    return pl.CostEstimate(flops=flops, bytes_accessed=flops, transcendentals=0)


def call(kernel, shape, kinds, outs, scratch, operands, estimate=None, aliases={}):
    return pl.pallas_call(
        functools.partial(kernel, shape),
        out_shape=outs,
        in_specs=[pl.BlockSpec(memory_space=kind) for kind in kinds],
        out_specs=[pl.BlockSpec(memory_space=pltpu.VMEM)] * len(outs),
        scratch_shapes=scratch,
        cost_estimate=estimate,
        input_output_aliases=aliases,
        compiler_params=pltpu.CompilerParams(vmem_limit_bytes=VMEM_BYTES),
    )(*operands)


def held(*arrays):
    return tuple(pltpu.with_memory_space_constraint(x, pltpu.VMEM) for x in arrays)


def shared(moments):
    return lax.all_to_all(moments, ("along", "cross"), 0, 0, tiled=True)


def shards(velocity, surface, wet_mask, bathy_class, depth_table, hull_ranges, hull_pressure):
    shape = Shape(*surface.shape)
    vmem, smem = pltpu.VMEM, pltpu.SMEM
    f32, i32 = jnp.float32, jnp.int32
    size = lax.axis_size("along")
    field = (shape.chunks, shape.total, LANES)
    fields = lambda count: vmem((count,) + field, f32)
    sums = jax.ShapeDtypeStruct((2 * size, 1, 8), f32)
    block = surface.shape
    wide = vmem((shape.own * SENT_ROWS + CORNER_ROWS, LANES), f32)
    full = vmem((FIELDS, shape.rows, LANES), f32)
    corner = vmem((SENT_ROWS, LANES), f32)
    tiles = FIELDS * shape.rows // TILE
    table = [smem(depth_table.shape, f32)]
    arrived = [pltpu.SemaphoreType.DMA((5,))]
    near = (shape.rows, LANES)
    inputs = tuple(
        pltpu.with_memory_space_constraint(x, pltpu.HBM)
        for x in (velocity, surface, wet_mask, bathy_class, depth_table)
    )
    (side,) = call(
        edge_kernel, shape, [pl.ANY] * 5,
        [vmem((-(-tiles // SLOTS) * TILE, LANES), f32)],
        [vmem((4,) + near, f32), vmem(near, f32), vmem(near, i32), vmem(near, i32)]
        + table + [full] + arrived,
        inputs,
        cost(10**5),
    )
    far = lax.ppermute(side, "cross", [(0, 1), (1, 0)])
    own, out_chip, in_chip = call(
        pack_kernel, shape, [pl.ANY] * 5,
        [vmem((FIELDS, shape.own, shape.rows, LANES), f32), wide, wide],
        [vmem(velocity.shape, f32), vmem(block, f32), vmem(block, i32), vmem(block, i32)]
        + table + arrived,
        inputs,
        cost(4 * 10**6),
    )
    out_chip, in_chip, side = call(
        corner_kernel, shape, [vmem] * 3, [wide, wide, full], [], held(far, out_chip, in_chip),
        cost(10**5), {1: 0, 2: 1},
    )
    firsts = [i for i in range(1, size, 2)]
    trades = lambda pairs: pairs + [(j, i) for i, j in pairs]
    ends = [(0, 1), (2 * size - 2, 2 * size - 1)]
    next_chip = [(2 * i + j, 2 * i + 2 + j) for i in firsts[:-1] for j in range(2)]
    from_out = lax.ppermute(out_chip, ("along", "cross"), trades(next_chip + ends))
    from_in = lax.ppermute(in_chip, "along", trades([(i - 1, i) for i in firsts]))
    (head,) = call(
        head_kernel, shape, [smem] * 2 + [vmem], [fields(1)],
        [vmem((SHIPS, shape.chunks, TILE, LANES), f32)],
        (hull_ranges.T, hull_pressure) + held(side),
        cost(2 * 10**6),
    )
    state = [fields(count) for count in (4, 5, 1, 6, 4, 1, 1)]
    partial = vmem((2 * ITERS, TILE, LANES), f32)
    *inner, partial = call(
        inner_kernel, shape, [vmem] * 3, state + [partial], [],
        held(own, side, head),
        cost(10**7),
    )
    moved, static, level, krylov, _, _, _, moments = call(
        outer_kernel, shape, [vmem] * 11, state + [sums], [corner, corner],
        held(from_out, from_in, head, partial, *inner),
        cost(10**7), {4 + number: number for number in range(7)},
    )
    moved, level, krylov, moments = call(
        second_kernel, shape, [vmem] * 5,
        [fields(4), fields(1), fields(6), sums],
        [fields(4), fields(1), fields(2), fields(2)],
        (shared(moments),) + held(moved, static, level, krylov),
    )
    whole = lambda like: jax.ShapeDtypeStruct(like, f32)
    return tuple(
        call(
            last_kernel, shape, [vmem] * 5,
            [whole(velocity.shape), whole(surface.shape), whole((2,) + surface.shape)],
            [fields(2), fields(2)],
            (shared(moments),) + held(moved, static, level, krylov),
        )
    )


def solution(mesh):
    cell = P("along", "cross")
    layered = P(None, "along", "cross")
    in_specs = (layered, cell, cell, cell, P(), P(), P())
    return jax.shard_map(
        shards, mesh=mesh, in_specs=in_specs, out_specs=(layered, cell, layered), check_vma=False
    )
```

```python
import functools

import jax
import jax.numpy as jnp
from jax import lax
from jax.experimental import pallas as pl
from jax.experimental.pallas import tpu as pltpu
from jax.sharding import PartitionSpec as P

ITERS = 3
CLASSES = 16
SHIPS = 8

gravity = 9.81
time_step = 0.1
storage = 0.1
corner_weight = 0.25

LANES = 128
TILE = 8
GUARD = 8
HALO = 16
FIELDS = 7
SENT = (13, 13, 13, 13, 12, 11, 11)
OFFSETS = (0, 13, 26, 39, 52, 64, 75)
SENT_ROWS = 88
CORNER_ROWS = 16
EDGE = 16
SLOTS = LANES // EDGE
VMEM_BYTES = 24 * 1024 * 1024


class Shape:
    def __init__(self, rows, cols):
        self.rows = rows
        self.own = cols // LANES
        self.chunks = self.own + 1
        self.first = GUARD + HALO
        self.total = rows + 2 * (GUARD + HALO)


class Ring:
    def __init__(self, make, chunks, lane):
        self.make = make
        self.chunks = chunks
        self.lane = lane
        self.held = {}

    def at(self, chunk):
        entry = self.held.setdefault(chunk, {})
        if 0 not in entry:
            entry[0] = self.make(chunk)
        return entry[0]

    def rolled(self, chunk, amount):
        value = self.at(chunk)
        entry = self.held[chunk]
        if amount not in entry:
            entry[amount] = pltpu.roll(value, amount, 1)
        return entry[amount]

    def before(self, chunk, step):
        other = (chunk - 1) % self.chunks
        return jnp.where(self.lane < step, self.rolled(other, step), self.rolled(chunk, step))

    def after(self, chunk, step):
        other = (chunk + 1) % self.chunks
        amount = LANES - step
        return jnp.where(self.lane >= amount, self.rolled(other, amount), self.rolled(chunk, amount))

    def done(self, chunk):
        self.held.pop((chunk - 1) % self.chunks, None)


def lanes_of():
    return lax.broadcasted_iota(jnp.int32, (TILE, LANES), 1)


def sweep(spans, body, carry=None):
    for first, tiles in spans:

        def turn(number, carry, first=first):
            row = first + number * TILE
            if carry is None:
                body(row)
                return None
            return body(row, carry)

        carry = lax.fori_loop(0, tiles, turn, carry)
    return carry


def load(ref, index, chunk, row):
    return ref[index, chunk, pl.ds(row, TILE), :]


def store(ref, index, chunk, row, value):
    ref[index, chunk, pl.ds(row, TILE), :] = value


CONDUCT, HALF_RATE, INVERSE, HEAD, DIAGONAL = range(5)


def predict_rows(shape, vel, head_pressure, static, moved, row):
    lane = lanes_of()
    rings = [
        Ring(lambda c, k=k: load(vel, k, c, row), shape.chunks, lane) for k in range(4)
    ]
    potential = Ring(lambda c: load(head_pressure, 0, c, row), shape.chunks, lane)
    for c in range(shape.chunks):
        wet = load(static, CONDUCT, c, row) > 0.0
        rate = time_step * load(static, HALF_RATE, c, row)
        slope_a = (0.5 * time_step) * (
            load(head_pressure, 0, c, row + 1) - load(head_pressure, 0, c, row - 1)
        )
        slope_c = (0.5 * time_step) * (potential.after(c, 1) - potential.before(c, 1))
        for layer in range(2):
            along = rings[layer].at(c)
            cross = rings[2 + layer].at(c)
            up_a = (0.5 * time_step) * jnp.maximum(along, 0.0)
            dn_a = (0.5 * time_step) * jnp.minimum(along, 0.0)
            up_c = (0.5 * time_step) * jnp.maximum(cross, 0.0)
            dn_c = (0.5 * time_step) * jnp.minimum(cross, 0.0)
            centre = (
                0.8 - 3.0 * ((up_a - dn_a) + (up_c - dn_c)) - (rate if layer == 0 else 2.0 * rate)
            )
            back_a = 0.05 + 4.0 * up_a
            fore_a = 0.05 - 4.0 * dn_a
            back_c = 0.05 + 4.0 * up_c
            fore_c = 0.05 - 4.0 * dn_c
            for part, slope in ((layer, slope_a), (2 + layer, slope_c)):
                ring = rings[part]
                other = rings[part + 1 - 2 * layer].at(c)
                value = centre * ring.at(c) + rate * other - slope
                value = value + (
                    back_a * load(vel, part, c, row - 1) - up_a * load(vel, part, c, row - 2)
                )
                value = value + (
                    fore_a * load(vel, part, c, row + 1) + dn_a * load(vel, part, c, row + 2)
                )
                value = value + (back_c * ring.before(c, 1) - up_c * ring.before(c, 2))
                value = value + (fore_c * ring.after(c, 1) + dn_c * ring.after(c, 2))
                store(moved, part, c, row, jnp.where(wet, value, 0.0))
        for ring in rings:
            ring.done(c)
        potential.done(c)


def source_rows(shape, moved, static, krylov, row):
    lane = lanes_of()
    rings = [
        Ring(
            lambda c, k=k: load(static, CONDUCT, c, row) * load(moved, 2 + k, c, row),
            shape.chunks,
            lane,
        )
        for k in range(2)
    ]
    for c in range(shape.chunks):
        above = load(static, CONDUCT, c, row - 1)
        below = load(static, CONDUCT, c, row + 1)
        scale = (-0.5 / time_step) * load(static, INVERSE, c, row)
        for layer in range(2):
            flow = (
                below * load(moved, layer, c, row + 1)
                - above * load(moved, layer, c, row - 1)
                + (rings[layer].after(c, 1) - rings[layer].before(c, 1))
            )
            store(krylov, layer, c, row, scale * flow)
            rings[layer].done(c)


def link_rows(shape, krylov, static, level, row, own_only):
    lane = lanes_of()

    def plain(layer, c):
        values = [load(krylov, 2 * level + layer, c, row + d) for d in (-1, 0, 1)]
        return values[1], values[0] + values[2]

    def weighted(layer, c):
        values = [
            load(static, CONDUCT, c, row + d) * load(krylov, 2 * level + layer, c, row + d)
            for d in (-1, 0, 1)
        ]
        return values[1], values[0] + values[2]

    sides = {}

    def ring_of(kind, layer):
        def make(c):
            middle, sums = kind(layer, c)
            sides[kind, layer, c] = sums
            return middle + corner_weight * sums

        return Ring(make, shape.chunks, lane)

    rings = [(ring_of(plain, layer), ring_of(weighted, layer)) for layer in range(2)]
    for c in range(shape.own if own_only else shape.chunks):
        conduct = load(static, CONDUCT, c, row)
        rate = load(static, HALF_RATE, c, row)
        centre = [load(krylov, 2 * level + layer, c, row) for layer in range(2)]
        results = []
        for layer in range(2):
            ring, scaled = rings[layer]
            around = (ring.before(c, 1) + ring.after(c, 1)) + sides[plain, layer, c]
            flows = (scaled.before(c, 1) + scaled.after(c, 1)) + sides[weighted, layer, c]
            results.append(0.5 * (conduct * around + flows) + rate * centre[1 - layer])
            ring.done(c)
            scaled.done(c)
        yield c, centre, results


def krylov_rows(shape, krylov, static, level, row):
    for c, _, results in link_rows(shape, krylov, static, level, row, False):
        inverse = load(static, INVERSE, c, row)
        for layer in range(2):
            store(krylov, 2 * level + 2 + layer, c, row, inverse * results[layer])


def moments_of(shape, krylov, static, span, sums):
    def turn(row, sums):
        sums = list(sums)
        for c, top, results in link_rows(shape, krylov, static, 2, row, True):
            diagonal = load(static, DIAGONAL, c, row)
            for layer in range(2):
                low = load(krylov, layer, c, row)
                mid = load(krylov, 2 + layer, c, row)
                low_d, mid_d, top_d = diagonal * low, diagonal * mid, diagonal * top[layer]
                terms = (
                    low * low_d,
                    low * mid_d,
                    mid * mid_d,
                    mid * top_d,
                    top[layer] * top_d,
                    top[layer] * results[layer],
                )
                sums = [a + b for a, b in zip(sums, terms)]
        return tuple(sums)

    return sweep(span, turn, tuple(sums))


def no_moments():
    return (jnp.zeros((TILE, LANES), jnp.float32),) * (2 * ITERS)


def put_moments(out, sums):
    lane = lanes_of()
    result = jnp.zeros((TILE, LANES), jnp.float32)
    for number, part in enumerate(sums):
        result = jnp.where(lane == number, jnp.sum(part), result)
    out[...] = jnp.broadcast_to(result[0:1, None, 0 : out.shape[2]], out.shape)


def project(shape, vel, potential, static, moved, krylov, spans, sums):
    sweep(spans[0], functools.partial(predict_rows, shape, vel, potential, static, moved))
    sweep(spans[1], functools.partial(source_rows, shape, moved, static, krylov))
    for level in range(2):
        sweep(spans[2 + level], functools.partial(krylov_rows, shape, krylov, static, level))
    return moments_of(shape, krylov, static, spans[4], sums)


def fetch(pairs, arrived):
    copies = [
        pltpu.make_async_copy(source, target, arrived.at[number])
        for number, (source, target) in enumerate(pairs)
    ]
    for copy in copies:
        copy.start()
    for copy in copies:
        copy.wait()


def cell_values(vel, surface, wet, bathy, table, rows, cols):
    flag = wet[rows, cols]
    entry = bathy[rows, cols]
    thick = jnp.zeros((TILE, LANES), jnp.float32)
    for choice in range(CLASSES):
        thick = jnp.where(entry == choice, 0.5 * table[choice], thick)
    values = [jnp.where(flag > 0, vel[k, rows, cols], 0.0) for k in range(4)]
    return values + [surface[rows, cols], flag.astype(jnp.float32), thick]


def edge_kernel(
    shape, vel_in, surface_in, wet_in, bathy_in, table_in, side,
    vel, surface, wet, bathy, table, edge, arrived,
):
    half = lax.axis_index("cross")
    first = jnp.where(half == 0, (shape.own - 1) * LANES, 0)
    near = pl.ds(pl.multiple_of(first, LANES), LANES)
    fetch(
        (
            (table_in, table),
            (bathy_in.at[:, near], bathy),
            (wet_in.at[:, near], wet),
            (surface_in.at[:, near], surface),
            (vel_in.at[:, :, near], vel),
        ),
        arrived,
    )
    for t in range(shape.rows // TILE):
        rows = pl.ds(t * TILE, TILE)
        values = cell_values(vel, surface, wet, bathy, table, rows, pl.ds(0, LANES))
        for k, value in enumerate(values):
            edge[k, rows, :] = value
    squeeze(side, 0, side_tiles(shape, edge), jnp.where(half == 0, EDGE, 0))


def pack_kernel(
    shape, vel_in, surface_in, wet_in, bathy_in, table_in,
    own, out_chip, in_chip,
    vel, surface, wet, bathy, table, arrived,
):
    fetch(
        (
            (table_in, table),
            (bathy_in, bathy),
            (wet_in, wet),
            (surface_in, surface),
            (vel_in, vel),
        ),
        arrived,
    )

    def turn(number, carry):
        rows = pl.ds(pl.multiple_of(number * TILE, TILE), TILE)
        for c in range(shape.own):
            cols = pl.ds(c * LANES, LANES)
            values = cell_values(vel, surface, wet, bathy, table, rows, cols)
            for k, value in enumerate(values):
                own[k, c, rows, :] = value
        return carry

    lax.fori_loop(0, shape.rows // TILE, turn, 0)
    core = lax.rem(lax.axis_index("along"), 2)
    for c in range(shape.own):
        for k in range(FIELDS):
            for part in (0, SENT[k] - TILE):
                to = pl.ds(c * SENT_ROWS + OFFSETS[k] + part, TILE)
                last = shape.rows - SENT[k]
                out_chip[to, :] = own[k, c, pl.ds(part + core * last, TILE), :]
                in_chip[to, :] = own[k, c, pl.ds(part + (1 - core) * last, TILE), :]


def corner_kernel(shape, far, out_in, in_in, out_chip, in_chip, side):
    half = lax.axis_index("cross")
    core = lax.rem(lax.axis_index("along"), 2)
    for number, tile in enumerate(side_tiles(shape, side)):
        tile[...] = spread(far, 0, number, half)
    shift = jnp.where(half == 0, 0, EDGE)
    squeeze(out_chip, shape.own * SENT_ROWS, corner_tiles(shape, side, core), shift)
    squeeze(in_chip, shape.own * SENT_ROWS, corner_tiles(shape, side, 1 - core), shift)


def side_tiles(shape, edge):
    return [
        edge.at[k, pl.ds(row, TILE), :] for k in range(FIELDS) for row in range(0, shape.rows, TILE)
    ]


def corner_parts():
    return [(k, part) for k in range(FIELDS) for part in (0, SENT[k] - TILE)]


def corner_tiles(shape, edge, last):
    return [
        edge.at[k, pl.ds(part + last * (shape.rows - SENT[k]), TILE), :]
        for k, part in corner_parts()
    ]


def squeeze(out, base, tiles, shift):
    slot = lanes_of() // EDGE
    for first in range(0, len(tiles), SLOTS):
        value = jnp.zeros((TILE, LANES), jnp.float32)
        for number, tile in enumerate(tiles[first : first + SLOTS]):
            moved = pltpu.roll(tile[...], lax.rem(EDGE * number + shift, LANES), 1)
            value = jnp.where(slot == number, moved, value)
        out[pl.ds(base + first, TILE), :] = value


def spread(source, base, number, half):
    lane = lanes_of()
    tile = source[pl.ds(base + number // SLOTS * TILE, TILE), :]
    amount = LANES - EDGE * (number % SLOTS) - jnp.where(half == 0, 0, EDGE)
    moved = pltpu.roll(tile, lax.rem(amount + LANES, LANES), 1)
    wanted = jnp.where(half == 0, lane, LANES - 1 - lane) < EDGE
    return jnp.where(wanted, moved, 0.0)


def head_kernel(shape, ranges, heads, side, head, columns):
    along = lax.axis_index("along")
    half = lax.axis_index("cross")
    lane = lanes_of()
    line = lax.broadcasted_iota(jnp.int32, (TILE, LANES), 0)
    for c in range(shape.chunks):
        if c < shape.own:
            index = half * (shape.own * LANES) + c * LANES + lane
        else:
            index = jnp.where(half == 0, shape.own * LANES, (shape.own - 1) * LANES) + lane
        for s in range(SHIPS):
            inside = jnp.logical_and(index >= ranges[2, s], index < ranges[3, s])
            columns[s, c] = jnp.where(inside, gravity * heads[s], 0.0)

    def head_rows(row):
        global_row = along * shape.rows + (row - shape.first) + line
        covered = [
            jnp.logical_and(global_row >= ranges[0, s], global_row < ranges[1, s])
            for s in range(SHIPS)
        ]
        for c in range(shape.chunks):
            value = jnp.zeros((TILE, LANES), jnp.float32)
            for s in range(SHIPS):
                value = value + jnp.where(covered[s], columns[s, c], 0.0)
            store(head, 0, c, row, value)

    sweep([(GUARD, shape.total // TILE - 2)], head_rows)


def place(refs, head, c, row, values):
    moved, static, surface, krylov, vel, potential, thick = refs
    for k in range(4):
        store(vel, k, c, row, values[k])
    depth = values[6]
    inside = depth > 0.0
    ship = jnp.where(inside, load(head, 0, c, row), 0.0)
    store(surface, 0, c, row, values[4])
    store(potential, 0, c, row, gravity * values[4] + ship)
    store(thick, 0, c, row, depth)
    store(static, CONDUCT, c, row, values[5] * depth)
    store(static, HALF_RATE, c, row, 0.5 / jnp.where(inside, depth, 1.0))
    store(static, HEAD, c, row, ship)


def diagonal_rows(shape, static, thick, row):
    sides = {}

    def make(c):
        sums = load(static, CONDUCT, c, row - 1) + load(static, CONDUCT, c, row + 1)
        sides[c] = sums
        return load(static, CONDUCT, c, row) + corner_weight * sums

    ring = Ring(make, shape.chunks, lanes_of())
    for c in range(shape.chunks):
        around = ring.before(c, 1) + ring.after(c, 1) + sides[c]
        depth = load(thick, 0, c, row)
        diagonal = (
            0.5 * (around + 5.0 * load(static, CONDUCT, c, row))
            + storage * depth
            + load(static, HALF_RATE, c, row)
        )
        store(static, DIAGONAL, c, row, diagonal)
        store(static, INVERSE, c, row, jnp.where(depth > 0.0, 1.0 / diagonal, 0.0))
        ring.done(c)


def inner_kernel(shape, own, side, head, *refs):
    refs, partial = refs[:7], refs[7]
    moved, static, surface, krylov, vel, potential, thick = refs

    def own_rows(row):
        at = row - shape.first
        for c in range(shape.chunks):
            if c < shape.own:
                values = [load(own, k, c, at) for k in range(FIELDS)]
            else:
                values = [side[k, pl.ds(at, TILE), :] for k in range(FIELDS)]
            place(refs, head, c, row, values)

    sweep([(shape.first, shape.rows // TILE)], own_rows)
    middle = [(shape.first + 4, shape.rows // TILE - 1)]
    sweep(middle, functools.partial(diagonal_rows, shape, static, thick))
    spans = [middle] * 4 + [[(shape.first + 8, shape.rows // TILE - 2)]]
    sums = project(shape, vel, potential, static, moved, krylov, spans, no_moments())
    for number, value in enumerate(sums):
        partial[number] = value


def halo_kernel(shape, from_chip, received, head, partial, *refs):
    refs = refs[7:]
    out, narrow = refs[7:]
    refs = refs[:7]
    moved, static, surface, krylov, vel, potential, thick = refs
    along = lax.axis_index("along")
    half = lax.axis_index("cross")
    for number, (k, part) in enumerate(corner_parts()):
        to = pl.ds(OFFSETS[k] + part, TILE)
        narrow[to, :] = spread(received, shape.own * SENT_ROWS, number, half)
    deepest = SENT[0]
    last = lax.axis_size("along") - 1

    def work(below):
        keep = (last - along if below else along) > 0
        for start in (0, deepest - TILE) if below else (-deepest, -TILE):
            for c in range(shape.chunks):
                source, skip = (received, c * SENT_ROWS) if c < shape.own else (narrow, 0)
                values = []
                for k in range(FIELDS):
                    at = skip + OFFSETS[k] + start + (0 if below else SENT[k])
                    values.append(jnp.where(keep, source[pl.ds(at, TILE), :], 0.0))
                place(refs, head, c, shape.first + start + (shape.rows if below else 0), values)

        def rows(halo):
            return [
                (shape.first + shape.rows + halo - 2 * TILE if below else shape.first - halo, 2)
            ]

        sweep(rows(11), functools.partial(diagonal_rows, shape, static, thick))
        spans = [rows(halo) for halo in (11, 10, 9, 8)]
        spans += [[(shape.first + shape.rows - TILE if below else shape.first, 1)]]
        sums = [partial[number] for number in range(2 * ITERS)]
        sums = project(shape, vel, potential, static, moved, krylov, spans, sums)
        if from_chip:
            put_moments(out, sums)
        else:
            for number, value in enumerate(sums):
                out[number] = value

    core = lax.rem(along, 2)
    for which in range(2):

        @pl.when(core == which)
        def _(which=which):
            work((which == 1) == from_chip)


def coefficients(shares):
    total = jnp.sum(shares[...], axis=0)
    mu = [jnp.broadcast_to(total[:, k : k + 1], (TILE, LANES)) for k in range(2 * ITERS)]

    def norm(c):
        return sum(c[i] * c[j] * mu[i + j] for i in range(len(c)) for j in range(len(c)))

    def energy(c):
        return sum(
            c[i] * c[j] * (mu[i + j] - mu[i + j + 1]) for i in range(len(c)) for j in range(len(c))
        )

    floor = 2e-7 * mu[0]
    one = jnp.ones((TILE, LANES), jnp.float32)
    z = [one]
    search = [one]
    result = [jnp.zeros((TILE, LANES), jnp.float32)] * ITERS
    norm_now = mu[0]
    for iteration in range(ITERS):
        step = norm_now / energy(search)
        if iteration:
            step = jnp.where(norm_now > floor, step, 0.0)
        for i, c in enumerate(search):
            result[i] = result[i] + step * c
        if iteration + 1 < ITERS:
            applied = [
                (search[i] if i < len(search) else 0.0) - (search[i - 1] if i else 0.0)
                for i in range(len(search) + 1)
            ]
            z = [(z[i] if i < len(z) else 0.0) - step * applied[i] for i in range(len(applied))]
            norm_next = norm(z)
            ratio = norm_next / norm_now
            if iteration:
                ratio = jnp.where(norm_now > floor, ratio, 0.0)
            search = [z[i] + (ratio * search[i] if i < len(search) else 0.0) for i in range(len(z))]
            norm_now = norm_next
    return result


def pressure_rows(shape, factors, krylov, pressure, row):
    for c in range(shape.chunks):
        for layer in range(2):
            value = factors[0] * load(krylov, layer, c, row)
            value = value + factors[1] * load(krylov, 2 + layer, c, row)
            value = value + factors[2] * load(krylov, 4 + layer, c, row)
            store(pressure, layer, c, row, value)


def along_moved(moved, pressure, layer, c, row):
    return load(moved, layer, c, row) - (0.5 * time_step) * (
        load(pressure, layer, c, row + 1) - load(pressure, layer, c, row - 1)
    )


def move_rows(shape, moved, pressure, static, flux, put, row):
    lane = lanes_of()
    rings = [
        Ring(lambda c, k=k: load(pressure, k, c, row), shape.chunks, lane) for k in range(2)
    ]
    for c in range(shape.chunks):
        conduct = load(static, CONDUCT, c, row)
        wet = conduct > 0.0
        along = [along_moved(moved, pressure, layer, c, row) for layer in range(2)]
        cross = [
            load(moved, 2 + layer, c, row)
            - (0.5 * time_step) * (rings[layer].after(c, 1) - rings[layer].before(c, 1))
            for layer in range(2)
        ]
        for part, value in enumerate(along + cross):
            put(part, c, row, jnp.where(wet, value, 0.0))
        store(flux, 0, c, row, conduct * (along[0] + along[1]))
        store(flux, 1, c, row, conduct * (cross[0] + cross[1]))
        for ring in rings:
            ring.done(c)


def surface_rows(shape, surface, flux, chunks, put, row):
    ring = Ring(lambda c: load(flux, 1, c, row), shape.chunks, lanes_of())
    for c in range(chunks):
        value = load(surface, 0, c, row) - (0.5 * time_step) * (
            load(flux, 0, c, row + 1)
            - load(flux, 0, c, row - 1)
            + (ring.after(c, 1) - ring.before(c, 1))
        )
        put(c, row, value)
        ring.done(c)


def second_kernel(
    shape, shares, moved_in, static, surface_in, krylov_in,
    moved, surface, krylov, moments,
    vel, potential, pressure, flux,
):
    factors = coefficients(shares)
    start = GUARD
    sweep([(start + 8, 6)], functools.partial(pressure_rows, shape, factors, krylov_in, pressure))
    put_vel = functools.partial(store, vel)
    sweep(
        [(start + 9, 6)],
        functools.partial(move_rows, shape, moved_in, pressure, static, flux, put_vel),
    )

    def put(c, row, value):
        value = jnp.where(load(static, INVERSE, c, row) > 0.0, value, 0.0)
        store(surface, 0, c, row, value)
        store(potential, 0, c, row, gravity * value + load(static, HEAD, c, row))

    sweep(
        [(start + 10, 6)],
        functools.partial(surface_rows, shape, surface_in, flux, shape.chunks, put),
    )
    spans = [[(start + 11, 6)], [(start + 12, 5)], [(start + 13, 5)], [(start + 14, 5)]]
    spans += [[(shape.first, shape.rows // TILE)]]
    put_moments(
        moments, project(shape, vel, potential, static, moved, krylov, spans, no_moments())
    )


def last_kernel(
    shape, shares, moved, static, surface, krylov,
    new_vel, new_surface, new_pressure,
    pressure, flux,
):
    factors = coefficients(shares)
    start = shape.first
    sweep([(start - 2, 5)], functools.partial(pressure_rows, shape, factors, krylov, pressure))

    def put_vel(part, c, row, value):
        if c < shape.own:
            at = pl.multiple_of(row - start, TILE)
            new_vel[part, pl.ds(at, TILE), pl.ds(c * LANES, LANES)] = value
            if part < 2:
                new_pressure[part, pl.ds(at, TILE), pl.ds(c * LANES, LANES)] = load(
                    pressure, part, c, row
                )

    sweep(
        [(start, shape.rows // TILE)],
        functools.partial(move_rows, shape, moved, pressure, static, flux, put_vel),
    )
    for row in (start - 1, start + shape.rows):
        for c in range(shape.own):
            one = slice(row, row + 1)
            total = jnp.zeros((1, LANES), jnp.float32)
            for layer in range(2):
                total = total + (
                    moved[layer, c, one, :]
                    - (0.5 * time_step)
                    * (
                        pressure[layer, c, row + 1 : row + 2, :]
                        - pressure[layer, c, row - 1 : row, :]
                    )
                )
            flux[0, c, one, :] = static[CONDUCT, c, one, :] * total

    def put(c, row, value):
        at = pl.multiple_of(row - start, TILE)
        new_surface[pl.ds(at, TILE), pl.ds(c * LANES, LANES)] = value

    sweep(
        [(start, shape.rows // TILE)],
        functools.partial(surface_rows, shape, surface, flux, shape.own, put),
    )


def cost(flops):
    return pl.CostEstimate(flops=flops, bytes_accessed=flops, transcendentals=0)


def call(kernel, shape, kinds, outs, scratch, operands, estimate=None, aliases={}):
    return pl.pallas_call(
        functools.partial(kernel, shape),
        out_shape=outs,
        in_specs=[pl.BlockSpec(memory_space=kind) for kind in kinds],
        out_specs=[pl.BlockSpec(memory_space=pltpu.VMEM)] * len(outs),
        scratch_shapes=scratch,
        cost_estimate=estimate,
        input_output_aliases=aliases,
        compiler_params=pltpu.CompilerParams(vmem_limit_bytes=VMEM_BYTES),
    )(*operands)


def held(*arrays):
    return tuple(pltpu.with_memory_space_constraint(x, pltpu.VMEM) for x in arrays)


def shared(moments):
    return lax.all_to_all(moments, ("along", "cross"), 0, 0, tiled=True)


def shards(velocity, surface, wet_mask, bathy_class, depth_table, hull_ranges, hull_pressure):
    shape = Shape(*surface.shape)
    vmem, smem = pltpu.VMEM, pltpu.SMEM
    f32, i32 = jnp.float32, jnp.int32
    size = lax.axis_size("along")
    field = (shape.chunks, shape.total, LANES)
    fields = lambda count: vmem((count,) + field, f32)
    sums = jax.ShapeDtypeStruct((2 * size, 1, 8), f32)
    block = surface.shape
    wide = vmem((shape.own * SENT_ROWS + CORNER_ROWS, LANES), f32)
    full = vmem((FIELDS, shape.rows, LANES), f32)
    corner = vmem((SENT_ROWS, LANES), f32)
    tiles = FIELDS * shape.rows // TILE
    table = [smem(depth_table.shape, f32)]
    arrived = [pltpu.SemaphoreType.DMA((5,))]
    near = (shape.rows, LANES)
    inputs = tuple(
        pltpu.with_memory_space_constraint(x, pltpu.HBM)
        for x in (velocity, surface, wet_mask, bathy_class, depth_table)
    )
    (side,) = call(
        edge_kernel, shape, [pl.ANY] * 5,
        [vmem((-(-tiles // SLOTS) * TILE, LANES), f32)],
        [vmem((4,) + near, f32), vmem(near, f32), vmem(near, i32), vmem(near, i32)]
        + table + [full] + arrived,
        inputs,
        cost(10**5),
    )
    far = lax.ppermute(side, "cross", [(0, 1), (1, 0)])
    own, out_chip, in_chip = call(
        pack_kernel, shape, [pl.ANY] * 5,
        [vmem((FIELDS, shape.own, shape.rows, LANES), f32), wide, wide],
        [vmem(velocity.shape, f32), vmem(block, f32), vmem(block, i32), vmem(block, i32)]
        + table + arrived,
        inputs,
        cost(4 * 10**6),
    )
    out_chip, in_chip, side = call(
        corner_kernel, shape, [vmem] * 3, [wide, wide, full], [], held(far, out_chip, in_chip),
        cost(10**5), {1: 0, 2: 1},
    )
    firsts = [i for i in range(1, size, 2)]
    trades = lambda pairs: pairs + [(j, i) for i, j in pairs]
    ends = [(0, 1), (2 * size - 2, 2 * size - 1)]
    next_chip = [(2 * i + j, 2 * i + 2 + j) for i in firsts[:-1] for j in range(2)]
    from_out = lax.ppermute(out_chip, ("along", "cross"), trades(next_chip + ends))
    from_in = lax.ppermute(in_chip, "along", trades([(i - 1, i) for i in firsts]))
    (head,) = call(
        head_kernel, shape, [smem] * 2 + [vmem], [fields(1)],
        [vmem((SHIPS, shape.chunks, TILE, LANES), f32)],
        (hull_ranges.T, hull_pressure) + held(side),
        cost(2 * 10**6),
    )
    state = [fields(count) for count in (4, 5, 1, 6, 4, 1, 1)]
    partials = vmem((2 * ITERS, TILE, LANES), f32)
    *inner, partial = call(
        inner_kernel, shape, [vmem] * 3, state + [partials], [],
        held(own, side, head),
        cost(10**7),
    )
    aliases = {3 + number: number for number in range(7)}
    near_kernel, next_kernel = (
        functools.partial(lambda chip, shape, *refs: halo_kernel(shape, chip, *refs), chip)
        for chip in (False, True)
    )
    *inner, partial = call(
        near_kernel, shape, [vmem] * 10, state + [partials], [corner],
        held(from_in, head, partial, *inner),
        cost(5 * 10**6), aliases,
    )
    moved, static, level, krylov, _, _, _, moments = call(
        next_kernel, shape, [vmem] * 10, state + [sums], [corner],
        held(from_out, head, partial, *inner),
        cost(5 * 10**6), aliases,
    )
    moved, level, krylov, moments = call(
        second_kernel, shape, [vmem] * 5,
        [fields(4), fields(1), fields(6), sums],
        [fields(4), fields(1), fields(2), fields(2)],
        (shared(moments),) + held(moved, static, level, krylov),
    )
    whole = lambda like: jax.ShapeDtypeStruct(like, f32)
    return tuple(
        call(
            last_kernel, shape, [vmem] * 5,
            [whole(velocity.shape), whole(surface.shape), whole((2,) + surface.shape)],
            [fields(2), fields(2)],
            (shared(moments),) + held(moved, static, level, krylov),
        )
    )


def solution(mesh):
    cell = P("along", "cross")
    layered = P(None, "along", "cross")
    in_specs = (layered, cell, cell, cell, P(), P(), P())
    return jax.shard_map(
        shards, mesh=mesh, in_specs=in_specs, out_specs=(layered, cell, layered), check_vma=False
    )
```

```python
import functools

import jax
import jax.numpy as jnp
from jax import lax
from jax.experimental import pallas as pl
from jax.experimental.pallas import tpu as pltpu
from jax.sharding import PartitionSpec as P

ITERS = 3
CLASSES = 16
SHIPS = 8

gravity = 9.81
time_step = 0.1
storage = 0.1
corner_weight = 0.25

LANES = 128
TILE = 8
GUARD = 8
HALO = 16
FIELDS = 7
SENT = (13, 13, 13, 13, 12, 11, 11)
OFFSETS = (0, 13, 26, 39, 52, 64, 75)
SENT_ROWS = 88
CORNER_ROWS = 16
EDGE = 16
SLOTS = LANES // EDGE
VMEM_BYTES = 24 * 1024 * 1024


class Shape:
    def __init__(self, rows, cols):
        self.rows = rows
        self.own = cols // LANES
        self.chunks = self.own + 1
        self.first = GUARD + HALO
        self.total = rows + 2 * (GUARD + HALO)


class Ring:
    def __init__(self, make, chunks, lane):
        self.make = make
        self.chunks = chunks
        self.lane = lane
        self.held = {}

    def at(self, chunk):
        entry = self.held.setdefault(chunk, {})
        if 0 not in entry:
            entry[0] = self.make(chunk)
        return entry[0]

    def rolled(self, chunk, amount):
        value = self.at(chunk)
        entry = self.held[chunk]
        if amount not in entry:
            entry[amount] = pltpu.roll(value, amount, 1)
        return entry[amount]

    def before(self, chunk, step):
        other = (chunk - 1) % self.chunks
        return jnp.where(self.lane < step, self.rolled(other, step), self.rolled(chunk, step))

    def after(self, chunk, step):
        other = (chunk + 1) % self.chunks
        amount = LANES - step
        return jnp.where(self.lane >= amount, self.rolled(other, amount), self.rolled(chunk, amount))

    def done(self, chunk):
        if chunk > 1:
            self.held.pop(chunk - 1, None)


def lanes_of():
    return lax.broadcasted_iota(jnp.int32, (TILE, LANES), 1)


def sweep(spans, body, carry=None):
    for first, tiles in spans:

        def turn(number, carry, first=first):
            row = first + number * TILE
            if carry is None:
                body(row)
                return None
            return body(row, carry)

        carry = lax.fori_loop(0, tiles, turn, carry)
    return carry


def load(ref, index, chunk, row):
    return ref[index, chunk, pl.ds(row, TILE), :]


def store(ref, index, chunk, row, value):
    ref[index, chunk, pl.ds(row, TILE), :] = value


CONDUCT, HALF_RATE, INVERSE, HEAD, DIAGONAL, PRIOR, NEXT = range(7)
STATICS = 7


def predict_rows(shape, vel, head_pressure, static, moved, row):
    lane = lanes_of()
    rings = [
        Ring(lambda c, k=k: load(vel, k, c, row), shape.chunks, lane) for k in range(4)
    ]
    potential = Ring(lambda c: load(head_pressure, 0, c, row), shape.chunks, lane)
    for c in range(shape.chunks):
        wet = load(static, CONDUCT, c, row) > 0.0
        rate = time_step * load(static, HALF_RATE, c, row)
        slope_a = (0.5 * time_step) * (
            load(head_pressure, 0, c, row + 1) - load(head_pressure, 0, c, row - 1)
        )
        slope_c = (0.5 * time_step) * (potential.after(c, 1) - potential.before(c, 1))
        for layer in range(2):
            along = rings[layer].at(c)
            cross = rings[2 + layer].at(c)
            up_a = (0.5 * time_step) * jnp.maximum(along, 0.0)
            dn_a = (0.5 * time_step) * jnp.minimum(along, 0.0)
            up_c = (0.5 * time_step) * jnp.maximum(cross, 0.0)
            dn_c = (0.5 * time_step) * jnp.minimum(cross, 0.0)
            centre = (
                0.8 - 3.0 * ((up_a - dn_a) + (up_c - dn_c)) - (rate if layer == 0 else 2.0 * rate)
            )
            back_a = 0.05 + 4.0 * up_a
            fore_a = 0.05 - 4.0 * dn_a
            back_c = 0.05 + 4.0 * up_c
            fore_c = 0.05 - 4.0 * dn_c
            for part, slope in ((layer, slope_a), (2 + layer, slope_c)):
                ring = rings[part]
                other = rings[part + 1 - 2 * layer].at(c)
                value = centre * ring.at(c) + rate * other - slope
                value = value + (
                    back_a * load(vel, part, c, row - 1) - up_a * load(vel, part, c, row - 2)
                )
                value = value + (
                    fore_a * load(vel, part, c, row + 1) + dn_a * load(vel, part, c, row + 2)
                )
                value = value + (back_c * ring.before(c, 1) - up_c * ring.before(c, 2))
                value = value + (fore_c * ring.after(c, 1) + dn_c * ring.after(c, 2))
                store(moved, part, c, row, jnp.where(wet, value, 0.0))
        for ring in rings:
            ring.done(c)
        potential.done(c)


def source_rows(shape, moved, static, krylov, row):
    lane = lanes_of()
    rings = [
        Ring(
            lambda c, k=k: load(static, CONDUCT, c, row) * load(moved, 2 + k, c, row),
            shape.chunks,
            lane,
        )
        for k in range(2)
    ]
    for c in range(shape.chunks):
        above = load(static, CONDUCT, c, row - 1)
        below = load(static, CONDUCT, c, row + 1)
        scale = (-0.5 / time_step) * load(static, INVERSE, c, row)
        for layer in range(2):
            flow = (
                below * load(moved, layer, c, row + 1)
                - above * load(moved, layer, c, row - 1)
                + (rings[layer].after(c, 1) - rings[layer].before(c, 1))
            )
            store(krylov, layer, c, row, scale * flow)
            rings[layer].done(c)


def link_rows(shape, krylov, static, level, row, own_only):
    lane = lanes_of()
    held = {}

    def terms(layer, c):
        if c not in held:
            conduct = [load(static, CONDUCT, c, row + d) for d in (-1, 0, 1)]
            prior, following = load(static, PRIOR, c, row), load(static, NEXT, c, row)
            held[c] = []
            for k in range(2):
                y = [load(krylov, 2 * level + k, c, row + d) for d in (-1, 0, 1)]
                sums = y[0] + y[2]
                flows = conduct[0] * y[0] + conduct[2] * y[2]
                middle = y[1] + corner_weight * sums
                scaled = conduct[1] * y[1] + corner_weight * flows
                held[c].append(
                    (
                        y[1],
                        conduct[1] * sums + flows,
                        following * middle + scaled,
                        prior * middle + scaled,
                    )
                )
        return held[c][layer]

    rings = [
        [Ring(lambda c, k=k, side=side: terms(k, c)[side], shape.chunks, lane) for side in (2, 3)]
        for k in range(2)
    ]
    for c in range(shape.own if own_only else shape.chunks):
        rate = load(static, HALF_RATE, c, row)
        results = []
        for layer in range(2):
            left, right = rings[layer]
            total = terms(layer, c)[1] + (left.before(c, 1) + right.after(c, 1))
            results.append(0.5 * total + rate * terms(1 - layer, c)[0])
        yield c, [terms(layer, c)[0] for layer in range(2)], results
        for ring in rings[0] + rings[1]:
            ring.done(c)
        if c > 1:
            held.pop(c - 1)


def krylov_rows(shape, krylov, static, level, row):
    for c, _, results in link_rows(shape, krylov, static, level, row, False):
        inverse = load(static, INVERSE, c, row)
        for layer in range(2):
            store(krylov, 2 * level + 2 + layer, c, row, inverse * results[layer])


def moments_of(shape, krylov, static, span, sums):
    def turn(row, sums):
        sums = list(sums)
        for c, top, results in link_rows(shape, krylov, static, 2, row, True):
            diagonal = load(static, DIAGONAL, c, row)
            for layer in range(2):
                low = load(krylov, layer, c, row)
                mid = load(krylov, 2 + layer, c, row)
                low_d, mid_d, top_d = diagonal * low, diagonal * mid, diagonal * top[layer]
                terms = (
                    low * low_d,
                    low * mid_d,
                    mid * mid_d,
                    mid * top_d,
                    top[layer] * top_d,
                    top[layer] * results[layer],
                )
                sums = [a + b for a, b in zip(sums, terms)]
        return tuple(sums)

    return sweep(span, turn, tuple(sums))


def no_moments():
    return (jnp.zeros((TILE, LANES), jnp.float32),) * (2 * ITERS)


def put_moments(out, sums):
    lane = lanes_of()
    result = jnp.zeros((TILE, LANES), jnp.float32)
    for number, part in enumerate(sums):
        result = jnp.where(lane == number, jnp.sum(part), result)
    out[...] = jnp.broadcast_to(result[0:1, None, 0 : out.shape[2]], out.shape)


def project(shape, vel, potential, static, moved, krylov, spans, sums):
    sweep(spans[0], functools.partial(predict_rows, shape, vel, potential, static, moved))
    sweep(spans[1], functools.partial(source_rows, shape, moved, static, krylov))
    for level in range(2):
        sweep(spans[2 + level], functools.partial(krylov_rows, shape, krylov, static, level))
    return moments_of(shape, krylov, static, spans[4], sums)


def fetch(pairs, arrived):
    copies = [
        pltpu.make_async_copy(source, target, arrived.at[number])
        for number, (source, target) in enumerate(pairs)
    ]
    for copy in copies:
        copy.start()
    for copy in copies:
        copy.wait()


def cell_values(vel, surface, wet, bathy, table, rows, cols):
    flag = wet[rows, cols]
    entry = bathy[rows, cols]
    thick = jnp.zeros((TILE, LANES), jnp.float32)
    for choice in range(CLASSES):
        thick = jnp.where(entry == choice, 0.5 * table[choice], thick)
    values = [jnp.where(flag > 0, vel[k, rows, cols], 0.0) for k in range(4)]
    return values + [surface[rows, cols], flag.astype(jnp.float32), thick]


def edge_kernel(
    shape, vel_in, surface_in, wet_in, bathy_in, table_in, side,
    vel, surface, wet, bathy, table, edge, arrived,
):
    half = lax.axis_index("cross")
    first = jnp.where(half == 0, (shape.own - 1) * LANES, 0)
    near = pl.ds(pl.multiple_of(first, LANES), LANES)
    fetch(
        (
            (table_in, table),
            (bathy_in.at[:, near], bathy),
            (wet_in.at[:, near], wet),
            (surface_in.at[:, near], surface),
            (vel_in.at[:, :, near], vel),
        ),
        arrived,
    )
    for t in range(shape.rows // TILE):
        rows = pl.ds(t * TILE, TILE)
        values = cell_values(vel, surface, wet, bathy, table, rows, pl.ds(0, LANES))
        for k, value in enumerate(values):
            edge[k, rows, :] = value
    squeeze(side, 0, side_tiles(shape, edge), jnp.where(half == 0, EDGE, 0))


def pack_kernel(
    shape, vel_in, surface_in, wet_in, bathy_in, table_in,
    own, out_chip, in_chip,
    vel, surface, wet, bathy, table, arrived,
):
    fetch(
        (
            (table_in, table),
            (bathy_in, bathy),
            (wet_in, wet),
            (surface_in, surface),
            (vel_in, vel),
        ),
        arrived,
    )

    def turn(number, carry):
        rows = pl.ds(pl.multiple_of(number * TILE, TILE), TILE)
        for c in range(shape.own):
            cols = pl.ds(c * LANES, LANES)
            values = cell_values(vel, surface, wet, bathy, table, rows, cols)
            for k, value in enumerate(values):
                own[k, c, rows, :] = value
        return carry

    lax.fori_loop(0, shape.rows // TILE, turn, 0)
    core = lax.rem(lax.axis_index("along"), 2)
    for c in range(shape.own):
        for k in range(FIELDS):
            for part in (0, SENT[k] - TILE):
                to = pl.ds(c * SENT_ROWS + OFFSETS[k] + part, TILE)
                last = shape.rows - SENT[k]
                out_chip[to, :] = own[k, c, pl.ds(part + core * last, TILE), :]
                in_chip[to, :] = own[k, c, pl.ds(part + (1 - core) * last, TILE), :]


def corner_kernel(shape, far, out_in, in_in, out_chip, in_chip, side):
    half = lax.axis_index("cross")
    core = lax.rem(lax.axis_index("along"), 2)
    for number, tile in enumerate(side_tiles(shape, side)):
        tile[...] = spread(far, 0, number, half)
    shift = jnp.where(half == 0, 0, EDGE)
    squeeze(out_chip, shape.own * SENT_ROWS, corner_tiles(shape, side, core), shift)
    squeeze(in_chip, shape.own * SENT_ROWS, corner_tiles(shape, side, 1 - core), shift)


def side_tiles(shape, edge):
    return [
        edge.at[k, pl.ds(row, TILE), :] for k in range(FIELDS) for row in range(0, shape.rows, TILE)
    ]


def corner_parts():
    return [(k, part) for k in range(FIELDS) for part in (0, SENT[k] - TILE)]


def corner_tiles(shape, edge, last):
    return [
        edge.at[k, pl.ds(part + last * (shape.rows - SENT[k]), TILE), :]
        for k, part in corner_parts()
    ]


def squeeze(out, base, tiles, shift):
    slot = lanes_of() // EDGE
    for first in range(0, len(tiles), SLOTS):
        value = jnp.zeros((TILE, LANES), jnp.float32)
        for number, tile in enumerate(tiles[first : first + SLOTS]):
            moved = pltpu.roll(tile[...], lax.rem(EDGE * number + shift, LANES), 1)
            value = jnp.where(slot == number, moved, value)
        out[pl.ds(base + first, TILE), :] = value


def spread(source, base, number, half):
    lane = lanes_of()
    tile = source[pl.ds(base + number // SLOTS * TILE, TILE), :]
    amount = LANES - EDGE * (number % SLOTS) - jnp.where(half == 0, 0, EDGE)
    moved = pltpu.roll(tile, lax.rem(amount + LANES, LANES), 1)
    wanted = jnp.where(half == 0, lane, LANES - 1 - lane) < EDGE
    return jnp.where(wanted, moved, 0.0)


def head_kernel(shape, ranges, heads, side, head, columns):
    along = lax.axis_index("along")
    half = lax.axis_index("cross")
    lane = lanes_of()
    line = lax.broadcasted_iota(jnp.int32, (TILE, LANES), 0)
    for c in range(shape.chunks):
        if c < shape.own:
            index = half * (shape.own * LANES) + c * LANES + lane
        else:
            index = jnp.where(half == 0, shape.own * LANES, (shape.own - 1) * LANES) + lane
        for s in range(SHIPS):
            inside = jnp.logical_and(index >= ranges[2, s], index < ranges[3, s])
            columns[s, c] = jnp.where(inside, gravity * heads[s], 0.0)

    def head_rows(row):
        global_row = along * shape.rows + (row - shape.first) + line
        covered = [
            jnp.logical_and(global_row >= ranges[0, s], global_row < ranges[1, s])
            for s in range(SHIPS)
        ]
        for c in range(shape.chunks):
            value = jnp.zeros((TILE, LANES), jnp.float32)
            for s in range(SHIPS):
                value = value + jnp.where(covered[s], columns[s, c], 0.0)
            store(head, 0, c, row, value)

    sweep([(GUARD, shape.total // TILE - 2)], head_rows)


def place(refs, head, c, row, values):
    moved, static, surface, krylov, vel, potential, thick = refs
    for k in range(4):
        store(vel, k, c, row, values[k])
    depth = values[6]
    inside = depth > 0.0
    ship = jnp.where(inside, load(head, 0, c, row), 0.0)
    store(surface, 0, c, row, values[4])
    store(potential, 0, c, row, gravity * values[4] + ship)
    store(thick, 0, c, row, depth)
    store(static, CONDUCT, c, row, values[5] * depth)
    store(static, HALF_RATE, c, row, 0.5 / jnp.where(inside, depth, 1.0))
    store(static, HEAD, c, row, ship)


def diagonal_rows(shape, static, thick, row):
    sides = {}

    def make(c):
        sums = load(static, CONDUCT, c, row - 1) + load(static, CONDUCT, c, row + 1)
        sides[c] = sums
        return load(static, CONDUCT, c, row) + corner_weight * sums

    ring = Ring(make, shape.chunks, lanes_of())
    plain = Ring(lambda c: load(static, CONDUCT, c, row), shape.chunks, lanes_of())
    for c in range(shape.chunks):
        store(static, PRIOR, c, row, plain.before(c, 1))
        store(static, NEXT, c, row, plain.after(c, 1))
        plain.done(c)
        around = ring.before(c, 1) + ring.after(c, 1) + sides[c]
        depth = load(thick, 0, c, row)
        diagonal = (
            0.5 * (around + 5.0 * load(static, CONDUCT, c, row))
            + storage * depth
            + load(static, HALF_RATE, c, row)
        )
        store(static, DIAGONAL, c, row, diagonal)
        store(static, INVERSE, c, row, jnp.where(depth > 0.0, 1.0 / diagonal, 0.0))
        ring.done(c)


def inner_kernel(shape, own, side, head, *refs):
    refs, partial = refs[:7], refs[7]
    moved, static, surface, krylov, vel, potential, thick = refs

    def own_rows(row):
        at = row - shape.first
        for c in range(shape.chunks):
            if c < shape.own:
                values = [load(own, k, c, at) for k in range(FIELDS)]
            else:
                values = [side[k, pl.ds(at, TILE), :] for k in range(FIELDS)]
            place(refs, head, c, row, values)

    sweep([(shape.first, shape.rows // TILE)], own_rows)
    middle = [(shape.first + 4, shape.rows // TILE - 1)]
    sweep(middle, functools.partial(diagonal_rows, shape, static, thick))
    spans = [middle] * 4 + [[(shape.first + 8, shape.rows // TILE - 2)]]
    sums = project(shape, vel, potential, static, moved, krylov, spans, no_moments())
    for number, value in enumerate(sums):
        partial[number] = value


def halo_kernel(shape, from_chip, received, head, partial, *refs):
    refs = refs[7:]
    out, narrow = refs[7:]
    refs = refs[:7]
    moved, static, surface, krylov, vel, potential, thick = refs
    along = lax.axis_index("along")
    half = lax.axis_index("cross")
    for number, (k, part) in enumerate(corner_parts()):
        to = pl.ds(OFFSETS[k] + part, TILE)
        narrow[to, :] = spread(received, shape.own * SENT_ROWS, number, half)
    deepest = SENT[0]
    last = lax.axis_size("along") - 1

    def work(below):
        keep = (last - along if below else along) > 0
        for start in (0, deepest - TILE) if below else (-deepest, -TILE):
            for c in range(shape.chunks):
                source, skip = (received, c * SENT_ROWS) if c < shape.own else (narrow, 0)
                values = []
                for k in range(FIELDS):
                    at = skip + OFFSETS[k] + start + (0 if below else SENT[k])
                    values.append(jnp.where(keep, source[pl.ds(at, TILE), :], 0.0))
                place(refs, head, c, shape.first + start + (shape.rows if below else 0), values)

        def rows(halo):
            return [
                (shape.first + shape.rows + halo - 2 * TILE if below else shape.first - halo, 2)
            ]

        sweep(rows(11), functools.partial(diagonal_rows, shape, static, thick))
        spans = [rows(halo) for halo in (11, 10, 9, 8)]
        spans += [[(shape.first + shape.rows - TILE if below else shape.first, 1)]]
        sums = [partial[number] for number in range(2 * ITERS)]
        sums = project(shape, vel, potential, static, moved, krylov, spans, sums)
        if from_chip:
            put_moments(out, sums)
        else:
            for number, value in enumerate(sums):
                out[number] = value

    core = lax.rem(along, 2)
    for which in range(2):

        @pl.when(core == which)
        def _(which=which):
            work((which == 1) == from_chip)


def coefficients(shares):
    total = jnp.sum(shares[...], axis=0)
    mu = [jnp.broadcast_to(total[:, k : k + 1], (TILE, LANES)) for k in range(2 * ITERS)]

    def norm(c):
        return sum(c[i] * c[j] * mu[i + j] for i in range(len(c)) for j in range(len(c)))

    def energy(c):
        return sum(
            c[i] * c[j] * (mu[i + j] - mu[i + j + 1]) for i in range(len(c)) for j in range(len(c))
        )

    floor = 2e-7 * mu[0]
    one = jnp.ones((TILE, LANES), jnp.float32)
    z = [one]
    search = [one]
    result = [jnp.zeros((TILE, LANES), jnp.float32)] * ITERS
    norm_now = mu[0]
    for iteration in range(ITERS):
        step = norm_now / energy(search)
        if iteration:
            step = jnp.where(norm_now > floor, step, 0.0)
        for i, c in enumerate(search):
            result[i] = result[i] + step * c
        if iteration + 1 < ITERS:
            applied = [
                (search[i] if i < len(search) else 0.0) - (search[i - 1] if i else 0.0)
                for i in range(len(search) + 1)
            ]
            z = [(z[i] if i < len(z) else 0.0) - step * applied[i] for i in range(len(applied))]
            norm_next = norm(z)
            ratio = norm_next / norm_now
            if iteration:
                ratio = jnp.where(norm_now > floor, ratio, 0.0)
            search = [z[i] + (ratio * search[i] if i < len(search) else 0.0) for i in range(len(z))]
            norm_now = norm_next
    return result


def pressure_rows(shape, factors, krylov, pressure, row):
    for c in range(shape.chunks):
        for layer in range(2):
            value = factors[0] * load(krylov, layer, c, row)
            value = value + factors[1] * load(krylov, 2 + layer, c, row)
            value = value + factors[2] * load(krylov, 4 + layer, c, row)
            store(pressure, layer, c, row, value)


def along_moved(moved, pressure, layer, c, row):
    return load(moved, layer, c, row) - (0.5 * time_step) * (
        load(pressure, layer, c, row + 1) - load(pressure, layer, c, row - 1)
    )


def move_rows(shape, moved, pressure, static, flux, put, row):
    lane = lanes_of()
    rings = [
        Ring(lambda c, k=k: load(pressure, k, c, row), shape.chunks, lane) for k in range(2)
    ]
    for c in range(shape.chunks):
        conduct = load(static, CONDUCT, c, row)
        wet = conduct > 0.0
        along = [along_moved(moved, pressure, layer, c, row) for layer in range(2)]
        cross = [
            load(moved, 2 + layer, c, row)
            - (0.5 * time_step) * (rings[layer].after(c, 1) - rings[layer].before(c, 1))
            for layer in range(2)
        ]
        for part, value in enumerate(along + cross):
            put(part, c, row, jnp.where(wet, value, 0.0))
        store(flux, 0, c, row, conduct * (along[0] + along[1]))
        store(flux, 1, c, row, conduct * (cross[0] + cross[1]))
        for ring in rings:
            ring.done(c)


def surface_rows(shape, surface, flux, chunks, put, row):
    ring = Ring(lambda c: load(flux, 1, c, row), shape.chunks, lanes_of())
    for c in range(chunks):
        value = load(surface, 0, c, row) - (0.5 * time_step) * (
            load(flux, 0, c, row + 1)
            - load(flux, 0, c, row - 1)
            + (ring.after(c, 1) - ring.before(c, 1))
        )
        put(c, row, value)
        ring.done(c)


def second_kernel(
    shape, shares, moved_in, static, surface_in, krylov_in,
    moved, surface, krylov, moments,
    vel, potential, pressure, flux,
):
    factors = coefficients(shares)
    start = GUARD
    sweep([(start + 8, 6)], functools.partial(pressure_rows, shape, factors, krylov_in, pressure))
    put_vel = functools.partial(store, vel)
    sweep(
        [(start + 9, 6)],
        functools.partial(move_rows, shape, moved_in, pressure, static, flux, put_vel),
    )

    def put(c, row, value):
        value = jnp.where(load(static, INVERSE, c, row) > 0.0, value, 0.0)
        store(surface, 0, c, row, value)
        store(potential, 0, c, row, gravity * value + load(static, HEAD, c, row))

    sweep(
        [(start + 10, 6)],
        functools.partial(surface_rows, shape, surface_in, flux, shape.chunks, put),
    )
    spans = [[(start + 11, 6)], [(start + 12, 5)], [(start + 13, 5)], [(start + 14, 5)]]
    spans += [[(shape.first, shape.rows // TILE)]]
    put_moments(
        moments, project(shape, vel, potential, static, moved, krylov, spans, no_moments())
    )


def last_kernel(
    shape, shares, moved, static, surface, krylov,
    new_vel, new_surface, new_pressure,
    pressure, flux,
):
    factors = coefficients(shares)
    start = shape.first
    sweep([(start - 2, 5)], functools.partial(pressure_rows, shape, factors, krylov, pressure))

    def put_vel(part, c, row, value):
        if c < shape.own:
            at = pl.multiple_of(row - start, TILE)
            new_vel[part, pl.ds(at, TILE), pl.ds(c * LANES, LANES)] = value
            if part < 2:
                new_pressure[part, pl.ds(at, TILE), pl.ds(c * LANES, LANES)] = load(
                    pressure, part, c, row
                )

    sweep(
        [(start, shape.rows // TILE)],
        functools.partial(move_rows, shape, moved, pressure, static, flux, put_vel),
    )
    for row in (start - 1, start + shape.rows):
        for c in range(shape.own):
            one = slice(row, row + 1)
            total = jnp.zeros((1, LANES), jnp.float32)
            for layer in range(2):
                total = total + (
                    moved[layer, c, one, :]
                    - (0.5 * time_step)
                    * (
                        pressure[layer, c, row + 1 : row + 2, :]
                        - pressure[layer, c, row - 1 : row, :]
                    )
                )
            flux[0, c, one, :] = static[CONDUCT, c, one, :] * total

    def put(c, row, value):
        at = pl.multiple_of(row - start, TILE)
        new_surface[pl.ds(at, TILE), pl.ds(c * LANES, LANES)] = value

    sweep(
        [(start, shape.rows // TILE)],
        functools.partial(surface_rows, shape, surface, flux, shape.own, put),
    )


def cost(flops):
    return pl.CostEstimate(flops=flops, bytes_accessed=flops, transcendentals=0)


def call(kernel, shape, kinds, outs, scratch, operands, estimate=None, aliases={}):
    return pl.pallas_call(
        functools.partial(kernel, shape),
        out_shape=outs,
        in_specs=[pl.BlockSpec(memory_space=kind) for kind in kinds],
        out_specs=[pl.BlockSpec(memory_space=pltpu.VMEM)] * len(outs),
        scratch_shapes=scratch,
        cost_estimate=estimate,
        input_output_aliases=aliases,
        compiler_params=pltpu.CompilerParams(vmem_limit_bytes=VMEM_BYTES),
    )(*operands)


def held(*arrays):
    return tuple(pltpu.with_memory_space_constraint(x, pltpu.VMEM) for x in arrays)


def shared(moments):
    return lax.all_to_all(moments, ("along", "cross"), 0, 0, tiled=True)


def shards(velocity, surface, wet_mask, bathy_class, depth_table, hull_ranges, hull_pressure):
    shape = Shape(*surface.shape)
    vmem, smem = pltpu.VMEM, pltpu.SMEM
    f32, i32 = jnp.float32, jnp.int32
    size = lax.axis_size("along")
    field = (shape.chunks, shape.total, LANES)
    fields = lambda count: vmem((count,) + field, f32)
    sums = jax.ShapeDtypeStruct((2 * size, 1, 8), f32)
    block = surface.shape
    wide = vmem((shape.own * SENT_ROWS + CORNER_ROWS, LANES), f32)
    full = vmem((FIELDS, shape.rows, LANES), f32)
    corner = vmem((SENT_ROWS, LANES), f32)
    tiles = FIELDS * shape.rows // TILE
    table = [smem(depth_table.shape, f32)]
    arrived = [pltpu.SemaphoreType.DMA((5,))]
    near = (shape.rows, LANES)
    inputs = tuple(
        pltpu.with_memory_space_constraint(x, pltpu.HBM)
        for x in (velocity, surface, wet_mask, bathy_class, depth_table)
    )
    (side,) = call(
        edge_kernel, shape, [pl.ANY] * 5,
        [vmem((-(-tiles // SLOTS) * TILE, LANES), f32)],
        [vmem((4,) + near, f32), vmem(near, f32), vmem(near, i32), vmem(near, i32)]
        + table + [full] + arrived,
        inputs,
        cost(10**5),
    )
    far = lax.ppermute(side, "cross", [(0, 1), (1, 0)])
    own, out_chip, in_chip = call(
        pack_kernel, shape, [pl.ANY] * 5,
        [vmem((FIELDS, shape.own, shape.rows, LANES), f32), wide, wide],
        [vmem(velocity.shape, f32), vmem(block, f32), vmem(block, i32), vmem(block, i32)]
        + table + arrived,
        inputs,
        cost(4 * 10**6),
    )
    out_chip, in_chip, side = call(
        corner_kernel, shape, [vmem] * 3, [wide, wide, full], [], held(far, out_chip, in_chip),
        cost(10**5), {1: 0, 2: 1},
    )
    firsts = [i for i in range(1, size, 2)]
    trades = lambda pairs: pairs + [(j, i) for i, j in pairs]
    ends = [(0, 1), (2 * size - 2, 2 * size - 1)]
    next_chip = [(2 * i + j, 2 * i + 2 + j) for i in firsts[:-1] for j in range(2)]
    from_out = lax.ppermute(out_chip, ("along", "cross"), trades(next_chip + ends))
    from_in = lax.ppermute(in_chip, "along", trades([(i - 1, i) for i in firsts]))
    (head,) = call(
        head_kernel, shape, [smem] * 2 + [vmem], [fields(1)],
        [vmem((SHIPS, shape.chunks, TILE, LANES), f32)],
        (hull_ranges.T, hull_pressure) + held(side),
        cost(2 * 10**6),
    )
    state = [fields(count) for count in (4, STATICS, 1, 6, 4, 1, 1)]
    partials = vmem((2 * ITERS, TILE, LANES), f32)
    *inner, partial = call(
        inner_kernel, shape, [vmem] * 3, state + [partials], [],
        held(own, side, head),
        cost(10**7),
    )
    aliases = {3 + number: number for number in range(7)}
    near_kernel, next_kernel = (
        functools.partial(lambda chip, shape, *refs: halo_kernel(shape, chip, *refs), chip)
        for chip in (False, True)
    )
    *inner, partial = call(
        near_kernel, shape, [vmem] * 10, state + [partials], [corner],
        held(from_in, head, partial, *inner),
        cost(5 * 10**6), aliases,
    )
    moved, static, level, krylov, _, _, _, moments = call(
        next_kernel, shape, [vmem] * 10, state + [sums], [corner],
        held(from_out, head, partial, *inner),
        cost(5 * 10**6), aliases,
    )
    moved, level, krylov, moments = call(
        second_kernel, shape, [vmem] * 5,
        [fields(4), fields(1), fields(6), sums],
        [fields(4), fields(1), fields(2), fields(2)],
        (shared(moments),) + held(moved, static, level, krylov),
    )
    whole = lambda like: jax.ShapeDtypeStruct(like, f32)
    return tuple(
        call(
            last_kernel, shape, [vmem] * 5,
            [whole(velocity.shape), whole(surface.shape), whole((2,) + surface.shape)],
            [fields(2), fields(2)],
            (shared(moments),) + held(moved, static, level, krylov),
        )
    )


def solution(mesh):
    cell = P("along", "cross")
    layered = P(None, "along", "cross")
    in_specs = (layered, cell, cell, cell, P(), P(), P())
    return jax.shard_map(
        shards, mesh=mesh, in_specs=in_specs, out_specs=(layered, cell, layered), check_vma=False
    )
```

```python
import functools

import jax
import jax.numpy as jnp
from jax import lax
from jax.experimental import pallas as pl
from jax.experimental.pallas import tpu as pltpu
from jax.sharding import PartitionSpec as P

ITERS = 3
CLASSES = 16
SHIPS = 8

gravity = 9.81
time_step = 0.1
storage = 0.1
corner_weight = 0.25

LANES = 128
TILE = 8
GUARD = 8
HALO = 16
FIELDS = 7
SENT = (13, 13, 13, 13, 12, 11, 11)
OFFSETS = (0, 13, 26, 39, 52, 64, 75)
SENT_ROWS = 88
CORNER_ROWS = 16
EDGE = 16
SLOTS = LANES // EDGE
VMEM_BYTES = 24 * 1024 * 1024


class Shape:
    def __init__(self, rows, cols):
        self.rows = rows
        self.own = cols // LANES
        self.chunks = self.own + 1
        self.first = GUARD + HALO
        self.total = rows + 2 * (GUARD + HALO)


class Ring:
    def __init__(self, make, chunks, lane):
        self.make = make
        self.chunks = chunks
        self.lane = lane
        self.held = {}

    def at(self, chunk):
        entry = self.held.setdefault(chunk, {})
        if 0 not in entry:
            entry[0] = self.make(chunk)
        return entry[0]

    def rolled(self, chunk, amount):
        value = self.at(chunk)
        entry = self.held[chunk]
        if amount not in entry:
            entry[amount] = pltpu.roll(value, amount, 1)
        return entry[amount]

    def before(self, chunk, step):
        other = (chunk - 1) % self.chunks
        return jnp.where(self.lane < step, self.rolled(other, step), self.rolled(chunk, step))

    def after(self, chunk, step):
        other = (chunk + 1) % self.chunks
        amount = LANES - step
        return jnp.where(self.lane >= amount, self.rolled(other, amount), self.rolled(chunk, amount))

    def done(self, chunk):
        if chunk > 1:
            self.held.pop(chunk - 1, None)


def lanes_of():
    return lax.broadcasted_iota(jnp.int32, (TILE, LANES), 1)


def sweep(spans, body, carry=None):
    for first, tiles in spans:

        def turn(number, carry, first=first):
            row = first + number * TILE
            if carry is None:
                body(row)
                return None
            return body(row, carry)

        carry = lax.fori_loop(0, tiles, turn, carry)
    return carry


def load(ref, index, chunk, row):
    return ref[index, chunk, pl.ds(row, TILE), :]


def store(ref, index, chunk, row, value):
    ref[index, chunk, pl.ds(row, TILE), :] = value


CONDUCT, HALF_RATE, INVERSE, HEAD, DIAGONAL, PRIOR, NEXT = range(7)
STATICS = 7


def predict_rows(shape, vel, head_pressure, static, moved, row):
    lane = lanes_of()
    rings = [
        Ring(lambda c, k=k: load(vel, k, c, row), shape.chunks, lane) for k in range(4)
    ]
    potential = Ring(lambda c: load(head_pressure, 0, c, row), shape.chunks, lane)
    for c in range(shape.chunks):
        wet = load(static, CONDUCT, c, row) > 0.0
        rate = time_step * load(static, HALF_RATE, c, row)
        slope_a = (0.5 * time_step) * (
            load(head_pressure, 0, c, row + 1) - load(head_pressure, 0, c, row - 1)
        )
        slope_c = (0.5 * time_step) * (potential.after(c, 1) - potential.before(c, 1))
        for layer in range(2):
            along = rings[layer].at(c)
            cross = rings[2 + layer].at(c)
            up_a = (0.5 * time_step) * jnp.maximum(along, 0.0)
            dn_a = (0.5 * time_step) * jnp.minimum(along, 0.0)
            up_c = (0.5 * time_step) * jnp.maximum(cross, 0.0)
            dn_c = (0.5 * time_step) * jnp.minimum(cross, 0.0)
            centre = (
                0.8 - 3.0 * ((up_a - dn_a) + (up_c - dn_c)) - (rate if layer == 0 else 2.0 * rate)
            )
            back_a = 0.05 + 4.0 * up_a
            fore_a = 0.05 - 4.0 * dn_a
            back_c = 0.05 + 4.0 * up_c
            fore_c = 0.05 - 4.0 * dn_c
            for part, slope in ((layer, slope_a), (2 + layer, slope_c)):
                ring = rings[part]
                other = rings[part + 1 - 2 * layer].at(c)
                value = centre * ring.at(c) + rate * other - slope
                value = value + (
                    back_a * load(vel, part, c, row - 1) - up_a * load(vel, part, c, row - 2)
                )
                value = value + (
                    fore_a * load(vel, part, c, row + 1) + dn_a * load(vel, part, c, row + 2)
                )
                value = value + (back_c * ring.before(c, 1) - up_c * ring.before(c, 2))
                value = value + (fore_c * ring.after(c, 1) + dn_c * ring.after(c, 2))
                store(moved, part, c, row, jnp.where(wet, value, 0.0))
        for ring in rings:
            ring.done(c)
        potential.done(c)


def source_rows(shape, moved, static, krylov, row):
    lane = lanes_of()
    rings = [
        Ring(
            lambda c, k=k: load(static, CONDUCT, c, row) * load(moved, 2 + k, c, row),
            shape.chunks,
            lane,
        )
        for k in range(2)
    ]
    for c in range(shape.chunks):
        above = load(static, CONDUCT, c, row - 1)
        below = load(static, CONDUCT, c, row + 1)
        scale = (-0.5 / time_step) * load(static, INVERSE, c, row)
        for layer in range(2):
            flow = (
                below * load(moved, layer, c, row + 1)
                - above * load(moved, layer, c, row - 1)
                + (rings[layer].after(c, 1) - rings[layer].before(c, 1))
            )
            store(krylov, layer, c, row, scale * flow)
            rings[layer].done(c)


def link_rows(shape, krylov, static, level, row, own_only):
    lane = lanes_of()
    held = {}

    def terms(layer, c):
        if c not in held:
            conduct = [load(static, CONDUCT, c, row + d) for d in (-1, 0, 1)]
            prior, following = load(static, PRIOR, c, row), load(static, NEXT, c, row)
            held[c] = []
            for k in range(2):
                y = [load(krylov, 2 * level + k, c, row + d) for d in (-1, 0, 1)]
                sums = y[0] + y[2]
                flows = conduct[0] * y[0] + conduct[2] * y[2]
                middle = y[1] + corner_weight * sums
                scaled = conduct[1] * y[1] + corner_weight * flows
                held[c].append(
                    (
                        y[1],
                        conduct[1] * sums + flows,
                        following * middle + scaled,
                        prior * middle + scaled,
                    )
                )
        return held[c][layer]

    rings = [
        [Ring(lambda c, k=k, side=side: terms(k, c)[side], shape.chunks, lane) for side in (2, 3)]
        for k in range(2)
    ]
    for c in range(shape.own if own_only else shape.chunks):
        rate = load(static, HALF_RATE, c, row)
        results = []
        for layer in range(2):
            left, right = rings[layer]
            total = terms(layer, c)[1] + (left.before(c, 1) + right.after(c, 1))
            results.append(0.5 * total + rate * terms(1 - layer, c)[0])
        yield c, [terms(layer, c)[0] for layer in range(2)], results
        for ring in rings[0] + rings[1]:
            ring.done(c)
        if c > 1:
            held.pop(c - 1)


def krylov_rows(shape, krylov, static, level, row):
    for c, _, results in link_rows(shape, krylov, static, level, row, False):
        inverse = load(static, INVERSE, c, row)
        for layer in range(2):
            store(krylov, 2 * level + 2 + layer, c, row, inverse * results[layer])


def moments_of(shape, krylov, static, span, sums):
    def turn(row, sums):
        sums = list(sums)
        for c, top, results in link_rows(shape, krylov, static, 2, row, True):
            diagonal = load(static, DIAGONAL, c, row)
            for layer in range(2):
                low = load(krylov, layer, c, row)
                mid = load(krylov, 2 + layer, c, row)
                low_d, mid_d, top_d = diagonal * low, diagonal * mid, diagonal * top[layer]
                terms = (
                    low * low_d,
                    low * mid_d,
                    mid * mid_d,
                    mid * top_d,
                    top[layer] * top_d,
                    top[layer] * results[layer],
                )
                sums = [a + b for a, b in zip(sums, terms)]
        return tuple(sums)

    return sweep(span, turn, tuple(sums))


def no_moments():
    return (jnp.zeros((TILE, LANES), jnp.float32),) * (2 * ITERS)


def put_moments(out, sums):
    lane = lanes_of()
    result = jnp.zeros((TILE, LANES), jnp.float32)
    for number, part in enumerate(sums):
        result = jnp.where(lane == number, jnp.sum(part), result)
    out[...] = jnp.broadcast_to(result[0:1, None, 0 : out.shape[2]], out.shape)


def project(shape, vel, potential, static, moved, krylov, spans, sums):
    sweep(spans[0], functools.partial(predict_rows, shape, vel, potential, static, moved))
    sweep(spans[1], functools.partial(source_rows, shape, moved, static, krylov))
    for level in range(2):
        sweep(spans[2 + level], functools.partial(krylov_rows, shape, krylov, static, level))
    return moments_of(shape, krylov, static, spans[4], sums)


def fetch(pairs, arrived):
    copies = [
        pltpu.make_async_copy(source, target, arrived.at[number])
        for number, (source, target) in enumerate(pairs)
    ]
    for copy in copies:
        copy.start()
    for copy in copies:
        copy.wait()


def cell_values(vel, surface, wet, bathy, table, rows, cols):
    flag = wet[rows, cols]
    entry = bathy[rows, cols]
    thick = jnp.zeros((TILE, LANES), jnp.float32)
    for choice in range(CLASSES):
        thick = jnp.where(entry == choice, 0.5 * table[choice], thick)
    values = [jnp.where(flag > 0, vel[k, rows, cols], 0.0) for k in range(4)]
    return values + [surface[rows, cols], flag.astype(jnp.float32), thick]


def edge_kernel(
    shape, vel_in, surface_in, wet_in, bathy_in, table_in, side,
    vel, surface, wet, bathy, table, edge, arrived,
):
    half = lax.axis_index("cross")
    first = jnp.where(half == 0, (shape.own - 1) * LANES, 0)
    near = pl.ds(pl.multiple_of(first, LANES), LANES)
    fetch(
        (
            (table_in, table),
            (bathy_in.at[:, near], bathy),
            (wet_in.at[:, near], wet),
            (surface_in.at[:, near], surface),
            (vel_in.at[:, :, near], vel),
        ),
        arrived,
    )
    for t in range(shape.rows // TILE):
        rows = pl.ds(t * TILE, TILE)
        values = cell_values(vel, surface, wet, bathy, table, rows, pl.ds(0, LANES))
        for k, value in enumerate(values):
            edge[k, rows, :] = value
    squeeze(side, 0, side_tiles(shape, edge), jnp.where(half == 0, EDGE, 0))


def pack_kernel(
    shape, vel_in, surface_in, wet_in, bathy_in, table_in,
    own, out_chip, in_chip, in_rest,
    vel, surface, wet, bathy, table, arrived,
):
    fetch(
        (
            (table_in, table),
            (bathy_in, bathy),
            (wet_in, wet),
            (surface_in, surface),
            (vel_in, vel),
        ),
        arrived,
    )

    def turn(number, carry):
        rows = pl.ds(pl.multiple_of(number * TILE, TILE), TILE)
        for c in range(shape.own):
            cols = pl.ds(c * LANES, LANES)
            values = cell_values(vel, surface, wet, bathy, table, rows, cols)
            for k, value in enumerate(values):
                own[k, c, rows, :] = value
        return carry

    lax.fori_loop(0, shape.rows // TILE, turn, 0)
    core = lax.rem(lax.axis_index("along"), 2)
    for c in range(shape.own):
        for k in range(FIELDS):
            for part in (0, SENT[k] - TILE):
                to = pl.ds(c * SENT_ROWS + OFFSETS[k] + part, TILE)
                last = shape.rows - SENT[k]
                out_chip[to, :] = own[k, c, pl.ds(part + core * last, TILE), :]
                target = in_chip if c < shape.own // 2 else in_rest
                to = pl.ds(c % (shape.own // 2) * SENT_ROWS + OFFSETS[k] + part, TILE)
                target[to, :] = own[k, c, pl.ds(part + (1 - core) * last, TILE), :]


def corner_kernel(shape, far, out_in, in_in, out_chip, in_chip, side):
    half = lax.axis_index("cross")
    core = lax.rem(lax.axis_index("along"), 2)
    for number, tile in enumerate(side_tiles(shape, side)):
        tile[...] = spread(far, 0, number, half)
    shift = jnp.where(half == 0, 0, EDGE)
    squeeze(out_chip, shape.own * SENT_ROWS, corner_tiles(shape, side, core), shift)
    squeeze(in_chip, shape.own // 2 * SENT_ROWS, corner_tiles(shape, side, 1 - core), shift)


def side_tiles(shape, edge):
    return [
        edge.at[k, pl.ds(row, TILE), :] for k in range(FIELDS) for row in range(0, shape.rows, TILE)
    ]


def corner_parts():
    return [(k, part) for k in range(FIELDS) for part in (0, SENT[k] - TILE)]


def corner_tiles(shape, edge, last):
    return [
        edge.at[k, pl.ds(part + last * (shape.rows - SENT[k]), TILE), :]
        for k, part in corner_parts()
    ]


def squeeze(out, base, tiles, shift):
    slot = lanes_of() // EDGE
    for first in range(0, len(tiles), SLOTS):
        value = jnp.zeros((TILE, LANES), jnp.float32)
        for number, tile in enumerate(tiles[first : first + SLOTS]):
            moved = pltpu.roll(tile[...], lax.rem(EDGE * number + shift, LANES), 1)
            value = jnp.where(slot == number, moved, value)
        out[pl.ds(base + first, TILE), :] = value


def spread(source, base, number, half):
    lane = lanes_of()
    tile = source[pl.ds(base + number // SLOTS * TILE, TILE), :]
    amount = LANES - EDGE * (number % SLOTS) - jnp.where(half == 0, 0, EDGE)
    moved = pltpu.roll(tile, lax.rem(amount + LANES, LANES), 1)
    wanted = jnp.where(half == 0, lane, LANES - 1 - lane) < EDGE
    return jnp.where(wanted, moved, 0.0)


def head_kernel(shape, ranges, heads, side, head, columns):
    along = lax.axis_index("along")
    half = lax.axis_index("cross")
    lane = lanes_of()
    line = lax.broadcasted_iota(jnp.int32, (TILE, LANES), 0)
    for c in range(shape.chunks):
        if c < shape.own:
            index = half * (shape.own * LANES) + c * LANES + lane
        else:
            index = jnp.where(half == 0, shape.own * LANES, (shape.own - 1) * LANES) + lane
        for s in range(SHIPS):
            inside = jnp.logical_and(index >= ranges[2, s], index < ranges[3, s])
            columns[s, c] = jnp.where(inside, gravity * heads[s], 0.0)

    def head_rows(row):
        global_row = along * shape.rows + (row - shape.first) + line
        covered = [
            jnp.logical_and(global_row >= ranges[0, s], global_row < ranges[1, s])
            for s in range(SHIPS)
        ]
        for c in range(shape.chunks):
            value = jnp.zeros((TILE, LANES), jnp.float32)
            for s in range(SHIPS):
                value = value + jnp.where(covered[s], columns[s, c], 0.0)
            store(head, 0, c, row, value)

    sweep([(GUARD, shape.total // TILE - 2)], head_rows)


def place(refs, head, c, row, values):
    moved, static, surface, krylov, vel, potential, thick = refs
    for k in range(4):
        store(vel, k, c, row, values[k])
    depth = values[6]
    inside = depth > 0.0
    ship = jnp.where(inside, load(head, 0, c, row), 0.0)
    store(surface, 0, c, row, values[4])
    store(potential, 0, c, row, gravity * values[4] + ship)
    store(thick, 0, c, row, depth)
    store(static, CONDUCT, c, row, values[5] * depth)
    store(static, HALF_RATE, c, row, 0.5 / jnp.where(inside, depth, 1.0))
    store(static, HEAD, c, row, ship)


def diagonal_rows(shape, static, thick, row):
    sides = {}

    def make(c):
        sums = load(static, CONDUCT, c, row - 1) + load(static, CONDUCT, c, row + 1)
        sides[c] = sums
        return load(static, CONDUCT, c, row) + corner_weight * sums

    ring = Ring(make, shape.chunks, lanes_of())
    plain = Ring(lambda c: load(static, CONDUCT, c, row), shape.chunks, lanes_of())
    for c in range(shape.chunks):
        store(static, PRIOR, c, row, plain.before(c, 1))
        store(static, NEXT, c, row, plain.after(c, 1))
        plain.done(c)
        around = ring.before(c, 1) + ring.after(c, 1) + sides[c]
        depth = load(thick, 0, c, row)
        diagonal = (
            0.5 * (around + 5.0 * load(static, CONDUCT, c, row))
            + storage * depth
            + load(static, HALF_RATE, c, row)
        )
        store(static, DIAGONAL, c, row, diagonal)
        store(static, INVERSE, c, row, jnp.where(depth > 0.0, 1.0 / diagonal, 0.0))
        ring.done(c)


def inner_kernel(shape, own, side, head, *refs):
    refs, partial = refs[:7], refs[7]
    moved, static, surface, krylov, vel, potential, thick = refs

    def own_rows(row):
        at = row - shape.first
        for c in range(shape.chunks):
            if c < shape.own:
                values = [load(own, k, c, at) for k in range(FIELDS)]
            else:
                values = [side[k, pl.ds(at, TILE), :] for k in range(FIELDS)]
            place(refs, head, c, row, values)

    sweep([(shape.first, shape.rows // TILE)], own_rows)
    middle = [(shape.first + 4, shape.rows // TILE - 1)]
    sweep(middle, functools.partial(diagonal_rows, shape, static, thick))
    spans = [middle] * 4 + [[(shape.first + 8, shape.rows // TILE - 2)]]
    sums = project(shape, vel, potential, static, moved, krylov, spans, no_moments())
    for number, value in enumerate(sums):
        partial[number] = value


def halo_kernel(shape, from_chip, *refs):
    parts = 1 if from_chip else 2
    received = refs[:parts]
    head, partial = refs[parts : parts + 2]
    refs = refs[parts + 9 :]
    out, narrow = refs[7:]
    refs = refs[:7]
    share = shape.own // parts
    moved, static, surface, krylov, vel, potential, thick = refs
    along = lax.axis_index("along")
    half = lax.axis_index("cross")
    for number, (k, part) in enumerate(corner_parts()):
        to = pl.ds(OFFSETS[k] + part, TILE)
        narrow[to, :] = spread(received[-1], share * SENT_ROWS, number, half)
    deepest = SENT[0]
    last = lax.axis_size("along") - 1

    def work(below):
        keep = (last - along if below else along) > 0
        for start in (0, deepest - TILE) if below else (-deepest, -TILE):
            for c in range(shape.chunks):
                source, skip = narrow, 0
                if c < shape.own:
                    source, skip = received[c // share], c % share * SENT_ROWS
                values = []
                for k in range(FIELDS):
                    at = skip + OFFSETS[k] + start + (0 if below else SENT[k])
                    values.append(jnp.where(keep, source[pl.ds(at, TILE), :], 0.0))
                place(refs, head, c, shape.first + start + (shape.rows if below else 0), values)

        def rows(halo):
            return [
                (shape.first + shape.rows + halo - 2 * TILE if below else shape.first - halo, 2)
            ]

        sweep(rows(11), functools.partial(diagonal_rows, shape, static, thick))
        spans = [rows(halo) for halo in (11, 10, 9, 8)]
        spans += [[(shape.first + shape.rows - TILE if below else shape.first, 1)]]
        sums = [partial[number] for number in range(2 * ITERS)]
        sums = project(shape, vel, potential, static, moved, krylov, spans, sums)
        if from_chip:
            put_moments(out, sums)
        else:
            for number, value in enumerate(sums):
                out[number] = value

    core = lax.rem(along, 2)
    for which in range(2):

        @pl.when(core == which)
        def _(which=which):
            work((which == 1) == from_chip)


def coefficients(shares):
    total = jnp.sum(shares[...], axis=0)
    mu = [jnp.broadcast_to(total[:, k : k + 1], (TILE, LANES)) for k in range(2 * ITERS)]

    def norm(c):
        return sum(c[i] * c[j] * mu[i + j] for i in range(len(c)) for j in range(len(c)))

    def energy(c):
        return sum(
            c[i] * c[j] * (mu[i + j] - mu[i + j + 1]) for i in range(len(c)) for j in range(len(c))
        )

    floor = 2e-7 * mu[0]
    one = jnp.ones((TILE, LANES), jnp.float32)
    z = [one]
    search = [one]
    result = [jnp.zeros((TILE, LANES), jnp.float32)] * ITERS
    norm_now = mu[0]
    for iteration in range(ITERS):
        step = norm_now / energy(search)
        if iteration:
            step = jnp.where(norm_now > floor, step, 0.0)
        for i, c in enumerate(search):
            result[i] = result[i] + step * c
        if iteration + 1 < ITERS:
            applied = [
                (search[i] if i < len(search) else 0.0) - (search[i - 1] if i else 0.0)
                for i in range(len(search) + 1)
            ]
            z = [(z[i] if i < len(z) else 0.0) - step * applied[i] for i in range(len(applied))]
            norm_next = norm(z)
            ratio = norm_next / norm_now
            if iteration:
                ratio = jnp.where(norm_now > floor, ratio, 0.0)
            search = [z[i] + (ratio * search[i] if i < len(search) else 0.0) for i in range(len(z))]
            norm_now = norm_next
    return result


def pressure_rows(shape, factors, krylov, pressure, row):
    for c in range(shape.chunks):
        for layer in range(2):
            value = factors[0] * load(krylov, layer, c, row)
            value = value + factors[1] * load(krylov, 2 + layer, c, row)
            value = value + factors[2] * load(krylov, 4 + layer, c, row)
            store(pressure, layer, c, row, value)


def along_moved(moved, pressure, layer, c, row):
    return load(moved, layer, c, row) - (0.5 * time_step) * (
        load(pressure, layer, c, row + 1) - load(pressure, layer, c, row - 1)
    )


def move_rows(shape, moved, pressure, static, flux, put, row):
    lane = lanes_of()
    rings = [
        Ring(lambda c, k=k: load(pressure, k, c, row), shape.chunks, lane) for k in range(2)
    ]
    for c in range(shape.chunks):
        conduct = load(static, CONDUCT, c, row)
        wet = conduct > 0.0
        along = [along_moved(moved, pressure, layer, c, row) for layer in range(2)]
        cross = [
            load(moved, 2 + layer, c, row)
            - (0.5 * time_step) * (rings[layer].after(c, 1) - rings[layer].before(c, 1))
            for layer in range(2)
        ]
        for part, value in enumerate(along + cross):
            put(part, c, row, jnp.where(wet, value, 0.0))
        store(flux, 0, c, row, conduct * (along[0] + along[1]))
        store(flux, 1, c, row, conduct * (cross[0] + cross[1]))
        for ring in rings:
            ring.done(c)


def surface_rows(shape, surface, flux, chunks, put, row):
    ring = Ring(lambda c: load(flux, 1, c, row), shape.chunks, lanes_of())
    for c in range(chunks):
        value = load(surface, 0, c, row) - (0.5 * time_step) * (
            load(flux, 0, c, row + 1)
            - load(flux, 0, c, row - 1)
            + (ring.after(c, 1) - ring.before(c, 1))
        )
        put(c, row, value)
        ring.done(c)


def second_kernel(
    shape, shares, moved_in, static, surface_in, krylov_in,
    moved, surface, krylov, moments,
    vel, potential, pressure, flux,
):
    factors = coefficients(shares)
    start = GUARD
    sweep([(start + 8, 6)], functools.partial(pressure_rows, shape, factors, krylov_in, pressure))
    put_vel = functools.partial(store, vel)
    sweep(
        [(start + 9, 6)],
        functools.partial(move_rows, shape, moved_in, pressure, static, flux, put_vel),
    )

    def put(c, row, value):
        value = jnp.where(load(static, INVERSE, c, row) > 0.0, value, 0.0)
        store(surface, 0, c, row, value)
        store(potential, 0, c, row, gravity * value + load(static, HEAD, c, row))

    sweep(
        [(start + 10, 6)],
        functools.partial(surface_rows, shape, surface_in, flux, shape.chunks, put),
    )
    spans = [[(start + 11, 6)], [(start + 12, 5)], [(start + 13, 5)], [(start + 14, 5)]]
    spans += [[(shape.first, shape.rows // TILE)]]
    put_moments(
        moments, project(shape, vel, potential, static, moved, krylov, spans, no_moments())
    )


def last_kernel(
    shape, shares, moved, static, surface, krylov,
    new_vel, new_surface, new_pressure,
    pressure, flux,
):
    factors = coefficients(shares)
    start = shape.first
    sweep([(start - 2, 5)], functools.partial(pressure_rows, shape, factors, krylov, pressure))

    def put_vel(part, c, row, value):
        if c < shape.own:
            at = pl.multiple_of(row - start, TILE)
            new_vel[part, pl.ds(at, TILE), pl.ds(c * LANES, LANES)] = value
            if part < 2:
                new_pressure[part, pl.ds(at, TILE), pl.ds(c * LANES, LANES)] = load(
                    pressure, part, c, row
                )

    sweep(
        [(start, shape.rows // TILE)],
        functools.partial(move_rows, shape, moved, pressure, static, flux, put_vel),
    )
    for row in (start - 1, start + shape.rows):
        for c in range(shape.own):
            one = slice(row, row + 1)
            total = jnp.zeros((1, LANES), jnp.float32)
            for layer in range(2):
                total = total + (
                    moved[layer, c, one, :]
                    - (0.5 * time_step)
                    * (
                        pressure[layer, c, row + 1 : row + 2, :]
                        - pressure[layer, c, row - 1 : row, :]
                    )
                )
            flux[0, c, one, :] = static[CONDUCT, c, one, :] * total

    def put(c, row, value):
        at = pl.multiple_of(row - start, TILE)
        new_surface[pl.ds(at, TILE), pl.ds(c * LANES, LANES)] = value

    sweep(
        [(start, shape.rows // TILE)],
        functools.partial(surface_rows, shape, surface, flux, shape.own, put),
    )


def cost(flops):
    return pl.CostEstimate(flops=flops, bytes_accessed=flops, transcendentals=0)


def call(kernel, shape, kinds, outs, scratch, operands, estimate=None, aliases={}):
    return pl.pallas_call(
        functools.partial(kernel, shape),
        out_shape=outs,
        in_specs=[pl.BlockSpec(memory_space=kind) for kind in kinds],
        out_specs=[pl.BlockSpec(memory_space=pltpu.VMEM)] * len(outs),
        scratch_shapes=scratch,
        cost_estimate=estimate,
        input_output_aliases=aliases,
        compiler_params=pltpu.CompilerParams(vmem_limit_bytes=VMEM_BYTES),
    )(*operands)


def held(*arrays):
    return tuple(pltpu.with_memory_space_constraint(x, pltpu.VMEM) for x in arrays)


def shared(moments):
    return lax.all_to_all(moments, ("along", "cross"), 0, 0, tiled=True)


def shards(velocity, surface, wet_mask, bathy_class, depth_table, hull_ranges, hull_pressure):
    shape = Shape(*surface.shape)
    vmem, smem = pltpu.VMEM, pltpu.SMEM
    f32, i32 = jnp.float32, jnp.int32
    size = lax.axis_size("along")
    field = (shape.chunks, shape.total, LANES)
    fields = lambda count: vmem((count,) + field, f32)
    sums = jax.ShapeDtypeStruct((2 * size, 1, 8), f32)
    block = surface.shape
    wide = vmem((shape.own * SENT_ROWS + CORNER_ROWS, LANES), f32)
    full = vmem((FIELDS, shape.rows, LANES), f32)
    corner = vmem((SENT_ROWS, LANES), f32)
    tiles = FIELDS * shape.rows // TILE
    table = [smem(depth_table.shape, f32)]
    arrived = [pltpu.SemaphoreType.DMA((5,))]
    near = (shape.rows, LANES)
    inputs = tuple(
        pltpu.with_memory_space_constraint(x, pltpu.HBM)
        for x in (velocity, surface, wet_mask, bathy_class, depth_table)
    )
    (side,) = call(
        edge_kernel, shape, [pl.ANY] * 5,
        [vmem((-(-tiles // SLOTS) * TILE, LANES), f32)],
        [vmem((4,) + near, f32), vmem(near, f32), vmem(near, i32), vmem(near, i32)]
        + table + [full] + arrived,
        inputs,
        cost(10**5),
    )
    far = lax.ppermute(side, "cross", [(0, 1), (1, 0)])
    half_rows = shape.own // 2 * SENT_ROWS
    first_half = vmem((half_rows, LANES), f32)
    second_half = vmem((half_rows + CORNER_ROWS, LANES), f32)
    own, out_chip, in_chip, in_rest = call(
        pack_kernel, shape, [pl.ANY] * 5,
        [vmem((FIELDS, shape.own, shape.rows, LANES), f32), wide, first_half, second_half],
        [vmem(velocity.shape, f32), vmem(block, f32), vmem(block, i32), vmem(block, i32)]
        + table + arrived,
        inputs,
        cost(4 * 10**6),
    )
    out_chip, in_rest, side = call(
        corner_kernel, shape, [vmem] * 3, [wide, second_half, full], [],
        held(far, out_chip, in_rest),
        cost(10**5), {1: 0, 2: 1},
    )
    firsts = [i for i in range(1, size, 2)]
    trades = lambda pairs: pairs + [(j, i) for i, j in pairs]
    ends = [(0, 1), (2 * size - 2, 2 * size - 1)]
    next_chip = [(2 * i + j, 2 * i + 2 + j) for i in firsts[:-1] for j in range(2)]
    from_out = lax.ppermute(out_chip, ("along", "cross"), trades(next_chip + ends))
    same_chip = trades([(i - 1, i) for i in firsts])
    from_in = [lax.ppermute(piece, "along", same_chip) for piece in (in_chip, in_rest)]
    (head,) = call(
        head_kernel, shape, [smem] * 2 + [vmem], [fields(1)],
        [vmem((SHIPS, shape.chunks, TILE, LANES), f32)],
        (hull_ranges.T, hull_pressure) + held(side),
        cost(2 * 10**6),
    )
    state = [fields(count) for count in (4, STATICS, 1, 6, 4, 1, 1)]
    partials = vmem((2 * ITERS, TILE, LANES), f32)
    *inner, partial = call(
        inner_kernel, shape, [vmem] * 3, state + [partials], [],
        held(own, side, head),
        cost(10**7),
    )
    near_kernel, next_kernel = (
        functools.partial(lambda chip, shape, *refs: halo_kernel(shape, chip, *refs), chip)
        for chip in (False, True)
    )
    *inner, partial = call(
        near_kernel, shape, [vmem] * 11, state + [partials], [corner],
        held(*from_in, head, partial, *inner),
        cost(5 * 10**6), {4 + number: number for number in range(7)},
    )
    moved, static, level, krylov, _, _, _, moments = call(
        next_kernel, shape, [vmem] * 10, state + [sums], [corner],
        held(from_out, head, partial, *inner),
        cost(5 * 10**6), {3 + number: number for number in range(7)},
    )
    moved, level, krylov, moments = call(
        second_kernel, shape, [vmem] * 5,
        [fields(4), fields(1), fields(6), sums],
        [fields(4), fields(1), fields(2), fields(2)],
        (shared(moments),) + held(moved, static, level, krylov),
    )
    whole = lambda like: jax.ShapeDtypeStruct(like, f32)
    return tuple(
        call(
            last_kernel, shape, [vmem] * 5,
            [whole(velocity.shape), whole(surface.shape), whole((2,) + surface.shape)],
            [fields(2), fields(2)],
            (shared(moments),) + held(moved, static, level, krylov),
        )
    )


def solution(mesh):
    cell = P("along", "cross")
    layered = P(None, "along", "cross")
    in_specs = (layered, cell, cell, cell, P(), P(), P())
    return jax.shard_map(
        shards, mesh=mesh, in_specs=in_specs, out_specs=(layered, cell, layered), check_vma=False
    )
```

```python
import functools

import jax
import jax.numpy as jnp
from jax import lax
from jax.experimental import pallas as pl
from jax.experimental.pallas import tpu as pltpu
from jax.sharding import PartitionSpec as P

ITERS = 3
CLASSES = 16
SHIPS = 8

gravity = 9.81
time_step = 0.1
storage = 0.1
corner_weight = 0.25

LANES = 128
TILE = 8
GUARD = 8
HALO = 16
FIELDS = 7
SENT = (13, 13, 13, 13, 12, 11, 11)
OFFSETS = (0, 13, 26, 39, 52, 64, 75)
SENT_ROWS = 88
CORNER_ROWS = 16
EDGE = 16
SLOTS = LANES // EDGE
VMEM_BYTES = 24 * 1024 * 1024


class Shape:
    def __init__(self, rows, cols):
        self.rows = rows
        self.own = cols // LANES
        self.chunks = self.own + 1
        self.first = GUARD + HALO
        self.total = rows + 2 * (GUARD + HALO)


class Ring:
    def __init__(self, make, chunks, lane):
        self.make = make
        self.chunks = chunks
        self.lane = lane
        self.held = {}

    def at(self, chunk):
        entry = self.held.setdefault(chunk, {})
        if 0 not in entry:
            entry[0] = self.make(chunk)
        return entry[0]

    def rolled(self, chunk, amount):
        value = self.at(chunk)
        entry = self.held[chunk]
        if amount not in entry:
            entry[amount] = pltpu.roll(value, amount, 1)
        return entry[amount]

    def before(self, chunk, step):
        other = (chunk - 1) % self.chunks
        return jnp.where(self.lane < step, self.rolled(other, step), self.rolled(chunk, step))

    def after(self, chunk, step):
        other = (chunk + 1) % self.chunks
        amount = LANES - step
        return jnp.where(self.lane >= amount, self.rolled(other, amount), self.rolled(chunk, amount))

    def done(self, chunk):
        if chunk > 1:
            self.held.pop(chunk - 1, None)


def lanes_of():
    return lax.broadcasted_iota(jnp.int32, (TILE, LANES), 1)


UNROLL = 4


def sweep(spans, body, carry=None):
    for first, tiles in spans:

        def turn(number, carry, first=first, count=UNROLL, skipped=0):
            for tile in range(count):
                row = first + number * (UNROLL * TILE) + (skipped + tile) * TILE
                if carry is None:
                    body(row)
                else:
                    carry = body(row, carry)
            return carry

        turns = tiles // UNROLL
        if turns == 1:
            carry = turn(0, carry)
        elif turns:
            carry = lax.fori_loop(0, turns, turn, carry)
        if tiles % UNROLL:
            carry = turn(0, carry, count=tiles % UNROLL, skipped=turns * UNROLL)
    return carry


def load(ref, index, chunk, row):
    return ref[index, chunk, pl.ds(row, TILE), :]


def store(ref, index, chunk, row, value):
    ref[index, chunk, pl.ds(row, TILE), :] = value


CONDUCT, HALF_RATE, INVERSE, HEAD, DIAGONAL, PRIOR, NEXT = range(7)
STATICS = 7


def predict_rows(shape, vel, head_pressure, static, moved, row):
    lane = lanes_of()
    rings = [
        Ring(lambda c, k=k: load(vel, k, c, row), shape.chunks, lane) for k in range(4)
    ]
    potential = Ring(lambda c: load(head_pressure, 0, c, row), shape.chunks, lane)
    for c in range(shape.chunks):
        wet = load(static, CONDUCT, c, row) > 0.0
        rate = time_step * load(static, HALF_RATE, c, row)
        slope_a = (0.5 * time_step) * (
            load(head_pressure, 0, c, row + 1) - load(head_pressure, 0, c, row - 1)
        )
        slope_c = (0.5 * time_step) * (potential.after(c, 1) - potential.before(c, 1))
        for layer in range(2):
            along = rings[layer].at(c)
            cross = rings[2 + layer].at(c)
            up_a = (0.5 * time_step) * jnp.maximum(along, 0.0)
            dn_a = (0.5 * time_step) * jnp.minimum(along, 0.0)
            up_c = (0.5 * time_step) * jnp.maximum(cross, 0.0)
            dn_c = (0.5 * time_step) * jnp.minimum(cross, 0.0)
            centre = (
                0.8 - 3.0 * ((up_a - dn_a) + (up_c - dn_c)) - (rate if layer == 0 else 2.0 * rate)
            )
            back_a = 0.05 + 4.0 * up_a
            fore_a = 0.05 - 4.0 * dn_a
            back_c = 0.05 + 4.0 * up_c
            fore_c = 0.05 - 4.0 * dn_c
            for part, slope in ((layer, slope_a), (2 + layer, slope_c)):
                ring = rings[part]
                other = rings[part + 1 - 2 * layer].at(c)
                value = centre * ring.at(c) + rate * other - slope
                value = value + (
                    back_a * load(vel, part, c, row - 1) - up_a * load(vel, part, c, row - 2)
                )
                value = value + (
                    fore_a * load(vel, part, c, row + 1) + dn_a * load(vel, part, c, row + 2)
                )
                value = value + (back_c * ring.before(c, 1) - up_c * ring.before(c, 2))
                value = value + (fore_c * ring.after(c, 1) + dn_c * ring.after(c, 2))
                store(moved, part, c, row, jnp.where(wet, value, 0.0))
        for ring in rings:
            ring.done(c)
        potential.done(c)


def source_rows(shape, moved, static, krylov, row):
    lane = lanes_of()
    rings = [
        Ring(
            lambda c, k=k: load(static, CONDUCT, c, row) * load(moved, 2 + k, c, row),
            shape.chunks,
            lane,
        )
        for k in range(2)
    ]
    for c in range(shape.chunks):
        above = load(static, CONDUCT, c, row - 1)
        below = load(static, CONDUCT, c, row + 1)
        scale = (-0.5 / time_step) * load(static, INVERSE, c, row)
        for layer in range(2):
            flow = (
                below * load(moved, layer, c, row + 1)
                - above * load(moved, layer, c, row - 1)
                + (rings[layer].after(c, 1) - rings[layer].before(c, 1))
            )
            store(krylov, layer, c, row, scale * flow)
            rings[layer].done(c)


def link_rows(shape, krylov, static, level, row, own_only):
    lane = lanes_of()
    held = {}

    def terms(layer, c):
        if c not in held:
            conduct = [load(static, CONDUCT, c, row + d) for d in (-1, 0, 1)]
            prior, following = load(static, PRIOR, c, row), load(static, NEXT, c, row)
            held[c] = []
            for k in range(2):
                y = [load(krylov, 2 * level + k, c, row + d) for d in (-1, 0, 1)]
                sums = y[0] + y[2]
                flows = conduct[0] * y[0] + conduct[2] * y[2]
                middle = y[1] + corner_weight * sums
                scaled = conduct[1] * y[1] + corner_weight * flows
                held[c].append(
                    (
                        y[1],
                        conduct[1] * sums + flows,
                        following * middle + scaled,
                        prior * middle + scaled,
                    )
                )
        return held[c][layer]

    rings = [
        [Ring(lambda c, k=k, side=side: terms(k, c)[side], shape.chunks, lane) for side in (2, 3)]
        for k in range(2)
    ]
    for c in range(shape.own if own_only else shape.chunks):
        rate = load(static, HALF_RATE, c, row)
        results = []
        for layer in range(2):
            left, right = rings[layer]
            total = terms(layer, c)[1] + (left.before(c, 1) + right.after(c, 1))
            results.append(0.5 * total + rate * terms(1 - layer, c)[0])
        yield c, [terms(layer, c)[0] for layer in range(2)], results
        for ring in rings[0] + rings[1]:
            ring.done(c)
        if c > 1:
            held.pop(c - 1)


def krylov_rows(shape, krylov, static, level, row):
    for c, _, results in link_rows(shape, krylov, static, level, row, False):
        inverse = load(static, INVERSE, c, row)
        for layer in range(2):
            store(krylov, 2 * level + 2 + layer, c, row, inverse * results[layer])


def moments_of(shape, krylov, static, span, sums):
    def turn(row, sums):
        sums = list(sums)
        for c, top, results in link_rows(shape, krylov, static, 2, row, True):
            diagonal = load(static, DIAGONAL, c, row)
            for layer in range(2):
                low = load(krylov, layer, c, row)
                mid = load(krylov, 2 + layer, c, row)
                low_d, mid_d, top_d = diagonal * low, diagonal * mid, diagonal * top[layer]
                terms = (
                    low * low_d,
                    low * mid_d,
                    mid * mid_d,
                    mid * top_d,
                    top[layer] * top_d,
                    top[layer] * results[layer],
                )
                sums = [a + b for a, b in zip(sums, terms)]
        return tuple(sums)

    return sweep(span, turn, tuple(sums))


def no_moments():
    return (jnp.zeros((TILE, LANES), jnp.float32),) * (2 * ITERS)


def put_moments(out, sums):
    lane = lanes_of()
    result = jnp.zeros((TILE, LANES), jnp.float32)
    for number, part in enumerate(sums):
        result = jnp.where(lane == number, jnp.sum(part), result)
    out[...] = jnp.broadcast_to(result[0:1, None, 0 : out.shape[2]], out.shape)


def project(shape, vel, potential, static, moved, krylov, spans, sums):
    sweep(spans[0], functools.partial(predict_rows, shape, vel, potential, static, moved))
    sweep(spans[1], functools.partial(source_rows, shape, moved, static, krylov))
    for level in range(2):
        sweep(spans[2 + level], functools.partial(krylov_rows, shape, krylov, static, level))
    return moments_of(shape, krylov, static, spans[4], sums)


def fetch(pairs, arrived):
    copies = [
        pltpu.make_async_copy(source, target, arrived.at[number])
        for number, (source, target) in enumerate(pairs)
    ]
    for copy in copies:
        copy.start()
    for copy in copies:
        copy.wait()


def cell_values(vel, surface, wet, bathy, table, rows, cols):
    flag = wet[rows, cols]
    entry = bathy[rows, cols]
    thick = jnp.zeros((TILE, LANES), jnp.float32)
    for choice in range(CLASSES):
        thick = jnp.where(entry == choice, 0.5 * table[choice], thick)
    values = [jnp.where(flag > 0, vel[k, rows, cols], 0.0) for k in range(4)]
    return values + [surface[rows, cols], flag.astype(jnp.float32), thick]


def edge_kernel(
    shape, vel_in, surface_in, wet_in, bathy_in, table_in, side,
    vel, surface, wet, bathy, table, edge, arrived,
):
    half = lax.axis_index("cross")
    first = jnp.where(half == 0, (shape.own - 1) * LANES, 0)
    near = pl.ds(pl.multiple_of(first, LANES), LANES)
    fetch(
        (
            (table_in, table),
            (bathy_in.at[:, near], bathy),
            (wet_in.at[:, near], wet),
            (surface_in.at[:, near], surface),
            (vel_in.at[:, :, near], vel),
        ),
        arrived,
    )
    for t in range(shape.rows // TILE):
        rows = pl.ds(t * TILE, TILE)
        values = cell_values(vel, surface, wet, bathy, table, rows, pl.ds(0, LANES))
        for k, value in enumerate(values):
            edge[k, rows, :] = value
    squeeze(side, 0, side_tiles(shape, edge), jnp.where(half == 0, EDGE, 0))


def pack_kernel(
    shape, vel_in, surface_in, wet_in, bathy_in, table_in,
    own, out_chip, in_chip, in_rest,
    vel, surface, wet, bathy, table, arrived,
):
    fetch(
        (
            (table_in, table),
            (bathy_in, bathy),
            (wet_in, wet),
            (surface_in, surface),
            (vel_in, vel),
        ),
        arrived,
    )

    def turn(number, carry):
        rows = pl.ds(pl.multiple_of(number * TILE, TILE), TILE)
        for c in range(shape.own):
            cols = pl.ds(c * LANES, LANES)
            values = cell_values(vel, surface, wet, bathy, table, rows, cols)
            for k, value in enumerate(values):
                own[k, c, rows, :] = value
        return carry

    lax.fori_loop(0, shape.rows // TILE, turn, 0)
    core = lax.rem(lax.axis_index("along"), 2)
    for c in range(shape.own):
        for k in range(FIELDS):
            for part in (0, SENT[k] - TILE):
                to = pl.ds(c * SENT_ROWS + OFFSETS[k] + part, TILE)
                last = shape.rows - SENT[k]
                out_chip[to, :] = own[k, c, pl.ds(part + core * last, TILE), :]
                target = in_chip if c < shape.own // 2 else in_rest
                to = pl.ds(c % (shape.own // 2) * SENT_ROWS + OFFSETS[k] + part, TILE)
                target[to, :] = own[k, c, pl.ds(part + (1 - core) * last, TILE), :]


def corner_kernel(shape, far, out_in, in_in, out_chip, in_chip, side):
    half = lax.axis_index("cross")
    core = lax.rem(lax.axis_index("along"), 2)
    for number, tile in enumerate(side_tiles(shape, side)):
        tile[...] = spread(far, 0, number, half)
    shift = jnp.where(half == 0, 0, EDGE)
    squeeze(out_chip, shape.own * SENT_ROWS, corner_tiles(shape, side, core), shift)
    squeeze(in_chip, shape.own // 2 * SENT_ROWS, corner_tiles(shape, side, 1 - core), shift)


def side_tiles(shape, edge):
    return [
        edge.at[k, pl.ds(row, TILE), :] for k in range(FIELDS) for row in range(0, shape.rows, TILE)
    ]


def corner_parts():
    return [(k, part) for k in range(FIELDS) for part in (0, SENT[k] - TILE)]


def corner_tiles(shape, edge, last):
    return [
        edge.at[k, pl.ds(part + last * (shape.rows - SENT[k]), TILE), :]
        for k, part in corner_parts()
    ]


def squeeze(out, base, tiles, shift):
    slot = lanes_of() // EDGE
    for first in range(0, len(tiles), SLOTS):
        value = jnp.zeros((TILE, LANES), jnp.float32)
        for number, tile in enumerate(tiles[first : first + SLOTS]):
            moved = pltpu.roll(tile[...], lax.rem(EDGE * number + shift, LANES), 1)
            value = jnp.where(slot == number, moved, value)
        out[pl.ds(base + first, TILE), :] = value


def spread(source, base, number, half):
    lane = lanes_of()
    tile = source[pl.ds(base + number // SLOTS * TILE, TILE), :]
    amount = LANES - EDGE * (number % SLOTS) - jnp.where(half == 0, 0, EDGE)
    moved = pltpu.roll(tile, lax.rem(amount + LANES, LANES), 1)
    wanted = jnp.where(half == 0, lane, LANES - 1 - lane) < EDGE
    return jnp.where(wanted, moved, 0.0)


def head_kernel(shape, ranges, heads, side, head, columns):
    along = lax.axis_index("along")
    half = lax.axis_index("cross")
    lane = lanes_of()
    line = lax.broadcasted_iota(jnp.int32, (TILE, LANES), 0)
    for c in range(shape.chunks):
        if c < shape.own:
            index = half * (shape.own * LANES) + c * LANES + lane
        else:
            index = jnp.where(half == 0, shape.own * LANES, (shape.own - 1) * LANES) + lane
        for s in range(SHIPS):
            inside = jnp.logical_and(index >= ranges[2, s], index < ranges[3, s])
            columns[s, c] = jnp.where(inside, gravity * heads[s], 0.0)

    def head_rows(row):
        global_row = along * shape.rows + (row - shape.first) + line
        covered = [
            jnp.logical_and(global_row >= ranges[0, s], global_row < ranges[1, s])
            for s in range(SHIPS)
        ]
        for c in range(shape.chunks):
            value = jnp.zeros((TILE, LANES), jnp.float32)
            for s in range(SHIPS):
                value = value + jnp.where(covered[s], columns[s, c], 0.0)
            store(head, 0, c, row, value)

    sweep([(GUARD, shape.total // TILE - 2)], head_rows)


def place(refs, head, c, row, values):
    moved, static, surface, krylov, vel, potential, thick = refs
    for k in range(4):
        store(vel, k, c, row, values[k])
    depth = values[6]
    inside = depth > 0.0
    ship = jnp.where(inside, load(head, 0, c, row), 0.0)
    store(surface, 0, c, row, values[4])
    store(potential, 0, c, row, gravity * values[4] + ship)
    store(thick, 0, c, row, depth)
    store(static, CONDUCT, c, row, values[5] * depth)
    store(static, HALF_RATE, c, row, 0.5 / jnp.where(inside, depth, 1.0))
    store(static, HEAD, c, row, ship)


def diagonal_rows(shape, static, thick, row):
    sides = {}

    def make(c):
        sums = load(static, CONDUCT, c, row - 1) + load(static, CONDUCT, c, row + 1)
        sides[c] = sums
        return load(static, CONDUCT, c, row) + corner_weight * sums

    ring = Ring(make, shape.chunks, lanes_of())
    plain = Ring(lambda c: load(static, CONDUCT, c, row), shape.chunks, lanes_of())
    for c in range(shape.chunks):
        store(static, PRIOR, c, row, plain.before(c, 1))
        store(static, NEXT, c, row, plain.after(c, 1))
        plain.done(c)
        around = ring.before(c, 1) + ring.after(c, 1) + sides[c]
        depth = load(thick, 0, c, row)
        diagonal = (
            0.5 * (around + 5.0 * load(static, CONDUCT, c, row))
            + storage * depth
            + load(static, HALF_RATE, c, row)
        )
        store(static, DIAGONAL, c, row, diagonal)
        store(static, INVERSE, c, row, jnp.where(depth > 0.0, 1.0 / diagonal, 0.0))
        ring.done(c)


def inner_kernel(shape, own, side, head, *refs):
    refs, partial = refs[:7], refs[7]
    moved, static, surface, krylov, vel, potential, thick = refs

    def own_rows(row):
        at = row - shape.first
        for c in range(shape.chunks):
            if c < shape.own:
                values = [load(own, k, c, at) for k in range(FIELDS)]
            else:
                values = [side[k, pl.ds(at, TILE), :] for k in range(FIELDS)]
            place(refs, head, c, row, values)

    sweep([(shape.first, shape.rows // TILE)], own_rows)
    middle = [(shape.first + 4, shape.rows // TILE - 1)]
    sweep(middle, functools.partial(diagonal_rows, shape, static, thick))
    spans = [middle] * 4 + [[(shape.first + 8, shape.rows // TILE - 2)]]
    sums = project(shape, vel, potential, static, moved, krylov, spans, no_moments())
    for number, value in enumerate(sums):
        partial[number] = value


def halo_kernel(shape, from_chip, *refs):
    parts = 1 if from_chip else 2
    received = refs[:parts]
    head, partial = refs[parts : parts + 2]
    refs = refs[parts + 9 :]
    out, narrow = refs[7:]
    refs = refs[:7]
    share = shape.own // parts
    moved, static, surface, krylov, vel, potential, thick = refs
    along = lax.axis_index("along")
    half = lax.axis_index("cross")
    for number, (k, part) in enumerate(corner_parts()):
        to = pl.ds(OFFSETS[k] + part, TILE)
        narrow[to, :] = spread(received[-1], share * SENT_ROWS, number, half)
    deepest = SENT[0]
    last = lax.axis_size("along") - 1

    def work(below):
        keep = (last - along if below else along) > 0
        for start in (0, deepest - TILE) if below else (-deepest, -TILE):
            for c in range(shape.chunks):
                source, skip = narrow, 0
                if c < shape.own:
                    source, skip = received[c // share], c % share * SENT_ROWS
                values = []
                for k in range(FIELDS):
                    at = skip + OFFSETS[k] + start + (0 if below else SENT[k])
                    values.append(jnp.where(keep, source[pl.ds(at, TILE), :], 0.0))
                place(refs, head, c, shape.first + start + (shape.rows if below else 0), values)

        def rows(halo):
            return [
                (shape.first + shape.rows + halo - 2 * TILE if below else shape.first - halo, 2)
            ]

        sweep(rows(11), functools.partial(diagonal_rows, shape, static, thick))
        spans = [rows(halo) for halo in (11, 10, 9, 8)]
        spans += [[(shape.first + shape.rows - TILE if below else shape.first, 1)]]
        sums = [partial[number] for number in range(2 * ITERS)]
        sums = project(shape, vel, potential, static, moved, krylov, spans, sums)
        if from_chip:
            put_moments(out, sums)
        else:
            for number, value in enumerate(sums):
                out[number] = value

    core = lax.rem(along, 2)
    for which in range(2):

        @pl.when(core == which)
        def _(which=which):
            work((which == 1) == from_chip)


def coefficients(shares):
    total = jnp.sum(shares[...], axis=0)
    mu = [jnp.broadcast_to(total[:, k : k + 1], (TILE, LANES)) for k in range(2 * ITERS)]

    def norm(c):
        return sum(c[i] * c[j] * mu[i + j] for i in range(len(c)) for j in range(len(c)))

    def energy(c):
        return sum(
            c[i] * c[j] * (mu[i + j] - mu[i + j + 1]) for i in range(len(c)) for j in range(len(c))
        )

    floor = 2e-7 * mu[0]
    one = jnp.ones((TILE, LANES), jnp.float32)
    z = [one]
    search = [one]
    result = [jnp.zeros((TILE, LANES), jnp.float32)] * ITERS
    norm_now = mu[0]
    for iteration in range(ITERS):
        step = norm_now / energy(search)
        if iteration:
            step = jnp.where(norm_now > floor, step, 0.0)
        for i, c in enumerate(search):
            result[i] = result[i] + step * c
        if iteration + 1 < ITERS:
            applied = [
                (search[i] if i < len(search) else 0.0) - (search[i - 1] if i else 0.0)
                for i in range(len(search) + 1)
            ]
            z = [(z[i] if i < len(z) else 0.0) - step * applied[i] for i in range(len(applied))]
            norm_next = norm(z)
            ratio = norm_next / norm_now
            if iteration:
                ratio = jnp.where(norm_now > floor, ratio, 0.0)
            search = [z[i] + (ratio * search[i] if i < len(search) else 0.0) for i in range(len(z))]
            norm_now = norm_next
    return result


def pressure_rows(shape, factors, krylov, pressure, row):
    for c in range(shape.chunks):
        for layer in range(2):
            value = factors[0] * load(krylov, layer, c, row)
            value = value + factors[1] * load(krylov, 2 + layer, c, row)
            value = value + factors[2] * load(krylov, 4 + layer, c, row)
            store(pressure, layer, c, row, value)


def along_moved(moved, pressure, layer, c, row):
    return load(moved, layer, c, row) - (0.5 * time_step) * (
        load(pressure, layer, c, row + 1) - load(pressure, layer, c, row - 1)
    )


def move_rows(shape, moved, pressure, static, flux, put, row):
    lane = lanes_of()
    rings = [
        Ring(lambda c, k=k: load(pressure, k, c, row), shape.chunks, lane) for k in range(2)
    ]
    for c in range(shape.chunks):
        conduct = load(static, CONDUCT, c, row)
        wet = conduct > 0.0
        along = [along_moved(moved, pressure, layer, c, row) for layer in range(2)]
        cross = [
            load(moved, 2 + layer, c, row)
            - (0.5 * time_step) * (rings[layer].after(c, 1) - rings[layer].before(c, 1))
            for layer in range(2)
        ]
        for part, value in enumerate(along + cross):
            put(part, c, row, jnp.where(wet, value, 0.0))
        store(flux, 0, c, row, conduct * (along[0] + along[1]))
        store(flux, 1, c, row, conduct * (cross[0] + cross[1]))
        for ring in rings:
            ring.done(c)


def surface_rows(shape, surface, flux, chunks, put, row):
    ring = Ring(lambda c: load(flux, 1, c, row), shape.chunks, lanes_of())
    for c in range(chunks):
        value = load(surface, 0, c, row) - (0.5 * time_step) * (
            load(flux, 0, c, row + 1)
            - load(flux, 0, c, row - 1)
            + (ring.after(c, 1) - ring.before(c, 1))
        )
        put(c, row, value)
        ring.done(c)


def second_kernel(
    shape, shares, moved_in, static, surface_in, krylov_in,
    moved, surface, krylov, moments,
    vel, potential, pressure, flux,
):
    factors = coefficients(shares)
    start = GUARD
    sweep([(start + 8, 6)], functools.partial(pressure_rows, shape, factors, krylov_in, pressure))
    put_vel = functools.partial(store, vel)
    sweep(
        [(start + 9, 6)],
        functools.partial(move_rows, shape, moved_in, pressure, static, flux, put_vel),
    )

    def put(c, row, value):
        value = jnp.where(load(static, INVERSE, c, row) > 0.0, value, 0.0)
        store(surface, 0, c, row, value)
        store(potential, 0, c, row, gravity * value + load(static, HEAD, c, row))

    sweep(
        [(start + 10, 6)],
        functools.partial(surface_rows, shape, surface_in, flux, shape.chunks, put),
    )
    spans = [[(start + 11, 6)], [(start + 12, 5)], [(start + 13, 5)], [(start + 14, 5)]]
    spans += [[(shape.first, shape.rows // TILE)]]
    put_moments(
        moments, project(shape, vel, potential, static, moved, krylov, spans, no_moments())
    )


def last_kernel(
    shape, shares, moved, static, surface, krylov,
    new_vel, new_surface, new_pressure,
    pressure, flux,
):
    factors = coefficients(shares)
    start = shape.first
    sweep([(start - 2, 5)], functools.partial(pressure_rows, shape, factors, krylov, pressure))

    def put_vel(part, c, row, value):
        if c < shape.own:
            at = pl.multiple_of(row - start, TILE)
            new_vel[part, pl.ds(at, TILE), pl.ds(c * LANES, LANES)] = value
            if part < 2:
                new_pressure[part, pl.ds(at, TILE), pl.ds(c * LANES, LANES)] = load(
                    pressure, part, c, row
                )

    sweep(
        [(start, shape.rows // TILE)],
        functools.partial(move_rows, shape, moved, pressure, static, flux, put_vel),
    )
    for row in (start - 1, start + shape.rows):
        for c in range(shape.own):
            one = slice(row, row + 1)
            total = jnp.zeros((1, LANES), jnp.float32)
            for layer in range(2):
                total = total + (
                    moved[layer, c, one, :]
                    - (0.5 * time_step)
                    * (
                        pressure[layer, c, row + 1 : row + 2, :]
                        - pressure[layer, c, row - 1 : row, :]
                    )
                )
            flux[0, c, one, :] = static[CONDUCT, c, one, :] * total

    def put(c, row, value):
        at = pl.multiple_of(row - start, TILE)
        new_surface[pl.ds(at, TILE), pl.ds(c * LANES, LANES)] = value

    sweep(
        [(start, shape.rows // TILE)],
        functools.partial(surface_rows, shape, surface, flux, shape.own, put),
    )


def cost(flops):
    return pl.CostEstimate(flops=flops, bytes_accessed=flops, transcendentals=0)


def call(kernel, shape, kinds, outs, scratch, operands, estimate=None, aliases={}):
    return pl.pallas_call(
        functools.partial(kernel, shape),
        out_shape=outs,
        in_specs=[pl.BlockSpec(memory_space=kind) for kind in kinds],
        out_specs=[pl.BlockSpec(memory_space=pltpu.VMEM)] * len(outs),
        scratch_shapes=scratch,
        cost_estimate=estimate,
        input_output_aliases=aliases,
        compiler_params=pltpu.CompilerParams(vmem_limit_bytes=VMEM_BYTES),
    )(*operands)


def held(*arrays):
    return tuple(pltpu.with_memory_space_constraint(x, pltpu.VMEM) for x in arrays)


def shared(moments):
    return lax.all_to_all(moments, ("along", "cross"), 0, 0, tiled=True)


def shards(velocity, surface, wet_mask, bathy_class, depth_table, hull_ranges, hull_pressure):
    shape = Shape(*surface.shape)
    vmem, smem = pltpu.VMEM, pltpu.SMEM
    f32, i32 = jnp.float32, jnp.int32
    size = lax.axis_size("along")
    field = (shape.chunks, shape.total, LANES)
    fields = lambda count: vmem((count,) + field, f32)
    sums = jax.ShapeDtypeStruct((2 * size, 1, 8), f32)
    block = surface.shape
    wide = vmem((shape.own * SENT_ROWS + CORNER_ROWS, LANES), f32)
    full = vmem((FIELDS, shape.rows, LANES), f32)
    corner = vmem((SENT_ROWS, LANES), f32)
    tiles = FIELDS * shape.rows // TILE
    table = [smem(depth_table.shape, f32)]
    arrived = [pltpu.SemaphoreType.DMA((5,))]
    near = (shape.rows, LANES)
    inputs = tuple(
        pltpu.with_memory_space_constraint(x, pltpu.HBM)
        for x in (velocity, surface, wet_mask, bathy_class, depth_table)
    )
    (side,) = call(
        edge_kernel, shape, [pl.ANY] * 5,
        [vmem((-(-tiles // SLOTS) * TILE, LANES), f32)],
        [vmem((4,) + near, f32), vmem(near, f32), vmem(near, i32), vmem(near, i32)]
        + table + [full] + arrived,
        inputs,
        cost(10**5),
    )
    far = lax.ppermute(side, "cross", [(0, 1), (1, 0)])
    half_rows = shape.own // 2 * SENT_ROWS
    first_half = vmem((half_rows, LANES), f32)
    second_half = vmem((half_rows + CORNER_ROWS, LANES), f32)
    own, out_chip, in_chip, in_rest = call(
        pack_kernel, shape, [pl.ANY] * 5,
        [vmem((FIELDS, shape.own, shape.rows, LANES), f32), wide, first_half, second_half],
        [vmem(velocity.shape, f32), vmem(block, f32), vmem(block, i32), vmem(block, i32)]
        + table + arrived,
        inputs,
        cost(4 * 10**6),
    )
    out_chip, in_rest, side = call(
        corner_kernel, shape, [vmem] * 3, [wide, second_half, full], [],
        held(far, out_chip, in_rest),
        cost(10**5), {1: 0, 2: 1},
    )
    firsts = [i for i in range(1, size, 2)]
    trades = lambda pairs: pairs + [(j, i) for i, j in pairs]
    ends = [(0, 1), (2 * size - 2, 2 * size - 1)]
    next_chip = [(2 * i + j, 2 * i + 2 + j) for i in firsts[:-1] for j in range(2)]
    from_out = lax.ppermute(out_chip, ("along", "cross"), trades(next_chip + ends))
    same_chip = trades([(i - 1, i) for i in firsts])
    from_in = [lax.ppermute(piece, "along", same_chip) for piece in (in_chip, in_rest)]
    (head,) = call(
        head_kernel, shape, [smem] * 2 + [vmem], [fields(1)],
        [vmem((SHIPS, shape.chunks, TILE, LANES), f32)],
        (hull_ranges.T, hull_pressure) + held(side),
        cost(2 * 10**6),
    )
    state = [fields(count) for count in (4, STATICS, 1, 6, 4, 1, 1)]
    partials = vmem((2 * ITERS, TILE, LANES), f32)
    *inner, partial = call(
        inner_kernel, shape, [vmem] * 3, state + [partials], [],
        held(own, side, head),
        cost(10**7),
    )
    near_kernel, next_kernel = (
        functools.partial(lambda chip, shape, *refs: halo_kernel(shape, chip, *refs), chip)
        for chip in (False, True)
    )
    *inner, partial = call(
        near_kernel, shape, [vmem] * 11, state + [partials], [corner],
        held(*from_in, head, partial, *inner),
        cost(5 * 10**6), {4 + number: number for number in range(7)},
    )
    moved, static, level, krylov, _, _, _, moments = call(
        next_kernel, shape, [vmem] * 10, state + [sums], [corner],
        held(from_out, head, partial, *inner),
        cost(5 * 10**6), {3 + number: number for number in range(7)},
    )
    moved, level, krylov, moments = call(
        second_kernel, shape, [vmem] * 5,
        [fields(4), fields(1), fields(6), sums],
        [fields(4), fields(1), fields(2), fields(2)],
        (shared(moments),) + held(moved, static, level, krylov),
    )
    whole = lambda like: jax.ShapeDtypeStruct(like, f32)
    return tuple(
        call(
            last_kernel, shape, [vmem] * 5,
            [whole(velocity.shape), whole(surface.shape), whole((2,) + surface.shape)],
            [fields(2), fields(2)],
            (shared(moments),) + held(moved, static, level, krylov),
        )
    )


def solution(mesh):
    cell = P("along", "cross")
    layered = P(None, "along", "cross")
    in_specs = (layered, cell, cell, cell, P(), P(), P())
    return jax.shard_map(
        shards, mesh=mesh, in_specs=in_specs, out_specs=(layered, cell, layered), check_vma=False
    )
```
